128 devices in a mesh: gx: 8 (over y, core), gy: 16 (over x, z).
Axes of the slice: x: 4, y: 4, z: 4, core: 2. Of those that a mesh axis runs over, the one named last changes fastest.
Arguments:
- level_input: bfloat16 [32, 128, 64, 64], P('gx', 'gy'), may hold values from -6 to 6
- weight_upper: bfloat16 [3, 3, 3, 64, 64], replicated, may hold values from -0.15625 to 0.15625
- weight_deep: bfloat16 [3, 3, 3, 64, 128], replicated, may hold values from -0.15625 to 0.15625
- deep_cotangent: bfloat16 [16, 64, 64, 128], P('gx', 'gy'), may hold values from -6 to 6
Outputs:
- input_grad: bfloat16 [32, 128, 64, 64], P('gx', 'gy')
- upper_weight_grad: float32 [3, 3, 3, 64, 64], replicated
- deep_weight_grad: float32 [3, 3, 3, 64, 128], replicated
The draws below stay inside these ranges and needn't reach their ends.
All inputs are finite; a program needn't handle non-finite values.
Results may differ from the reference program's by a relative error of at most 0.015.
Values may be sent and summed in bfloat16 or wider, within the bound.
No kernel may reach another device: no remote copies, remote signals or barrier semaphores. Data moves between devices by JAX's collectives and lax.ppermute only.
A program may use at most 128 MiB of HBM per device.

```python
import math
import jax
import jax.numpy as jnp
from jax import lax

C3 = 64
C4 = 128
Z = 64
NX3 = 32
NY3 = 128
NX4 = 16
NY4 = 64


def block_scale(rng, extent, split, low, largest):
    loudness = 1.0
    for position, parts in split:
        draws = jax.random.uniform(jax.random.fold_in(jax.random.fold_in(rng, 6), position), (parts,), jnp.float32, low / len(split), largest / len(split))
        loudness = loudness * jnp.repeat(jnp.exp(draws), extent[position] // parts).reshape((-1,) + (1,) * (len(extent) - 1 - position))
    return loudness


def normal_values(key, extent, spread, most, cuts=(), kind=jnp.bfloat16):
    level = block_scale(key, extent, cuts, -0.22, 0.18) if cuts else 1.0
    result = jax.random.normal(key, extent, jnp.float32) * spread * level
    return jnp.minimum(jnp.maximum(result, -most), most).astype(kind)


def setup_inputs(seed: int = 0) -> dict:
    splits = jax.random.split(jax.random.key(seed), 5)
    level_input = normal_values(splits[0], (NX3, NY3, Z, C3), 1.0, 6.0, ((0, 8), (1, 16)))
    weight_upper = normal_values(splits[1], (3, 3, 3, C3, C3), (27 * C3) ** -0.5, 0.15625)
    weight_deep = normal_values(splits[2], (3, 3, 3, C3, C4), (27 * C3) ** -0.5, 0.15625)
    deep_cotangent = normal_values(splits[3], (NX4, NY4, Z, C4), 1.0, 6.0, ((0, 8), (1, 16)))
    return dict(level_input=level_input, weight_upper=weight_upper, weight_deep=weight_deep, deep_cotangent=deep_cotangent)


def pad_volume(field):
    return jnp.pad(field, ((1, 1), (1, 1), (1, 1), (0, 0)))

def conv_forward(padded, weight):
    size_x, size_y, size_z = (padded.shape[0] - 2, padded.shape[1] - 2, padded.shape[2] - 2)
    total = jnp.zeros((size_x * size_y * size_z, weight.shape[4]), jnp.float32)
    for shift_x in range(3):
        for shift_y in range(3):
            for shift_z in range(3):
                window = padded[shift_x:shift_x + size_x, shift_y:shift_y + size_y, shift_z:shift_z + size_z]
                total = total + jnp.dot(window.reshape(-1, weight.shape[3]), weight[shift_x, shift_y, shift_z], preferred_element_type=jnp.float32)
    return total.reshape(size_x, size_y, size_z, weight.shape[4])

def conv_transpose(padded, weight):
    size_x, size_y, size_z = (padded.shape[0] - 2, padded.shape[1] - 2, padded.shape[2] - 2)
    total = jnp.zeros((size_x * size_y * size_z, weight.shape[3]), jnp.float32)
    for shift_x in range(3):
        for shift_y in range(3):
            for shift_z in range(3):
                window = padded[2 - shift_x:2 - shift_x + size_x, 2 - shift_y:2 - shift_y + size_y, 2 - shift_z:2 - shift_z + size_z]
                total = total + jnp.dot(window.reshape(-1, weight.shape[4]), weight[shift_x, shift_y, shift_z].T, preferred_element_type=jnp.float32)
    return total.reshape(size_x, size_y, size_z, weight.shape[3])

def kernel_grad(padded, grad):
    size_x, size_y, size_z = (grad.shape[0], grad.shape[1], grad.shape[2])
    flat_grad = grad.reshape(-1, grad.shape[3])
    pieces = []
    for shift_x in range(3):
        for shift_y in range(3):
            for shift_z in range(3):
                window = padded[shift_x:shift_x + size_x, shift_y:shift_y + size_y, shift_z:shift_z + size_z]
                pieces.append(lax.dot_general(window.reshape(-1, padded.shape[3]), flat_grad, (((0,), (0,)), ((), ())), preferred_element_type=jnp.float32))
    return jnp.stack(pieces).reshape(3, 3, 3, padded.shape[3], grad.shape[3])

def pool_relu(pre):
    size_x, size_y, size_z, chans = pre.shape
    active = (pre * jax.nn.sigmoid(pre)).reshape(size_x // 2, 2, size_y // 2, 2, size_z, chans)
    return 0.25 * lax.optimization_barrier(jnp.sum(active, axis=(1, 3)))

def spread_back(grad, pre):
    size_x, size_y, size_z, chans = pre.shape
    wide = jnp.broadcast_to(grad[:, None, :, None], (size_x // 2, 2, size_y // 2, 2, size_z, chans)).reshape(pre.shape)
    sig = jax.nn.sigmoid(pre)
    return 0.25 * wide * (sig * (1.0 + pre * (1.0 - sig)))

def reference(level_input, weight_upper, weight_deep, deep_cotangent):
    padded = pad_volume(level_input)
    pre = conv_forward(padded, weight_upper)
    pooled = pool_relu(pre).astype(jnp.bfloat16)
    deep_count = deep_cotangent.shape[0] * deep_cotangent.shape[1] * deep_cotangent.shape[2]
    upper_count = level_input.shape[0] * level_input.shape[1] * level_input.shape[2]
    deep_weight_grad = kernel_grad(pad_volume(pooled), deep_cotangent) * (1.0 / math.sqrt(deep_count))
    pooled_grad = conv_transpose(pad_volume(deep_cotangent), weight_deep).astype(jnp.bfloat16)
    pre_grad = spread_back(pooled_grad.astype(jnp.float32), pre).astype(jnp.bfloat16)
    input_grad = conv_transpose(pad_volume(pre_grad), weight_upper).astype(jnp.bfloat16)
    upper_weight_grad = kernel_grad(padded, pre_grad) * (1.0 / math.sqrt(upper_count))
    return (input_grad, upper_weight_grad, deep_weight_grad)
```

```python
import math

import jax
import jax.numpy as jnp
from jax import lax
from jax.experimental import pallas as pl
from jax.experimental.pallas import tpu as pltpu
from jax.sharding import PartitionSpec as P

F32 = jnp.float32
BF16 = jnp.bfloat16
VMEM_BYTES = 56 * 1024 * 1024

PAIR_ROW = 9 * 64
DEEP_ROW = 14 * 64
PAY_ROWS = 42 * 64

CORE = ("gx", 1, (0,))
Y_NEAR = ("gx", 2, (1, 2))
Y_FAR = ("gx", 6, (2,))
Z_NEAR = ("gy", 1, (0, 1))
Z_FAR = ("gy", 3, (1,))
X_NEAR = ("gy", 4, (2, 3))
X_FAR = ("gy", 12, (3,))


def depth_taps(row, gap):
    row = row.astype(F32)
    edge = jnp.zeros((1, row.shape[1]), F32)
    below = jnp.concatenate([edge, row[:-1]], axis=0)
    above = jnp.concatenate([row[1:], edge], axis=0)
    pieces = [below, row, above]
    if gap:
        pieces.append(jnp.zeros((row.shape[0], gap), F32))
    return jnp.concatenate(pieces, axis=1).astype(BF16)


def window(taps, at_x, at_y):
    return jnp.concatenate(
        [taps[2 * x + at_x, 2 * y + at_y] for x in range(2) for y in range(4)], axis=0
    )


def deep_window(taps, at_x, at_y):
    return jnp.concatenate(
        [taps[x + at_x, y + at_y] for x in range(2) for y in range(4)], axis=0
    )


def grads_kernel(
    own, x_lo, x_hi, y_lo, y_hi, cot, cx_lo, cx_hi, cy_lo, cy_hi, w_up, w_deep,
    payload, pre_grad, gx_lo, gx_hi, gy_lo, gy_hi,
    taps, cot_taps, blocks, sums,
):
    for x in range(6):
        for y in range(10):
            if y == 0:
                row = y_lo[x]
            elif y == 9:
                row = y_hi[x]
            elif x == 0:
                row = x_lo[y - 1]
            elif x == 5:
                row = x_hi[y - 1]
            else:
                row = own[x - 1, y - 1]
            taps[x, y] = depth_taps(row, 64)
    for x in range(4):
        for y in range(6):
            if y == 0:
                row = cy_lo[x]
            elif y == 5:
                row = cy_hi[x]
            elif x == 0:
                row = cx_lo[y - 1]
            elif x == 3:
                row = cx_hi[y - 1]
            else:
                row = cot[x - 1, y - 1]
            cot_taps[x, y] = depth_taps(row, 0)

    empty = jnp.zeros((192, 64), BF16)
    for x in range(3):
        for y in range(4):
            left = w_up[x, y].reshape(192, 64) if y < 3 else empty
            right = w_up[x, y - 1].reshape(192, 64) if y > 0 else empty
            pair = jnp.concatenate([left, right], axis=1)
            blocks[x, y, 0:192, 0:128] = pair
            blocks[x + 1, y, 0:192, 128:256] = pair
    for y in range(4):
        blocks[3, y, 0:192, 0:128] = jnp.zeros((192, 128), BF16)
        blocks[0, y, 0:192, 128:256] = jnp.zeros((192, 128), BF16)
        for x in range(4):
            blocks[x, y, 192:256, :] = jnp.zeros((64, 256), BF16)

    pre = jnp.zeros((512, 256), F32)
    for x in range(4):
        for y in range(4):
            pre = pre + jnp.dot(window(taps, x, y), blocks[x, y], preferred_element_type=F32)
    sig = 1.0 / (1.0 + jnp.exp(-pre))
    act = pre * sig
    half = act[:, :128] + act[:, 128:]
    pooled = 0.25 * (half[:, :64] + half[:, 64:])
    pooled_t = pooled.T.astype(BF16)

    pooled_grad = jnp.zeros((512, 64), F32)
    for a in range(3):
        for b in range(3):
            weight = jnp.concatenate([w_deep[2 - a, 2 - b, 2 - j] for j in range(3)], axis=1)
            pooled_grad = pooled_grad + lax.dot_general(
                deep_window(cot_taps, a, b), weight, (((1,), (1,)), ((), ())),
                preferred_element_type=F32,
            )
    wide = pooled_grad.astype(BF16).astype(F32)
    wide = jnp.concatenate([wide, wide], axis=1)
    wide = jnp.concatenate([wide, wide], axis=1)
    grad = 0.25 * wide * (sig * (1.0 + pre * (1.0 - sig)))
    grad_t = grad.T.astype(BF16)
    rounded = grad.astype(BF16)
    pre_grad[...] = rounded

    def column(x, y):
        at = (x % 2) * 128 + (y % 2) * 64
        top = ((x // 2) * 4 + y // 2) * 64
        return rounded[top : top + 64, at : at + 64]

    for y in range(8):
        gx_lo[y] = column(0, y)
        gx_hi[y] = column(3, y)
    for x in range(4):
        gy_lo[x] = column(x, 0)
        gy_hi[x] = column(x, 7)

    for a in range(3):
        for b in range(3):
            out = jnp.dot(
                pooled_t, deep_window(cot_taps, 2 - a, 2 - b), preferred_element_type=F32
            ).astype(BF16)
            for j in range(3):
                top = DEEP_ROW + ((a * 3 + b) * 3 + 2 - j) * 64
                payload[top : top + 64, :] = out[:, j * 128 : j * 128 + 128]

    for x in range(4):
        for y in range(4):
            part = jnp.dot(grad_t, window(taps, x, y), preferred_element_type=F32)
            for s in range(2):
                for t in range(2):
                    a, b = x - s, y - t
                    if 0 <= a < 3 and 0 <= b < 3:
                        top = (s * 2 + t) * 64
                        piece = part[top : top + 64]
                        if s == 0 and t == 0:
                            sums[a * 3 + b] = piece
                        else:
                            sums[a * 3 + b] = sums[a * 3 + b] + piece
    for k in range(9):
        payload[k * 64 : k * 64 + 64, :] = sums[k, :, 0:128].astype(BF16)
    for k in range(5):
        left = sums[2 * k, :, 128:192]
        right = sums[2 * k + 1, :, 128:192] if k < 4 else jnp.zeros((64, 64), F32)
        top = PAIR_ROW + k * 64
        payload[top : top + 64, :] = jnp.concatenate([left, right], axis=1).astype(BF16)
    payload[PAY_ROWS - 64 :, :] = jnp.zeros((64, 128), BF16)


def local_grads(own, x_lo, x_hi, y_lo, y_hi, cot, cx_lo, cx_hi, cy_lo, cy_hi, w_up, w_deep):
    return pl.pallas_call(
        grads_kernel,
        out_shape=[
            jax.ShapeDtypeStruct((PAY_ROWS, 128), BF16),
            jax.ShapeDtypeStruct((512, 256), BF16),
            jax.ShapeDtypeStruct((8, 64, 64), BF16),
            jax.ShapeDtypeStruct((8, 64, 64), BF16),
            jax.ShapeDtypeStruct((4, 64, 64), BF16),
            jax.ShapeDtypeStruct((4, 64, 64), BF16),
        ],
        scratch_shapes=[
            pltpu.VMEM((6, 10, 64, 256), BF16),
            pltpu.VMEM((4, 6, 64, 384), BF16),
            pltpu.VMEM((4, 4, 256, 256), BF16),
            pltpu.VMEM((9, 64, 256), F32),
        ],
        compiler_params=pltpu.CompilerParams(vmem_limit_bytes=VMEM_BYTES),
        cost_estimate=pl.CostEstimate(
            flops=4_000_000_000, bytes_accessed=4_000_000, transcendentals=131072
        ),
        name="local_grads",
    )(own, x_lo, x_hi, y_lo, y_hi, cot, cx_lo, cx_hi, cy_lo, cy_hi, w_up, w_deep)


def input_kernel(pre_grad, x_lo, x_hi, y_lo, y_hi, w_up, out, taps):
    for x in range(6):
        for y in range(10):
            if y == 0:
                row = y_lo[x]
            elif y == 9:
                row = y_hi[x]
            elif x == 0:
                row = x_lo[y - 1]
            elif x == 5:
                row = x_hi[y - 1]
            else:
                u, v = x - 1, y - 1
                at = (u % 2) * 128 + (v % 2) * 64
                top = ((u // 2) * 4 + v // 2) * 64
                row = pre_grad[top : top + 64, at : at + 64]
            taps[x, y] = depth_taps(row, 64)
    empty = jnp.zeros((64, 256), BF16)
    spare = jnp.zeros((64, 64), BF16)
    weights = {}
    for a in range(3):
        for b in range(3):
            weights[a, b] = jnp.concatenate(
                [w_up[a, b, 2], w_up[a, b, 1], w_up[a, b, 0], spare], axis=1
            )
    total = jnp.zeros((512, 256), F32)
    for x in range(4):
        for y in range(4):
            block = jnp.concatenate(
                [weights.get((s + 2 - x, t + 2 - y), empty) for s in range(2) for t in range(2)],
                axis=0,
            )
            total = total + lax.dot_general(
                window(taps, x, y), block, (((1,), (1,)), ((), ())), preferred_element_type=F32
            )
    total = total.astype(BF16)
    for x in range(4):
        for y in range(8):
            at = (x % 2) * 128 + (y % 2) * 64
            top = ((x // 2) * 4 + y // 2) * 64
            out[x, y] = total[top : top + 64, at : at + 64]


def local_input(pre_grad, x_lo, x_hi, y_lo, y_hi, w_up):
    return pl.pallas_call(
        input_kernel,
        out_shape=jax.ShapeDtypeStruct((4, 8, 64, 64), BF16),
        scratch_shapes=[pltpu.VMEM((6, 10, 64, 256), BF16)],
        compiler_params=pltpu.CompilerParams(vmem_limit_bytes=VMEM_BYTES),
        cost_estimate=pl.CostEstimate(
            flops=1_000_000_000, bytes_accessed=4_000_000, transcendentals=0
        ),
        name="local_input",
    )(pre_grad, x_lo, x_hi, y_lo, y_hi, w_up)


def unpack_kernel(up_scale, deep_scale, payload, up, deep):
    for k in range(9):
        a, b = k // 3, k % 3
        first = payload[k * 64 : k * 64 + 64, :].astype(F32).T * up_scale
        up[a, b, 0] = first[:64]
        up[a, b, 1] = first[64:]
    for k in range(5):
        top = PAIR_ROW + k * 64
        pair = payload[top : top + 64, :].astype(F32).T * up_scale
        up[2 * k // 3, 2 * k % 3, 2] = pair[:64]
        if k < 4:
            up[(2 * k + 1) // 3, (2 * k + 1) % 3, 2] = pair[64:]
    for k in range(27):
        top = DEEP_ROW + k * 64
        deep[k // 9, k // 3 % 3, k % 3] = payload[top : top + 64, :].astype(F32) * deep_scale


def unpack(payload, up_scale, deep_scale):
    def body(*refs):
        unpack_kernel(up_scale, deep_scale, *refs)

    return pl.pallas_call(
        body,
        out_shape=[
            jax.ShapeDtypeStruct((3, 3, 3, 64, 64), F32),
            jax.ShapeDtypeStruct((3, 3, 3, 64, 128), F32),
        ],
        compiler_params=pltpu.CompilerParams(vmem_limit_bytes=VMEM_BYTES),
        name="unpack",
    )(payload)


def side_bit(step):
    index = lax.axis_index(step[0])
    return sum(index >> bit for bit in step[2]) & 1


def swap(value, steps, which):
    masks = {"gx": 0, "gy": 0}
    for place, (axis, mask, _) in enumerate(steps):
        if (which >> place) & 1:
            masks[axis] ^= mask
    axes = [axis for axis in ("gx", "gy") if masks[axis]]
    if len(axes) == 1:
        axis = axes[0]
        count = lax.axis_size(axis)
        return lax.ppermute(value, axis, [(i, i ^ masks[axis]) for i in range(count)])
    rows, cols = lax.axis_size("gx"), lax.axis_size("gy")
    pairs = [
        (i * cols + j, (i ^ masks["gx"]) * cols + (j ^ masks["gy"]))
        for i in range(rows)
        for j in range(cols)
    ]
    return lax.ppermute(value, ("gx", "gy"), pairs)


def place_of(steps):
    return sum(side_bit(step) << place for place, step in enumerate(steps))


def tree_sum(values):
    values = [value.astype(F32) for value in values]
    while len(values) > 1:
        values = [values[i] + values[i + 1] for i in range(0, len(values), 2)]
    return values[0].astype(BF16)


def scatter_sum(value, steps):
    parts = 1 << len(steps)
    rows = value.shape[0] // parts
    me = place_of(steps)
    found = [lax.dynamic_slice_in_dim(value, me * rows, rows, 0)]
    for k in range(1, parts):
        piece = lax.dynamic_slice_in_dim(value, (me ^ k) * rows, rows, 0)
        found.append(swap(piece, steps, k))
    return tree_sum(found)


def swap_sum(value, steps):
    return tree_sum([value] + [swap(value, steps, k) for k in range(1, 1 << len(steps))])


def gather(value, steps):
    parts = 1 << len(steps)
    me = place_of(steps)
    found = [value] + [swap(value, steps, k) for k in range(1, parts)]
    for place in range(len(steps)):
        near = ((me >> place) & 1) == 0
        other = 1 << place
        found = [
            jnp.where(near, found[i & ~other], found[i | other])
            if not i & other
            else jnp.where(near, found[i | other], found[i & ~other])
            for i in range(parts)
        ]
    return jnp.concatenate(found)


def sum_everywhere(value):
    value = scatter_sum(value, (CORE,))
    value = scatter_sum(value, (Z_NEAR, X_NEAR))
    for step in (Z_FAR, X_FAR, Y_NEAR, Y_FAR):
        value = swap_sum(value, (step,))
    value = gather(value, (Z_NEAR, X_NEAR))
    return gather(value, (CORE,))


def neighbours(head, tail, axis):
    count = lax.axis_size(axis)
    before = lax.ppermute(tail, axis, [(i, i + 1) for i in range(count - 1)])
    after = lax.ppermute(head, axis, [(i + 1, i) for i in range(count - 1)])
    return before, after


def local(level_input, weight_upper, weight_deep, deep_cotangent):
    tiles = lax.axis_size("gx") * lax.axis_size("gy")
    up_scale = 1.0 / math.sqrt(math.prod(level_input.shape[:3]) * tiles)
    deep_scale = 1.0 / math.sqrt(math.prod(deep_cotangent.shape[:3]) * tiles)
    own, cot = level_input, deep_cotangent

    x_lo, x_hi = neighbours(own[0], own[3], "gx")
    cx_lo, cx_hi = neighbours(cot[0], cot[1], "gx")

    def side(lo, mid, hi, y):
        return jnp.concatenate([lo[None, y], mid[:, y], hi[None, y]])

    y_lo, y_hi = neighbours(side(x_lo, own, x_hi, 0), side(x_lo, own, x_hi, 7), "gy")
    cy_lo, cy_hi = neighbours(side(cx_lo, cot, cx_hi, 0), side(cx_lo, cot, cx_hi, 3), "gy")

    payload, pre_grad, gx_lo, gx_hi, gy_lo, gy_hi = local_grads(
        own, x_lo, x_hi, y_lo, y_hi, cot, cx_lo, cx_hi, cy_lo, cy_hi, weight_upper, weight_deep
    )
    gx_lo, gx_hi = neighbours(gx_lo, gx_hi, "gx")
    gy_lo, gy_hi = neighbours(
        jnp.concatenate([gx_lo[None, 0], gy_lo, gx_hi[None, 0]]),
        jnp.concatenate([gx_lo[None, 7], gy_hi, gx_hi[None, 7]]),
        "gy",
    )
    input_grad = local_input(pre_grad, gx_lo, gx_hi, gy_lo, gy_hi, weight_upper)
    total = sum_everywhere(payload)
    upper, deep = unpack(total, up_scale, deep_scale)
    return (input_grad, upper, deep)


def solution(mesh):
    placed = (P("gx", "gy", None, None), P(), P(), P("gx", "gy", None, None))
    return jax.shard_map(
        local,
        mesh=mesh,
        in_specs=placed,
        out_specs=(P("gx", "gy", None, None), P(), P()),
        check_vma=False,
    )
```

```python
import functools
import math

import jax
import jax.numpy as jnp
from jax import lax
from jax.experimental import pallas as pl
from jax.experimental.pallas import tpu as pltpu
from jax.sharding import PartitionSpec as P

F32 = jnp.float32
BF16 = jnp.bfloat16
VMEM_BYTES = 28 * 1024 * 1024

PAIR_ROW = 9 * 64
DEEP_ROW = 14 * 64
PAY_ROWS = 42 * 64
HALF_ROWS = PAY_ROWS // 2

CORE = ("gx", 1, (0,))
Y_NEAR = ("gx", 2, (1, 2))
Y_FAR = ("gx", 6, (2,))
Z_NEAR = ("gy", 1, (0, 1))
Z_FAR = ("gy", 3, (1,))
X_NEAR = ("gy", 4, (2, 3))
X_FAR = ("gy", 12, (3,))


def depth_taps(row, gap):
    row = row.astype(F32)
    edge = jnp.zeros((1, row.shape[1]), F32)
    below = jnp.concatenate([edge, row[:-1]], axis=0)
    above = jnp.concatenate([row[1:], edge], axis=0)
    pieces = [below, row, above]
    if gap:
        pieces.append(jnp.zeros((row.shape[0], gap), F32))
    return jnp.concatenate(pieces, axis=1).astype(BF16)


def window(taps, at_x, at_y):
    return jnp.concatenate(
        [taps[2 * x + at_x, 2 * y + at_y] for x in range(2) for y in range(4)], axis=0
    )


def deep_window(taps, at_x, at_y):
    return jnp.concatenate(
        [taps[x + at_x, y + at_y] for x in range(2) for y in range(4)], axis=0
    )


def faces_kernel(odd, own, cot, to_core, to_chip, y_head, y_tail):
    swapped = odd[0] == 1
    for k in range(4):
        head = jnp.concatenate([own[0, 2 * k + 1], own[0, 2 * k]], axis=1)
        tail = jnp.concatenate([own[3, 2 * k], own[3, 2 * k + 1]], axis=1)
        to_core[k] = jnp.where(swapped, head, tail)
        to_chip[k] = jnp.where(swapped, tail, head)
        to_core[4 + k] = jnp.where(swapped, cot[0, k], cot[1, k])
        to_chip[4 + k] = jnp.where(swapped, cot[1, k], cot[0, k])
    for k in range(2):
        y_head[k] = jnp.concatenate([own[2 * k, 0], own[2 * k + 1, 0]], axis=1)
        y_tail[k] = jnp.concatenate([own[2 * k, 7], own[2 * k + 1, 7]], axis=1)
        y_head[2 + k] = cot[k, 0]
        y_tail[2 + k] = cot[k, 3]


def faces(odd, own, cot):
    vmem = pl.BlockSpec(memory_space=pltpu.VMEM)
    return pl.pallas_call(
        faces_kernel,
        in_specs=[pl.BlockSpec(memory_space=pltpu.SMEM), vmem, vmem],
        out_shape=[jax.ShapeDtypeStruct((8, 64, 128), BF16)] * 2
        + [jax.ShapeDtypeStruct((4, 64, 128), BF16)] * 2,
        name="faces",
    )(odd, own, cot)


def level_column(x, y, own, x_lo, x_hi, y_lo, y_hi):
    if y == 0 or y == 9:
        pairs = y_lo if y == 0 else y_hi
        if 1 <= x <= 4:
            return half(pairs(((x - 1) // 2)), (x - 1) % 2)
        return half(pairs(2), int((x == 5) == (y == 9)))
    if x == 0:
        return half(x_lo((y - 1) // 2), (y - 1) % 2)
    if x == 5:
        return half(x_hi((y - 1) // 2), 1 - (y - 1) % 2)
    return own(x - 1, y - 1)


def half(value, which):
    return value[:, which * 64 : which * 64 + 64]


def grads_kernel(
    odd_x, odd_y, own, cot, core, chip, near, far, w_up, w_deep,
    keep, send, pre_grad, to_core, to_chip, gy_head, gy_tail,
    taps, cot_taps, blocks, sums, payload,
):
    swap_x = odd_x[0] == 1
    swap_y = odd_y[0] == 1

    def x_lo(k):
        return jnp.where(swap_x, core[k], chip[k])

    def x_hi(k):
        return jnp.where(swap_x, chip[k], core[k])

    def y_lo(k):
        return jnp.where(swap_y, near[k], far[k])

    def y_hi(k):
        return jnp.where(swap_y, far[k], near[k])

    for x in range(6):
        for y in range(10):
            row = level_column(x, y, lambda u, v: own[u, v], x_lo, x_hi, y_lo, y_hi)
            taps[x, y] = depth_taps(row, 64)
    for x in range(4):
        for y in range(6):
            if y == 0:
                row = y_lo(3 + x)
            elif y == 5:
                row = y_hi(3 + x)
            elif x == 0:
                row = x_lo(3 + y)
            elif x == 3:
                row = x_hi(3 + y)
            else:
                row = cot[x - 1, y - 1]
            cot_taps[x, y] = depth_taps(row, 0)

    empty = jnp.zeros((192, 64), BF16)
    for x in range(3):
        for y in range(4):
            left = w_up[x, y].reshape(192, 64) if y < 3 else empty
            right = w_up[x, y - 1].reshape(192, 64) if y > 0 else empty
            pair = jnp.concatenate([left, right], axis=1)
            blocks[x, y, 0:192, 0:128] = pair
            blocks[x + 1, y, 0:192, 128:256] = pair
    for y in range(4):
        blocks[3, y, 0:192, 0:128] = jnp.zeros((192, 128), BF16)
        blocks[0, y, 0:192, 128:256] = jnp.zeros((192, 128), BF16)
        for x in range(4):
            blocks[x, y, 192:256, :] = jnp.zeros((64, 256), BF16)

    pre = jnp.zeros((512, 256), F32)
    for x in range(4):
        for y in range(4):
            pre = pre + jnp.dot(window(taps, x, y), blocks[x, y], preferred_element_type=F32)
    sig = 1.0 / (1.0 + jnp.exp(-pre))
    act = pre * sig
    summed = act[:, :128] + act[:, 128:]
    pooled = 0.25 * (summed[:, :64] + summed[:, 64:])
    pooled_t = pooled.T.astype(BF16)

    pooled_grad = jnp.zeros((512, 64), F32)
    for a in range(3):
        for b in range(3):
            weight = jnp.concatenate([w_deep[2 - a, 2 - b, 2 - j] for j in range(3)], axis=1)
            pooled_grad = pooled_grad + lax.dot_general(
                deep_window(cot_taps, a, b), weight, (((1,), (1,)), ((), ())),
                preferred_element_type=F32,
            )
    wide = pooled_grad.astype(BF16).astype(F32)
    wide = jnp.concatenate([wide, wide], axis=1)
    wide = jnp.concatenate([wide, wide], axis=1)
    grad = 0.25 * wide * (sig * (1.0 + pre * (1.0 - sig)))
    grad_t = grad.T.astype(BF16)
    rounded = grad.astype(BF16)
    pre_grad[...] = rounded

    for k in range(4):
        head = rounded[k * 64 : k * 64 + 64, 0:128]
        head = jnp.concatenate([half(head, 1), half(head, 0)], axis=1)
        tail = rounded[256 + k * 64 : 320 + k * 64, 128:256]
        to_core[k] = jnp.where(swap_x, head, tail)
        to_chip[k] = jnp.where(swap_x, tail, head)
    for k in range(2):
        first = rounded[k * 256 : k * 256 + 64]
        last = rounded[k * 256 + 192 : k * 256 + 256]
        gy_head[k] = jnp.concatenate([first[:, 0:64], first[:, 128:192]], axis=1)
        gy_tail[k] = jnp.concatenate([last[:, 64:128], last[:, 192:256]], axis=1)

    for a in range(3):
        for b in range(3):
            out = jnp.dot(
                pooled_t, deep_window(cot_taps, 2 - a, 2 - b), preferred_element_type=F32
            ).astype(BF16)
            for j in range(3):
                top = DEEP_ROW + ((a * 3 + b) * 3 + 2 - j) * 64
                payload[top : top + 64, :] = out[:, j * 128 : j * 128 + 128]

    for x in range(4):
        for y in range(4):
            part = jnp.dot(grad_t, window(taps, x, y), preferred_element_type=F32)
            for s in range(2):
                for t in range(2):
                    a, b = x - s, y - t
                    if 0 <= a < 3 and 0 <= b < 3:
                        top = (s * 2 + t) * 64
                        piece = part[top : top + 64]
                        if s == 0 and t == 0:
                            sums[a * 3 + b] = piece
                        else:
                            sums[a * 3 + b] = sums[a * 3 + b] + piece
    for k in range(9):
        payload[k * 64 : k * 64 + 64, :] = sums[k, :, 0:128].astype(BF16)
    for k in range(5):
        left = sums[2 * k, :, 128:192]
        right = sums[2 * k + 1, :, 128:192] if k < 4 else jnp.zeros((64, 64), F32)
        top = PAIR_ROW + k * 64
        payload[top : top + 64, :] = jnp.concatenate([left, right], axis=1).astype(BF16)
    payload[PAY_ROWS - 64 :, :] = jnp.zeros((64, 128), BF16)
    mine = pl.multiple_of(odd_x[0] * HALF_ROWS, HALF_ROWS)
    keep[...] = payload[pl.ds(mine, HALF_ROWS), :]
    send[...] = payload[pl.ds(HALF_ROWS - mine, HALF_ROWS), :]


def local_grads(odd_x, odd_y, own, cot, core, chip, near, far, w_up, w_deep):
    smem = pl.BlockSpec(memory_space=pltpu.SMEM)
    vmem = pl.BlockSpec(memory_space=pltpu.VMEM)
    return pl.pallas_call(
        grads_kernel,
        in_specs=[smem, smem] + [vmem] * 8,
        out_shape=[
            jax.ShapeDtypeStruct((HALF_ROWS, 128), BF16),
            jax.ShapeDtypeStruct((HALF_ROWS, 128), BF16),
            jax.ShapeDtypeStruct((512, 256), BF16),
            jax.ShapeDtypeStruct((4, 64, 128), BF16),
            jax.ShapeDtypeStruct((4, 64, 128), BF16),
            jax.ShapeDtypeStruct((2, 64, 128), BF16),
            jax.ShapeDtypeStruct((2, 64, 128), BF16),
        ],
        scratch_shapes=[
            pltpu.VMEM((6, 10, 64, 256), BF16),
            pltpu.VMEM((4, 6, 64, 384), BF16),
            pltpu.VMEM((4, 4, 256, 256), BF16),
            pltpu.VMEM((9, 64, 256), F32),
            pltpu.VMEM((PAY_ROWS, 128), BF16),
        ],
        compiler_params=pltpu.CompilerParams(vmem_limit_bytes=VMEM_BYTES),
        cost_estimate=pl.CostEstimate(
            flops=4_000_000_000, bytes_accessed=4_000_000, transcendentals=131072
        ),
        name="local_grads",
    )(odd_x, odd_y, own, cot, core, chip, near, far, w_up, w_deep)


def input_kernel(odd_x, odd_y, pre_grad, core, chip, near, far, w_up, out, taps):
    swap_x = odd_x[0] == 1
    swap_y = odd_y[0] == 1

    def x_lo(k):
        return jnp.where(swap_x, core[k], chip[k])

    def x_hi(k):
        return jnp.where(swap_x, chip[k], core[k])

    def y_lo(k):
        return jnp.where(swap_y, near[k], far[k])

    def y_hi(k):
        return jnp.where(swap_y, far[k], near[k])

    def own(u, v):
        at = (u % 2) * 128 + (v % 2) * 64
        top = ((u // 2) * 4 + v // 2) * 64
        return pre_grad[top : top + 64, at : at + 64]

    for x in range(6):
        for y in range(10):
            taps[x, y] = depth_taps(level_column(x, y, own, x_lo, x_hi, y_lo, y_hi), 64)
    empty = jnp.zeros((64, 256), BF16)
    spare = jnp.zeros((64, 64), BF16)
    weights = {}
    for a in range(3):
        for b in range(3):
            weights[a, b] = jnp.concatenate(
                [w_up[a, b, 2], w_up[a, b, 1], w_up[a, b, 0], spare], axis=1
            )
    total = jnp.zeros((512, 256), F32)
    for x in range(4):
        for y in range(4):
            block = jnp.concatenate(
                [weights.get((s + 2 - x, t + 2 - y), empty) for s in range(2) for t in range(2)],
                axis=0,
            )
            total = total + lax.dot_general(
                window(taps, x, y), block, (((1,), (1,)), ((), ())), preferred_element_type=F32
            )
    total = total.astype(BF16)
    for x in range(4):
        for y in range(8):
            at = (x % 2) * 128 + (y % 2) * 64
            top = ((x // 2) * 4 + y // 2) * 64
            out[x, y] = total[top : top + 64, at : at + 64]


def local_input(odd_x, odd_y, pre_grad, core, chip, near, far, w_up):
    smem = pl.BlockSpec(memory_space=pltpu.SMEM)
    vmem = pl.BlockSpec(memory_space=pltpu.VMEM)
    return pl.pallas_call(
        input_kernel,
        in_specs=[smem, smem] + [vmem] * 6,
        out_shape=jax.ShapeDtypeStruct((4, 8, 64, 64), BF16),
        scratch_shapes=[pltpu.VMEM((6, 10, 64, 256), BF16)],
        compiler_params=pltpu.CompilerParams(vmem_limit_bytes=VMEM_BYTES),
        cost_estimate=pl.CostEstimate(
            flops=1_000_000_000, bytes_accessed=4_000_000, transcendentals=0
        ),
        name="local_input",
    )(odd_x, odd_y, pre_grad, core, chip, near, far, w_up)


def unpack_kernel(up_scale, deep_scale, odd, mine, other, up, deep, payload):
    first = pl.multiple_of(odd[0] * HALF_ROWS, HALF_ROWS)
    payload[pl.ds(first, HALF_ROWS), :] = mine[...]
    payload[pl.ds(HALF_ROWS - first, HALF_ROWS), :] = other[...]
    for k in range(9):
        a, b = k // 3, k % 3
        pair = payload[k * 64 : k * 64 + 64, :].astype(F32).T * up_scale
        up[a, b, 0] = pair[:64]
        up[a, b, 1] = pair[64:]
    for k in range(5):
        top = PAIR_ROW + k * 64
        pair = payload[top : top + 64, :].astype(F32).T * up_scale
        up[2 * k // 3, 2 * k % 3, 2] = pair[:64]
        if k < 4:
            up[(2 * k + 1) // 3, (2 * k + 1) % 3, 2] = pair[64:]
    for k in range(27):
        top = DEEP_ROW + k * 64
        deep[k // 9, k // 3 % 3, k % 3] = payload[top : top + 64, :].astype(F32) * deep_scale


def unpack(odd, mine, other, up_scale, deep_scale):
    vmem = pl.BlockSpec(memory_space=pltpu.VMEM)
    return pl.pallas_call(
        functools.partial(unpack_kernel, up_scale, deep_scale),
        in_specs=[pl.BlockSpec(memory_space=pltpu.SMEM), vmem, vmem],
        out_shape=[
            jax.ShapeDtypeStruct((3, 3, 3, 64, 64), F32),
            jax.ShapeDtypeStruct((3, 3, 3, 64, 128), F32),
        ],
        scratch_shapes=[pltpu.VMEM((PAY_ROWS, 128), BF16)],
        compiler_params=pltpu.CompilerParams(vmem_limit_bytes=VMEM_BYTES),
        name="unpack",
    )(odd, mine, other)


def side_bit(step):
    index = lax.axis_index(step[0])
    return sum(index >> bit for bit in step[2]) & 1


def swap(value, steps, which):
    masks = {"gx": 0, "gy": 0}
    for place, (axis, mask, _) in enumerate(steps):
        if (which >> place) & 1:
            masks[axis] ^= mask
    axes = [axis for axis in ("gx", "gy") if masks[axis]]
    if len(axes) == 1:
        axis = axes[0]
        count = lax.axis_size(axis)
        return lax.ppermute(value, axis, [(i, i ^ masks[axis]) for i in range(count)])
    rows, cols = lax.axis_size("gx"), lax.axis_size("gy")
    pairs = [
        (i * cols + j, (i ^ masks["gx"]) * cols + (j ^ masks["gy"]))
        for i in range(rows)
        for j in range(cols)
    ]
    return lax.ppermute(value, ("gx", "gy"), pairs)


def place_of(steps):
    return sum(side_bit(step) << place for place, step in enumerate(steps))


def tree_sum(values):
    values = [value.astype(F32) for value in values]
    while len(values) > 1:
        values = [values[i] + values[i + 1] for i in range(0, len(values), 2)]
    return values[0].astype(BF16)


def scatter_sum(value, steps):
    parts = 1 << len(steps)
    rows = value.shape[0] // parts
    me = place_of(steps)
    found = [lax.dynamic_slice_in_dim(value, me * rows, rows, 0)]
    for k in range(1, parts):
        piece = lax.dynamic_slice_in_dim(value, (me ^ k) * rows, rows, 0)
        found.append(swap(piece, steps, k))
    return tree_sum(found)


def swap_sum(value, steps):
    return tree_sum([value] + [swap(value, steps, k) for k in range(1, 1 << len(steps))])


def gather(value, steps):
    parts = 1 << len(steps)
    me = place_of(steps)
    found = [value] + [swap(value, steps, k) for k in range(1, parts)]
    for place in range(len(steps)):
        near = ((me >> place) & 1) == 0
        other = 1 << place
        found = [
            jnp.where(near, found[i & ~other], found[i | other])
            if not i & other
            else jnp.where(near, found[i | other], found[i & ~other])
            for i in range(parts)
        ]
    return jnp.concatenate(found)


def pairs_of(axis, first):
    found = []
    for i in range(first, lax.axis_size(axis) - 1, 2):
        found += [(i, i + 1), (i + 1, i)]
    return found


def both_sides(first, second, axis):
    return (
        lax.ppermute(first, axis, pairs_of(axis, 0)),
        lax.ppermute(second, axis, pairs_of(axis, 1)),
    )


def column_ends(odd_x, odd_y, core, chip, head, tail, level_rows):
    lo = jnp.where(odd_x == 1, core, chip)
    hi = jnp.where(odd_x == 1, chip, core)
    left = lax.broadcasted_iota(jnp.int32, (1, 64, 128), 2) < 64
    head = [head[:2], jnp.where(left, lo[0:1], hi[0:1])] + (
        [lo[4:5], head[2:], hi[4:5]] if level_rows else []
    )
    tail = [tail[:2], jnp.where(left, hi[3:4], lo[3:4])] + (
        [lo[7:8], tail[2:], hi[7:8]] if level_rows else []
    )
    head, tail = jnp.concatenate(head), jnp.concatenate(tail)
    return jnp.where(odd_y == 1, head, tail), jnp.where(odd_y == 1, tail, head)


def local(level_input, weight_upper, weight_deep, deep_cotangent):
    tiles = lax.axis_size("gx") * lax.axis_size("gy")
    up_scale = 1.0 / math.sqrt(math.prod(level_input.shape[:3]) * tiles)
    deep_scale = 1.0 / math.sqrt(math.prod(deep_cotangent.shape[:3]) * tiles)
    odd_x = (lax.axis_index("gx") & 1).astype(jnp.int32)
    odd_y = (lax.axis_index("gy") & 1).astype(jnp.int32)
    flag_x, flag_y = odd_x.reshape(1), odd_y.reshape(1)

    to_core, to_chip, y_head, y_tail = faces(flag_x, level_input, deep_cotangent)
    core, chip = both_sides(to_core, to_chip, "gx")
    to_near, to_far = column_ends(odd_x, odd_y, core, chip, y_head, y_tail, True)
    near, far = both_sides(to_near, to_far, "gy")

    keep, send, pre_grad, to_core, to_chip, y_head, y_tail = local_grads(
        flag_x, flag_y, level_input, deep_cotangent, core, chip, near, far,
        weight_upper, weight_deep,
    )
    total = tree_sum([keep, swap(send, (CORE,), 1)])
    core, chip = both_sides(to_core, to_chip, "gx")
    total = scatter_sum(total, (Z_NEAR, X_NEAR))
    total, core, chip = lax.optimization_barrier((total, core, chip))
    to_near, to_far = column_ends(odd_x, odd_y, core, chip, y_head, y_tail, False)
    near, far = both_sides(to_near, to_far, "gy")
    total = swap_sum(total, (Z_FAR,))
    total, near, far = lax.optimization_barrier((total, near, far))
    input_grad = local_input(
        flag_x, flag_y, pre_grad, core, chip, near, far, weight_upper
    )
    for step in (X_FAR, Y_NEAR, Y_FAR):
        total = swap_sum(total, (step,))
    total = gather(total, (Z_NEAR, X_NEAR))
    other = swap(total, (CORE,), 1)
    upper, deep = unpack(flag_x, total, other, up_scale, deep_scale)
    return (input_grad, upper, deep)


def solution(mesh):
    placed = (P("gx", "gy", None, None), P(), P(), P("gx", "gy", None, None))
    return jax.shard_map(
        local,
        mesh=mesh,
        in_specs=placed,
        out_specs=(P("gx", "gy", None, None), P(), P()),
        check_vma=False,
    )
```

```python
import functools
import math

import jax
import jax.numpy as jnp
from jax import lax
from jax.experimental import pallas as pl
from jax.experimental.pallas import tpu as pltpu
from jax.sharding import PartitionSpec as P

F32 = jnp.float32
BF16 = jnp.bfloat16
VMEM_BYTES = 28 * 1024 * 1024

PAIR_ROW = 9 * 64
DEEP_ROW = 14 * 64
PAY_ROWS = 42 * 64
HALF_ROWS = PAY_ROWS // 2

CORE = ("gx", 1, (0,))
Y_NEAR = ("gx", 2, (1, 2))
Y_FAR = ("gx", 6, (2,))
Z_NEAR = ("gy", 1, (0, 1))
Z_FAR = ("gy", 3, (1,))
X_NEAR = ("gy", 4, (2, 3))
X_FAR = ("gy", 12, (3,))


def depth_taps(row, gap):
    row = row.astype(F32)
    edge = jnp.zeros((1, row.shape[1]), F32)
    below = jnp.concatenate([edge, row[:-1]], axis=0)
    above = jnp.concatenate([row[1:], edge], axis=0)
    pieces = [below, row, above]
    if gap:
        pieces.append(jnp.zeros((row.shape[0], gap), F32))
    return jnp.concatenate(pieces, axis=1).astype(BF16)


INNER = (1, 2)
OUTER = (0, 3)


def window(taps, at_x, at_y, ys):
    return jnp.concatenate(
        [taps[2 * x + at_x, 2 * y + at_y] for x in range(2) for y in ys], axis=0
    )


def deep_window(taps, at_x, at_y, ys):
    return jnp.concatenate([taps[x + at_x, y + at_y] for x in range(2) for y in ys], axis=0)


def faces_kernel(odd, own, cot, to_core, to_chip, y_head, y_tail):
    swapped = odd[0] == 1
    for k in range(4):
        head = jnp.concatenate([own[0, 2 * k + 1], own[0, 2 * k]], axis=1)
        tail = jnp.concatenate([own[3, 2 * k], own[3, 2 * k + 1]], axis=1)
        to_core[k] = jnp.where(swapped, head, tail)
        to_chip[k] = jnp.where(swapped, tail, head)
        to_core[4 + k] = jnp.where(swapped, cot[0, k], cot[1, k])
        to_chip[4 + k] = jnp.where(swapped, cot[1, k], cot[0, k])
    for k in range(2):
        y_head[k] = jnp.concatenate([own[2 * k, 0], own[2 * k + 1, 0]], axis=1)
        y_tail[k] = jnp.concatenate([own[2 * k, 7], own[2 * k + 1, 7]], axis=1)
        y_head[2 + k] = cot[k, 0]
        y_tail[2 + k] = cot[k, 3]


def faces(odd, own, cot):
    vmem = pl.BlockSpec(memory_space=pltpu.VMEM)
    return pl.pallas_call(
        faces_kernel,
        in_specs=[pl.BlockSpec(memory_space=pltpu.SMEM), vmem, vmem],
        out_shape=[jax.ShapeDtypeStruct((8, 64, 128), BF16)] * 2
        + [jax.ShapeDtypeStruct((4, 64, 128), BF16)] * 2,
        compiler_params=pltpu.CompilerParams(vmem_limit_bytes=6 * 1024 * 1024),
        name="faces",
    )(odd, own, cot)


def level_column(x, y, own, x_lo, x_hi, y_lo, y_hi):
    if y == 0 or y == 9:
        pairs = y_lo if y == 0 else y_hi
        if 1 <= x <= 4:
            return half(pairs(((x - 1) // 2)), (x - 1) % 2)
        return half(pairs(2), int((x == 5) == (y == 9)))
    if x == 0:
        return half(x_lo((y - 1) // 2), (y - 1) % 2)
    if x == 5:
        return half(x_hi((y - 1) // 2), 1 - (y - 1) % 2)
    return own(x - 1, y - 1)


def half(value, which):
    return value[:, which * 64 : which * 64 + 64]


def build_blocks(w_up, blocks):
    empty = jnp.zeros((192, 64), BF16)
    for x in range(3):
        for y in range(4):
            left = w_up[x, y].reshape(192, 64) if y < 3 else empty
            right = w_up[x, y - 1].reshape(192, 64) if y > 0 else empty
            pair = jnp.concatenate([left, right], axis=1)
            blocks[x, y, 0:192, 0:128] = pair
            blocks[x + 1, y, 0:192, 128:256] = pair
    for y in range(4):
        blocks[3, y, 0:192, 0:128] = jnp.zeros((192, 128), BF16)
        blocks[0, y, 0:192, 128:256] = jnp.zeros((192, 128), BF16)
        for x in range(4):
            blocks[x, y, 192:256, :] = jnp.zeros((64, 256), BF16)


def column_grads(ys, taps, cot_taps, blocks, w_deep, sums, deep):
    rows = 2 * len(ys) * 64
    pre = jnp.zeros((rows, 256), F32)
    for x in range(4):
        for y in range(4):
            pre = pre + jnp.dot(
                window(taps, x, y, ys), blocks[x, y], preferred_element_type=F32
            )
    sig = 1.0 / (1.0 + jnp.exp(-pre))
    act = pre * sig
    summed = act[:, :128] + act[:, 128:]
    pooled = 0.25 * (summed[:, :64] + summed[:, 64:])
    pooled_t = pooled.T.astype(BF16)

    pooled_grad = jnp.zeros((rows, 64), F32)
    for a in range(3):
        for b in range(3):
            weight = jnp.concatenate([w_deep[2 - a, 2 - b, 2 - j] for j in range(3)], axis=1)
            pooled_grad = pooled_grad + lax.dot_general(
                deep_window(cot_taps, a, b, ys), weight, (((1,), (1,)), ((), ())),
                preferred_element_type=F32,
            )
    wide = pooled_grad.astype(BF16).astype(F32)
    wide = jnp.concatenate([wide, wide], axis=1)
    wide = jnp.concatenate([wide, wide], axis=1)
    grad = 0.25 * wide * (sig * (1.0 + pre * (1.0 - sig)))
    grad_t = grad.T.astype(BF16)

    for a in range(3):
        for b in range(3):
            out = jnp.dot(
                pooled_t, deep_window(cot_taps, 2 - a, 2 - b, ys), preferred_element_type=F32
            )
            for j in range(3):
                deep((a * 3 + b) * 3 + 2 - j, out[:, j * 128 : j * 128 + 128])
    for x in range(4):
        for y in range(4):
            part = jnp.dot(grad_t, window(taps, x, y, ys), preferred_element_type=F32)
            for s in range(2):
                for t in range(2):
                    a, b = x - s, y - t
                    if 0 <= a < 3 and 0 <= b < 3:
                        top = (s * 2 + t) * 64
                        sums(a * 3 + b, part[top : top + 64], s == 0 and t == 0)
    return grad.astype(BF16)


def inner_kernel(odd_x, own, cot, core, chip, w_up, w_deep, sums, deep, inner, taps, cot_taps, blocks):
    swap_x = odd_x[0] == 1

    def x_lo(k):
        return jnp.where(swap_x, core[k], chip[k])

    def x_hi(k):
        return jnp.where(swap_x, chip[k], core[k])

    for x in range(6):
        for y in range(2, 8):
            row = level_column(x, y, lambda u, v: own[u, v], x_lo, x_hi, None, None)
            taps[x, y] = depth_taps(row, 64)
    for x in range(4):
        for y in range(1, 5):
            if x == 0:
                row = x_lo(3 + y)
            elif x == 3:
                row = x_hi(3 + y)
            else:
                row = cot[x - 1, y - 1]
            cot_taps[x, y] = depth_taps(row, 0)
    build_blocks(w_up, blocks)

    def add_sum(k, piece, first):
        sums[k] = piece if first else sums[k] + piece

    def add_deep(k, piece):
        deep[k] = piece

    inner[...] = column_grads(INNER, taps, cot_taps, blocks, w_deep, add_sum, add_deep)


def inner_grads(odd_x, own, cot, core, chip, w_up, w_deep):
    smem = pl.BlockSpec(memory_space=pltpu.SMEM)
    vmem = pl.BlockSpec(memory_space=pltpu.VMEM)
    return pl.pallas_call(
        inner_kernel,
        in_specs=[smem] + [vmem] * 6,
        out_shape=[
            jax.ShapeDtypeStruct((9, 64, 256), F32),
            jax.ShapeDtypeStruct((27, 64, 128), F32),
            jax.ShapeDtypeStruct((256, 256), BF16),
        ],
        scratch_shapes=[
            pltpu.VMEM((6, 10, 64, 256), BF16),
            pltpu.VMEM((4, 6, 64, 384), BF16),
            pltpu.VMEM((4, 4, 256, 256), BF16),
        ],
        compiler_params=pltpu.CompilerParams(vmem_limit_bytes=VMEM_BYTES),
        cost_estimate=pl.CostEstimate(
            flops=2_000_000_000, bytes_accessed=4_000_000, transcendentals=65536
        ),
        name="inner_grads",
    )(odd_x, own, cot, core, chip, w_up, w_deep)


def outer_kernel(
    odd_x, odd_y, own, cot, core, chip, near, far, w_up, w_deep, sums_in, deep_in, inner,
    keep, send, outer, to_core, to_chip, gy_head, gy_tail,
    taps, cot_taps, blocks, sums, payload,
):
    swap_x = odd_x[0] == 1
    swap_y = odd_y[0] == 1

    def x_lo(k):
        return jnp.where(swap_x, core[k], chip[k])

    def x_hi(k):
        return jnp.where(swap_x, chip[k], core[k])

    def y_lo(k):
        return jnp.where(swap_y, near[k], far[k])

    def y_hi(k):
        return jnp.where(swap_y, far[k], near[k])

    for x in range(6):
        for y in (0, 1, 2, 3, 6, 7, 8, 9):
            row = level_column(x, y, lambda u, v: own[u, v], x_lo, x_hi, y_lo, y_hi)
            taps[x, y] = depth_taps(row, 64)
    for x in range(4):
        for y in range(6):
            if y == 0:
                row = y_lo(3 + x)
            elif y == 5:
                row = y_hi(3 + x)
            elif x == 0:
                row = x_lo(3 + y)
            elif x == 3:
                row = x_hi(3 + y)
            else:
                row = cot[x - 1, y - 1]
            cot_taps[x, y] = depth_taps(row, 0)
    build_blocks(w_up, blocks)

    def add_sum(k, piece, first):
        sums[k] = (sums_in[k] if first else sums[k]) + piece

    def add_deep(k, piece):
        top = DEEP_ROW + k * 64
        payload[top : top + 64, :] = (deep_in[k] + piece).astype(BF16)

    rounded = column_grads(OUTER, taps, cot_taps, blocks, w_deep, add_sum, add_deep)
    outer[...] = rounded

    def block(x, y):
        top = (x * 2 + (y in (2, 3))) * 64
        return (inner if y in INNER else rounded)[top : top + 64]

    for k in range(4):
        head = block(0, k)[:, 0:128]
        head = jnp.concatenate([half(head, 1), half(head, 0)], axis=1)
        tail = block(1, k)[:, 128:256]
        to_core[k] = jnp.where(swap_x, head, tail)
        to_chip[k] = jnp.where(swap_x, tail, head)
    for k in range(2):
        first, last = block(k, 0), block(k, 3)
        gy_head[k] = jnp.concatenate([first[:, 0:64], first[:, 128:192]], axis=1)
        gy_tail[k] = jnp.concatenate([last[:, 64:128], last[:, 192:256]], axis=1)

    for k in range(9):
        payload[k * 64 : k * 64 + 64, :] = sums[k, :, 0:128].astype(BF16)
    for k in range(5):
        left = sums[2 * k, :, 128:192]
        right = sums[2 * k + 1, :, 128:192] if k < 4 else jnp.zeros((64, 64), F32)
        top = PAIR_ROW + k * 64
        payload[top : top + 64, :] = jnp.concatenate([left, right], axis=1).astype(BF16)
    payload[PAY_ROWS - 64 :, :] = jnp.zeros((64, 128), BF16)
    mine = pl.multiple_of(odd_x[0] * HALF_ROWS, HALF_ROWS)
    keep[...] = payload[pl.ds(mine, HALF_ROWS), :]
    send[...] = payload[pl.ds(HALF_ROWS - mine, HALF_ROWS), :]


def outer_grads(odd_x, odd_y, own, cot, core, chip, near, far, w_up, w_deep, sums, deep, inner):
    smem = pl.BlockSpec(memory_space=pltpu.SMEM)
    vmem = pl.BlockSpec(memory_space=pltpu.VMEM)
    return pl.pallas_call(
        outer_kernel,
        in_specs=[smem, smem] + [vmem] * 11,
        out_shape=[
            jax.ShapeDtypeStruct((HALF_ROWS, 128), BF16),
            jax.ShapeDtypeStruct((HALF_ROWS, 128), BF16),
            jax.ShapeDtypeStruct((256, 256), BF16),
            jax.ShapeDtypeStruct((4, 64, 128), BF16),
            jax.ShapeDtypeStruct((4, 64, 128), BF16),
            jax.ShapeDtypeStruct((2, 64, 128), BF16),
            jax.ShapeDtypeStruct((2, 64, 128), BF16),
        ],
        scratch_shapes=[
            pltpu.VMEM((6, 10, 64, 256), BF16),
            pltpu.VMEM((4, 6, 64, 384), BF16),
            pltpu.VMEM((4, 4, 256, 256), BF16),
            pltpu.VMEM((9, 64, 256), F32),
            pltpu.VMEM((PAY_ROWS, 128), BF16),
        ],
        compiler_params=pltpu.CompilerParams(vmem_limit_bytes=VMEM_BYTES),
        cost_estimate=pl.CostEstimate(
            flops=2_000_000_000, bytes_accessed=4_000_000, transcendentals=65536
        ),
        name="outer_grads",
    )(odd_x, odd_y, own, cot, core, chip, near, far, w_up, w_deep, sums, deep, inner)


def input_kernel(odd_x, odd_y, inner, outer, core, chip, near, far, w_up, out, taps):
    swap_x = odd_x[0] == 1
    swap_y = odd_y[0] == 1

    def x_lo(k):
        return jnp.where(swap_x, core[k], chip[k])

    def x_hi(k):
        return jnp.where(swap_x, chip[k], core[k])

    def y_lo(k):
        return jnp.where(swap_y, near[k], far[k])

    def y_hi(k):
        return jnp.where(swap_y, far[k], near[k])

    def own(u, v):
        at = (u % 2) * 128 + (v % 2) * 64
        top = ((u // 2) * 2 + (v // 2 in (2, 3))) * 64
        return (inner if v // 2 in INNER else outer)[top : top + 64, at : at + 64]

    for x in range(6):
        for y in range(10):
            taps[x, y] = depth_taps(level_column(x, y, own, x_lo, x_hi, y_lo, y_hi), 64)
    empty = jnp.zeros((64, 256), BF16)
    spare = jnp.zeros((64, 64), BF16)
    weights = {}
    for a in range(3):
        for b in range(3):
            weights[a, b] = jnp.concatenate(
                [w_up[a, b, 2], w_up[a, b, 1], w_up[a, b, 0], spare], axis=1
            )
    total = jnp.zeros((512, 256), F32)
    for x in range(4):
        for y in range(4):
            block = jnp.concatenate(
                [weights.get((s + 2 - x, t + 2 - y), empty) for s in range(2) for t in range(2)],
                axis=0,
            )
            total = total + lax.dot_general(
                window(taps, x, y, range(4)), block, (((1,), (1,)), ((), ())), preferred_element_type=F32
            )
    total = total.astype(BF16)
    for x in range(4):
        for y in range(8):
            at = (x % 2) * 128 + (y % 2) * 64
            top = ((x // 2) * 4 + y // 2) * 64
            out[x, y] = total[top : top + 64, at : at + 64]


def local_input(odd_x, odd_y, inner, outer, core, chip, near, far, w_up):
    smem = pl.BlockSpec(memory_space=pltpu.SMEM)
    vmem = pl.BlockSpec(memory_space=pltpu.VMEM)
    return pl.pallas_call(
        input_kernel,
        in_specs=[smem, smem] + [vmem] * 7,
        out_shape=jax.ShapeDtypeStruct((4, 8, 64, 64), BF16),
        scratch_shapes=[pltpu.VMEM((6, 10, 64, 256), BF16)],
        compiler_params=pltpu.CompilerParams(vmem_limit_bytes=VMEM_BYTES),
        cost_estimate=pl.CostEstimate(
            flops=1_000_000_000, bytes_accessed=4_000_000, transcendentals=0
        ),
        name="local_input",
    )(odd_x, odd_y, inner, outer, core, chip, near, far, w_up)


def unpack_kernel(up_scale, deep_scale, odd, mine, other, up, deep, payload):
    first = pl.multiple_of(odd[0] * HALF_ROWS, HALF_ROWS)
    payload[pl.ds(first, HALF_ROWS), :] = mine[...]
    payload[pl.ds(HALF_ROWS - first, HALF_ROWS), :] = other[...]
    for k in range(9):
        a, b = k // 3, k % 3
        pair = payload[k * 64 : k * 64 + 64, :].astype(F32).T * up_scale
        up[a, b, 0] = pair[:64]
        up[a, b, 1] = pair[64:]
    for k in range(5):
        top = PAIR_ROW + k * 64
        pair = payload[top : top + 64, :].astype(F32).T * up_scale
        up[2 * k // 3, 2 * k % 3, 2] = pair[:64]
        if k < 4:
            up[(2 * k + 1) // 3, (2 * k + 1) % 3, 2] = pair[64:]
    for k in range(27):
        top = DEEP_ROW + k * 64
        deep[k // 9, k // 3 % 3, k % 3] = payload[top : top + 64, :].astype(F32) * deep_scale


def unpack(odd, mine, other, up_scale, deep_scale):
    vmem = pl.BlockSpec(memory_space=pltpu.VMEM)
    return pl.pallas_call(
        functools.partial(unpack_kernel, up_scale, deep_scale),
        in_specs=[pl.BlockSpec(memory_space=pltpu.SMEM), vmem, vmem],
        out_shape=[
            jax.ShapeDtypeStruct((3, 3, 3, 64, 64), F32),
            jax.ShapeDtypeStruct((3, 3, 3, 64, 128), F32),
        ],
        scratch_shapes=[pltpu.VMEM((PAY_ROWS, 128), BF16)],
        compiler_params=pltpu.CompilerParams(vmem_limit_bytes=VMEM_BYTES),
        name="unpack",
    )(odd, mine, other)


def side_bit(step):
    index = lax.axis_index(step[0])
    return sum(index >> bit for bit in step[2]) & 1


def swap(value, steps, which):
    masks = {"gx": 0, "gy": 0}
    for place, (axis, mask, _) in enumerate(steps):
        if (which >> place) & 1:
            masks[axis] ^= mask
    axes = [axis for axis in ("gx", "gy") if masks[axis]]
    if len(axes) == 1:
        axis = axes[0]
        count = lax.axis_size(axis)
        return lax.ppermute(value, axis, [(i, i ^ masks[axis]) for i in range(count)])
    rows, cols = lax.axis_size("gx"), lax.axis_size("gy")
    pairs = [
        (i * cols + j, (i ^ masks["gx"]) * cols + (j ^ masks["gy"]))
        for i in range(rows)
        for j in range(cols)
    ]
    return lax.ppermute(value, ("gx", "gy"), pairs)


def place_of(steps):
    return sum(side_bit(step) << place for place, step in enumerate(steps))


def tree_sum(values):
    values = [value.astype(F32) for value in values]
    while len(values) > 1:
        values = [values[i] + values[i + 1] for i in range(0, len(values), 2)]
    return values[0].astype(BF16)


def scatter_sum(value, steps):
    parts = 1 << len(steps)
    rows = value.shape[0] // parts
    me = place_of(steps)
    found = [lax.dynamic_slice_in_dim(value, me * rows, rows, 0)]
    for k in range(1, parts):
        piece = lax.dynamic_slice_in_dim(value, (me ^ k) * rows, rows, 0)
        found.append(swap(piece, steps, k))
    return tree_sum(found)


def swap_sum(value, steps):
    return tree_sum([value] + [swap(value, steps, k) for k in range(1, 1 << len(steps))])


def gather(value, steps):
    parts = 1 << len(steps)
    me = place_of(steps)
    found = [value] + [swap(value, steps, k) for k in range(1, parts)]
    for place in range(len(steps)):
        near = ((me >> place) & 1) == 0
        other = 1 << place
        found = [
            jnp.where(near, found[i & ~other], found[i | other])
            if not i & other
            else jnp.where(near, found[i | other], found[i & ~other])
            for i in range(parts)
        ]
    return jnp.concatenate(found)


def pairs_of(axis, first):
    found = []
    for i in range(first, lax.axis_size(axis) - 1, 2):
        found += [(i, i + 1), (i + 1, i)]
    return found


def both_sides(first, second, axis):
    return (
        lax.ppermute(first, axis, pairs_of(axis, 0)),
        lax.ppermute(second, axis, pairs_of(axis, 1)),
    )


def column_ends(odd_x, odd_y, core, chip, head, tail, level_rows):
    lo = jnp.where(odd_x == 1, core, chip)
    hi = jnp.where(odd_x == 1, chip, core)
    left = lax.broadcasted_iota(jnp.int32, (1, 64, 128), 2) < 64
    head = [head[:2], jnp.where(left, lo[0:1], hi[0:1])] + (
        [lo[4:5], head[2:], hi[4:5]] if level_rows else []
    )
    tail = [tail[:2], jnp.where(left, hi[3:4], lo[3:4])] + (
        [lo[7:8], tail[2:], hi[7:8]] if level_rows else []
    )
    head, tail = jnp.concatenate(head), jnp.concatenate(tail)
    return jnp.where(odd_y == 1, head, tail), jnp.where(odd_y == 1, tail, head)


def local(level_input, weight_upper, weight_deep, deep_cotangent):
    tiles = lax.axis_size("gx") * lax.axis_size("gy")
    up_scale = 1.0 / math.sqrt(math.prod(level_input.shape[:3]) * tiles)
    deep_scale = 1.0 / math.sqrt(math.prod(deep_cotangent.shape[:3]) * tiles)
    odd_x = (lax.axis_index("gx") & 1).astype(jnp.int32)
    odd_y = (lax.axis_index("gy") & 1).astype(jnp.int32)
    flag_x, flag_y = odd_x.reshape(1), odd_y.reshape(1)

    to_core, to_chip, y_head, y_tail = faces(flag_x, level_input, deep_cotangent)
    core, chip = both_sides(to_core, to_chip, "gx")
    to_near, to_far = column_ends(odd_x, odd_y, core, chip, y_head, y_tail, True)
    near, far = both_sides(to_near, to_far, "gy")

    sums, deep, inner = inner_grads(
        flag_x, level_input, deep_cotangent, core, chip, weight_upper, weight_deep
    )
    keep, send, outer, to_core, to_chip, y_head, y_tail = outer_grads(
        flag_x, flag_y, level_input, deep_cotangent, core, chip, near, far,
        weight_upper, weight_deep, sums, deep, inner,
    )
    total = tree_sum([keep, swap(send, (CORE,), 1)])
    core = lax.ppermute(to_core, "gx", pairs_of("gx", 0))
    total, core = lax.optimization_barrier((total, core))
    total = scatter_sum(total, (Z_NEAR, X_NEAR))
    total, to_chip = lax.optimization_barrier((total, to_chip))
    total = swap_sum(total, (Z_FAR,))
    chip = lax.ppermute(to_chip, "gx", pairs_of("gx", 1))
    total, chip = lax.optimization_barrier((total, chip))
    to_near, to_far = column_ends(odd_x, odd_y, core, chip, y_head, y_tail, False)
    total = swap_sum(total, (X_FAR,))
    near = lax.ppermute(to_near, "gy", pairs_of("gy", 0))
    total, near, to_far = lax.optimization_barrier((total, near, to_far))
    total = swap_sum(total, (Y_NEAR,))
    far = lax.ppermute(to_far, "gy", pairs_of("gy", 1))
    total, far = lax.optimization_barrier((total, far))
    input_grad = local_input(
        flag_x, flag_y, inner, outer, core, chip, near, far, weight_upper
    )
    total = swap_sum(total, (Y_FAR,))
    total, input_grad = lax.optimization_barrier((total, input_grad))
    total = gather(total, (Z_NEAR, X_NEAR))
    other = swap(total, (CORE,), 1)
    upper, deep = unpack(flag_x, total, other, up_scale, deep_scale)
    return (input_grad, upper, deep)


def solution(mesh):
    placed = (P("gx", "gy", None, None), P(), P(), P("gx", "gy", None, None))
    return jax.shard_map(
        local,
        mesh=mesh,
        in_specs=placed,
        out_specs=(P("gx", "gy", None, None), P(), P()),
        check_vma=False,
    )
```

```python
import functools
import math

import jax
import jax.numpy as jnp
from jax import lax
from jax.experimental import pallas as pl
from jax.experimental.pallas import tpu as pltpu
from jax.sharding import PartitionSpec as P

F32 = jnp.float32
BF16 = jnp.bfloat16
VMEM_BYTES = 28 * 1024 * 1024

PAIR_ROW = 9 * 64
DEEP_ROW = 14 * 64
PAY_ROWS = 41 * 64
HALF_ROWS = PAY_ROWS // 2

CORE = ("gx", 1, (0, 1))
Y_NEAR = ("gx", 3, (1, 2))
Y_FAR = ("gx", 7, (2,))
Z_NEAR = ("gy", 1, (0, 1))
Z_FAR = ("gy", 3, (1,))
X_NEAR = ("gy", 4, (2, 3))
X_FAR = ("gy", 12, (3,))


def depth_taps(row, gap):
    row = row.astype(F32)
    edge = jnp.zeros((1, row.shape[1]), F32)
    below = jnp.concatenate([edge, row[:-1]], axis=0)
    above = jnp.concatenate([row[1:], edge], axis=0)
    pieces = [below, row, above]
    if gap:
        pieces.append(jnp.zeros((row.shape[0], gap), F32))
    return jnp.concatenate(pieces, axis=1).astype(BF16)


INNER = (1, 2)
OUTER = (0, 3)


def window(taps, at_x, at_y, ys):
    return jnp.concatenate(
        [taps[2 * x + at_x, 2 * y + at_y] for x in range(2) for y in ys], axis=0
    )


def deep_window(taps, at_x, at_y, ys):
    return jnp.concatenate([taps[x + at_x, y + at_y] for x in range(2) for y in ys], axis=0)


def faces_kernel(
    odd, own, cot, to_core, to_chip, y_head, y_tail, x_first, x_last, y_first, y_last, deep, sems
):
    copies = [
        pltpu.make_async_copy(source, target, sems.at[k])
        for k, (source, target) in enumerate(
            [
                (own.at[0], x_first),
                (own.at[3], x_last),
                (own.at[:, 0], y_first),
                (own.at[:, 7], y_last),
                (cot, deep),
            ]
        )
    ]
    for copy in copies:
        copy.start()
    for copy in copies:
        copy.wait()
    swapped = odd[0] == 1
    for k in range(4):
        head = jnp.concatenate([x_first[2 * k + 1], x_first[2 * k]], axis=1)
        tail = jnp.concatenate([x_last[2 * k], x_last[2 * k + 1]], axis=1)
        to_core[k] = jnp.where(swapped, head, tail)
        to_chip[k] = jnp.where(swapped, tail, head)
        to_core[4 + k] = jnp.where(swapped, deep[0, k], deep[1, k])
        to_chip[4 + k] = jnp.where(swapped, deep[1, k], deep[0, k])
    for k in range(2):
        y_head[k] = jnp.concatenate([y_first[2 * k], y_first[2 * k + 1]], axis=1)
        y_tail[k] = jnp.concatenate([y_last[2 * k], y_last[2 * k + 1]], axis=1)
        y_head[2 + k] = deep[k, 0]
        y_tail[2 + k] = deep[k, 3]


def faces(odd, own, cot):
    hbm = pl.BlockSpec(memory_space=pltpu.HBM)
    return pl.pallas_call(
        faces_kernel,
        in_specs=[pl.BlockSpec(memory_space=pltpu.SMEM), hbm, hbm],
        out_shape=[pltpu.VMEM((8, 64, 128), BF16)] * 2 + [pltpu.VMEM((4, 64, 128), BF16)] * 2,
        scratch_shapes=[
            pltpu.VMEM((8, 64, 64), BF16),
            pltpu.VMEM((8, 64, 64), BF16),
            pltpu.VMEM((4, 64, 64), BF16),
            pltpu.VMEM((4, 64, 64), BF16),
            pltpu.VMEM((2, 4, 64, 128), BF16),
            pltpu.SemaphoreType.DMA((5,)),
        ],
        name="faces",
    )(odd, own, cot)


def level_column(x, y, own, x_lo, x_hi, y_lo, y_hi):
    if y == 0 or y == 9:
        pairs = y_lo if y == 0 else y_hi
        if 1 <= x <= 4:
            return half(pairs(((x - 1) // 2)), (x - 1) % 2)
        return half(pairs(2), int((x == 5) == (y == 9)))
    if x == 0:
        return half(x_lo((y - 1) // 2), (y - 1) % 2)
    if x == 5:
        return half(x_hi((y - 1) // 2), 1 - (y - 1) % 2)
    return own(x - 1, y - 1)


def half(value, which):
    return value[:, which * 64 : which * 64 + 64]


def build_blocks(w_up, blocks):
    empty = jnp.zeros((192, 64), BF16)
    for x in range(3):
        for y in range(4):
            left = w_up[x, y].reshape(192, 64) if y < 3 else empty
            right = w_up[x, y - 1].reshape(192, 64) if y > 0 else empty
            pair = jnp.concatenate([left, right], axis=1)
            blocks[x, y, 0:192, 0:128] = pair
            blocks[x + 1, y, 0:192, 128:256] = pair
    for y in range(4):
        blocks[3, y, 0:192, 0:128] = jnp.zeros((192, 128), BF16)
        blocks[0, y, 0:192, 128:256] = jnp.zeros((192, 128), BF16)
        for x in range(4):
            blocks[x, y, 192:256, :] = jnp.zeros((64, 256), BF16)


def column_grads(ys, taps, cot_taps, blocks, w_deep, sums, deep):
    rows = 2 * len(ys) * 64
    pre = jnp.zeros((rows, 256), F32)
    for x in range(4):
        for y in range(4):
            pre = pre + jnp.dot(
                window(taps, x, y, ys), blocks[x, y], preferred_element_type=F32
            )
    sig = 1.0 / (1.0 + jnp.exp(-pre))
    act = pre * sig
    summed = act[:, :128] + act[:, 128:]
    pooled = 0.25 * (summed[:, :64] + summed[:, 64:])
    pooled_t = pooled.T.astype(BF16)

    pooled_grad = jnp.zeros((rows, 64), F32)
    for a in range(3):
        for b in range(3):
            weight = jnp.concatenate([w_deep[2 - a, 2 - b, 2 - j] for j in range(3)], axis=1)
            pooled_grad = pooled_grad + lax.dot_general(
                deep_window(cot_taps, a, b, ys), weight, (((1,), (1,)), ((), ())),
                preferred_element_type=F32,
            )
    wide = pooled_grad.astype(BF16).astype(F32)
    wide = jnp.concatenate([wide, wide], axis=1)
    wide = jnp.concatenate([wide, wide], axis=1)
    grad = 0.25 * wide * (sig * (1.0 + pre * (1.0 - sig)))
    grad_t = grad.T.astype(BF16)

    for a in range(3):
        for b in range(3):
            out = jnp.dot(
                pooled_t, deep_window(cot_taps, 2 - a, 2 - b, ys), preferred_element_type=F32
            )
            for j in range(3):
                deep((a * 3 + b) * 3 + 2 - j, out[:, j * 128 : j * 128 + 128])
    for x in range(4):
        for y in range(4):
            part = jnp.dot(grad_t, window(taps, x, y, ys), preferred_element_type=F32)
            for s in range(2):
                for t in range(2):
                    a, b = x - s, y - t
                    if 0 <= a < 3 and 0 <= b < 3:
                        top = (s * 2 + t) * 64
                        sums(a * 3 + b, part[top : top + 64], s == 0 and t == 0)
    return grad.astype(BF16)


def inner_kernel(odd_x, own, cot, core, chip, w_up, w_deep, sums, deep, inner, taps, cot_taps, blocks):
    swap_x = odd_x[0] == 1

    def x_lo(k):
        return jnp.where(swap_x, core[k], chip[k])

    def x_hi(k):
        return jnp.where(swap_x, chip[k], core[k])

    for x in range(6):
        for y in range(2, 8):
            row = level_column(x, y, lambda u, v: own[u, v], x_lo, x_hi, None, None)
            taps[x, y] = depth_taps(row, 64)
    for x in range(4):
        for y in range(1, 5):
            if x == 0:
                row = x_lo(3 + y)
            elif x == 3:
                row = x_hi(3 + y)
            else:
                row = cot[x - 1, y - 1]
            cot_taps[x, y] = depth_taps(row, 0)
    build_blocks(w_up, blocks)

    def add_sum(k, piece, first):
        sums[k] = piece if first else sums[k] + piece

    def add_deep(k, piece):
        deep[k] = piece

    inner[...] = column_grads(INNER, taps, cot_taps, blocks, w_deep, add_sum, add_deep)


def inner_grads(odd_x, own, cot, core, chip, w_up, w_deep):
    smem = pl.BlockSpec(memory_space=pltpu.SMEM)
    vmem = pl.BlockSpec(memory_space=pltpu.VMEM)
    return pl.pallas_call(
        inner_kernel,
        in_specs=[smem] + [vmem] * 6,
        out_shape=[
            jax.ShapeDtypeStruct((9, 64, 256), F32),
            jax.ShapeDtypeStruct((27, 64, 128), F32),
            jax.ShapeDtypeStruct((256, 256), BF16),
        ],
        scratch_shapes=[
            pltpu.VMEM((6, 10, 64, 256), BF16),
            pltpu.VMEM((4, 6, 64, 384), BF16),
            pltpu.VMEM((4, 4, 256, 256), BF16),
        ],
        compiler_params=pltpu.CompilerParams(vmem_limit_bytes=VMEM_BYTES),
        cost_estimate=pl.CostEstimate(
            flops=2_000_000_000, bytes_accessed=4_000_000, transcendentals=65536
        ),
        name="inner_grads",
    )(odd_x, own, cot, core, chip, w_up, w_deep)


def outer_kernel(
    odd_x, odd_y, part, own, cot, core, chip, near, far, w_up, w_deep, sums_in, deep_in, inner,
    keep, send, outer, to_core, to_chip, gy_head, gy_tail,
    taps, cot_taps, blocks, sums, payload,
):
    swap_x = odd_x[0] == 1
    swap_y = odd_y[0] == 1

    def x_lo(k):
        return jnp.where(swap_x, core[k], chip[k])

    def x_hi(k):
        return jnp.where(swap_x, chip[k], core[k])

    def y_lo(k):
        return jnp.where(swap_y, near[k], far[k])

    def y_hi(k):
        return jnp.where(swap_y, far[k], near[k])

    for x in range(6):
        for y in (0, 1, 2, 3, 6, 7, 8, 9):
            row = level_column(x, y, lambda u, v: own[u, v], x_lo, x_hi, y_lo, y_hi)
            taps[x, y] = depth_taps(row, 64)
    for x in range(4):
        for y in range(6):
            if y == 0:
                row = y_lo(3 + x)
            elif y == 5:
                row = y_hi(3 + x)
            elif x == 0:
                row = x_lo(3 + y)
            elif x == 3:
                row = x_hi(3 + y)
            else:
                row = cot[x - 1, y - 1]
            cot_taps[x, y] = depth_taps(row, 0)
    build_blocks(w_up, blocks)

    def add_sum(k, piece, first):
        sums[k] = (sums_in[k] if first else sums[k]) + piece

    def add_deep(k, piece):
        top = DEEP_ROW + k * 64
        payload[top : top + 64, :] = (deep_in[k] + piece).astype(BF16)

    rounded = column_grads(OUTER, taps, cot_taps, blocks, w_deep, add_sum, add_deep)
    outer[...] = rounded

    def block(x, y):
        top = (x * 2 + (y in (2, 3))) * 64
        return (inner if y in INNER else rounded)[top : top + 64]

    for k in range(4):
        head = block(0, k)[:, 0:128]
        head = jnp.concatenate([half(head, 1), half(head, 0)], axis=1)
        tail = block(1, k)[:, 128:256]
        to_core[k] = jnp.where(swap_x, head, tail)
        to_chip[k] = jnp.where(swap_x, tail, head)
    for k in range(2):
        first, last = block(k, 0), block(k, 3)
        gy_head[k] = jnp.concatenate([first[:, 0:64], first[:, 128:192]], axis=1)
        gy_tail[k] = jnp.concatenate([last[:, 64:128], last[:, 192:256]], axis=1)

    for k in range(9):
        payload[k * 64 : k * 64 + 64, :] = sums[k, :, 0:128].astype(BF16)
    for k in range(5):
        left = sums[2 * k, :, 128:192]
        right = sums[2 * k + 1, :, 128:192] if k < 4 else jnp.zeros((64, 64), F32)
        top = PAIR_ROW + k * 64
        payload[top : top + 64, :] = jnp.concatenate([left, right], axis=1).astype(BF16)
    mine = pl.multiple_of(part[0] * HALF_ROWS, HALF_ROWS)
    keep[...] = payload[pl.ds(mine, HALF_ROWS), :]
    send[...] = payload[pl.ds(HALF_ROWS - mine, HALF_ROWS), :]


def outer_grads(odd_x, odd_y, part, own, cot, core, chip, near, far, w_up, w_deep, sums, deep, inner):
    smem = pl.BlockSpec(memory_space=pltpu.SMEM)
    vmem = pl.BlockSpec(memory_space=pltpu.VMEM)
    return pl.pallas_call(
        outer_kernel,
        in_specs=[smem] * 3 + [vmem] * 11,
        out_shape=[
            jax.ShapeDtypeStruct((HALF_ROWS, 128), BF16),
            jax.ShapeDtypeStruct((HALF_ROWS, 128), BF16),
            jax.ShapeDtypeStruct((256, 256), BF16),
            jax.ShapeDtypeStruct((4, 64, 128), BF16),
            jax.ShapeDtypeStruct((4, 64, 128), BF16),
            jax.ShapeDtypeStruct((2, 64, 128), BF16),
            jax.ShapeDtypeStruct((2, 64, 128), BF16),
        ],
        scratch_shapes=[
            pltpu.VMEM((6, 10, 64, 256), BF16),
            pltpu.VMEM((4, 6, 64, 384), BF16),
            pltpu.VMEM((4, 4, 256, 256), BF16),
            pltpu.VMEM((9, 64, 256), F32),
            pltpu.VMEM((PAY_ROWS, 128), BF16),
        ],
        compiler_params=pltpu.CompilerParams(vmem_limit_bytes=VMEM_BYTES),
        cost_estimate=pl.CostEstimate(
            flops=2_000_000_000, bytes_accessed=4_000_000, transcendentals=65536
        ),
        name="outer_grads",
    )(odd_x, odd_y, part, own, cot, core, chip, near, far, w_up, w_deep, sums, deep, inner)


def input_columns(ys, taps, w_up):
    empty = jnp.zeros((64, 256), BF16)
    spare = jnp.zeros((64, 64), BF16)
    weights = {}
    for a in range(3):
        for b in range(3):
            weights[a, b] = jnp.concatenate(
                [w_up[a, b, 2], w_up[a, b, 1], w_up[a, b, 0], spare], axis=1
            )
    total = jnp.zeros((2 * len(ys) * 64, 256), F32)
    for x in range(4):
        for y in range(4):
            block = jnp.concatenate(
                [weights.get((s + 2 - x, t + 2 - y), empty) for s in range(2) for t in range(2)],
                axis=0,
            )
            total = total + lax.dot_general(
                window(taps, x, y, ys), block, (((1,), (1,)), ((), ())),
                preferred_element_type=F32,
            )
    return total.astype(BF16)


def picked(inner, outer, x, y):
    at = (x % 2) * 128 + (y % 2) * 64
    top = ((x // 2) * 2 + (y // 2 in (2, 3))) * 64
    return (inner if y // 2 in INNER else outer)[top : top + 64, at : at + 64]


def inner_input_kernel(odd_x, inner, outer, core, chip, w_up, out, taps):
    swap_x = odd_x[0] == 1

    def x_lo(k):
        return jnp.where(swap_x, core[k], chip[k])

    def x_hi(k):
        return jnp.where(swap_x, chip[k], core[k])

    def own(u, v):
        return picked(inner, outer, u, v)

    for x in range(6):
        for y in range(2, 8):
            taps[x, y] = depth_taps(level_column(x, y, own, x_lo, x_hi, None, None), 64)
    out[...] = input_columns(INNER, taps, w_up)


def inner_input(odd_x, inner, outer, core, chip, w_up):
    smem = pl.BlockSpec(memory_space=pltpu.SMEM)
    vmem = pl.BlockSpec(memory_space=pltpu.VMEM)
    return pl.pallas_call(
        inner_input_kernel,
        in_specs=[smem] + [vmem] * 5,
        out_shape=jax.ShapeDtypeStruct((256, 256), BF16),
        scratch_shapes=[pltpu.VMEM((6, 10, 64, 256), BF16)],
        compiler_params=pltpu.CompilerParams(vmem_limit_bytes=VMEM_BYTES),
        cost_estimate=pl.CostEstimate(
            flops=500_000_000, bytes_accessed=2_000_000, transcendentals=0
        ),
        name="inner_input",
    )(odd_x, inner, outer, core, chip, w_up)


def outer_input_kernel(
    odd_x, odd_y, inner, outer, core, chip, near, far, w_up, inner_part, out, taps
):
    swap_x = odd_x[0] == 1
    swap_y = odd_y[0] == 1

    def x_lo(k):
        return jnp.where(swap_x, core[k], chip[k])

    def x_hi(k):
        return jnp.where(swap_x, chip[k], core[k])

    def y_lo(k):
        return jnp.where(swap_y, near[k], far[k])

    def y_hi(k):
        return jnp.where(swap_y, far[k], near[k])

    def own(u, v):
        return picked(inner, outer, u, v)

    for x in range(6):
        for y in (0, 1, 2, 3, 6, 7, 8, 9):
            taps[x, y] = depth_taps(level_column(x, y, own, x_lo, x_hi, y_lo, y_hi), 64)
    outer_part = input_columns(OUTER, taps, w_up)
    for x in range(4):
        for y in range(8):
            out[x, y] = picked(inner_part, outer_part, x, y)


def outer_input(odd_x, odd_y, inner, outer, core, chip, near, far, w_up, inner_part):
    smem = pl.BlockSpec(memory_space=pltpu.SMEM)
    vmem = pl.BlockSpec(memory_space=pltpu.VMEM)
    return pl.pallas_call(
        outer_input_kernel,
        in_specs=[smem, smem] + [vmem] * 8,
        out_shape=jax.ShapeDtypeStruct((4, 8, 64, 64), BF16),
        scratch_shapes=[pltpu.VMEM((6, 10, 64, 256), BF16)],
        compiler_params=pltpu.CompilerParams(vmem_limit_bytes=VMEM_BYTES),
        cost_estimate=pl.CostEstimate(
            flops=500_000_000, bytes_accessed=4_000_000, transcendentals=0
        ),
        name="outer_input",
    )(odd_x, odd_y, inner, outer, core, chip, near, far, w_up, inner_part)


def unpack_kernel(up_scale, deep_scale, odd, mine, other, up, deep, payload):
    first = pl.multiple_of(odd[0] * HALF_ROWS, HALF_ROWS)
    payload[pl.ds(first, HALF_ROWS), :] = mine[...]
    payload[pl.ds(HALF_ROWS - first, HALF_ROWS), :] = other[...]
    for k in range(9):
        a, b = k // 3, k % 3
        pair = payload[k * 64 : k * 64 + 64, :].astype(F32).T * up_scale
        up[a, b, 0] = pair[:64]
        up[a, b, 1] = pair[64:]
    for k in range(5):
        top = PAIR_ROW + k * 64
        pair = payload[top : top + 64, :].astype(F32).T * up_scale
        up[2 * k // 3, 2 * k % 3, 2] = pair[:64]
        if k < 4:
            up[(2 * k + 1) // 3, (2 * k + 1) % 3, 2] = pair[64:]
    for k in range(27):
        top = DEEP_ROW + k * 64
        deep[k // 9, k // 3 % 3, k % 3] = payload[top : top + 64, :].astype(F32) * deep_scale


def unpack(odd, mine, other, up_scale, deep_scale):
    vmem = pl.BlockSpec(memory_space=pltpu.VMEM)
    return pl.pallas_call(
        functools.partial(unpack_kernel, up_scale, deep_scale),
        in_specs=[pl.BlockSpec(memory_space=pltpu.SMEM), vmem, vmem],
        out_shape=[
            jax.ShapeDtypeStruct((3, 3, 3, 64, 64), F32),
            jax.ShapeDtypeStruct((3, 3, 3, 64, 128), F32),
        ],
        scratch_shapes=[pltpu.VMEM((PAY_ROWS, 128), BF16)],
        compiler_params=pltpu.CompilerParams(vmem_limit_bytes=VMEM_BYTES),
        name="unpack",
    )(odd, mine, other)


def side_bit(step):
    index = lax.axis_index(step[0])
    return sum(index >> bit for bit in step[2]) & 1


def swap(value, steps, which):
    masks = {"gx": 0, "gy": 0}
    for place, (axis, mask, _) in enumerate(steps):
        if (which >> place) & 1:
            masks[axis] ^= mask
    axes = [axis for axis in ("gx", "gy") if masks[axis]]
    if len(axes) == 1:
        axis = axes[0]
        count = lax.axis_size(axis)
        return lax.ppermute(value, axis, [(i, i ^ masks[axis]) for i in range(count)])
    rows, cols = lax.axis_size("gx"), lax.axis_size("gy")
    pairs = [
        (i * cols + j, (i ^ masks["gx"]) * cols + (j ^ masks["gy"]))
        for i in range(rows)
        for j in range(cols)
    ]
    return lax.ppermute(value, ("gx", "gy"), pairs)


def place_of(steps):
    return sum(side_bit(step) << place for place, step in enumerate(steps))


def tree_sum(values):
    values = [value.astype(F32) for value in values]
    while len(values) > 1:
        values = [values[i] + values[i + 1] for i in range(0, len(values), 2)]
    return values[0].astype(BF16)


def scatter_sum(value, steps):
    parts = 1 << len(steps)
    rows = value.shape[0] // parts
    me = place_of(steps)
    found = [lax.dynamic_slice_in_dim(value, me * rows, rows, 0)]
    for k in range(1, parts):
        piece = lax.dynamic_slice_in_dim(value, (me ^ k) * rows, rows, 0)
        found.append(swap(piece, steps, k))
    return tree_sum(found)


def swap_sum(value, step):
    return tree_sum([value, swap(value, (step,), 1)])


def swap_sum_with(value, step, rider):
    rows = value.shape[0]
    got = swap(jnp.concatenate([value, rider]), (step,), 1)
    return tree_sum([value, got[:rows]]), got[rows:]


def gather(value, steps, riders):
    parts = 1 << len(steps)
    rows = value.shape[0]
    me = place_of(steps)
    found, came = [value], []
    for k in range(1, parts):
        rider = riders[k - 1]
        sent = value if rider is None else jnp.concatenate([value, rider])
        got = swap(sent, steps, k)
        found.append(got[:rows])
        came.append(got[rows:])
    for place in range(len(steps)):
        near = ((me >> place) & 1) == 0
        other = 1 << place
        found = [
            jnp.where(near, found[i & ~other], found[i | other])
            if not i & other
            else jnp.where(near, found[i | other], found[i & ~other])
            for i in range(parts)
        ]
    return jnp.concatenate(found), came


def pairs_of(axis, first):
    found = []
    for i in range(first, lax.axis_size(axis) - 1, 2):
        found += [(i, i + 1), (i + 1, i)]
    return found


def chip_pairs(which):
    return [pair for pair in pairs_of("gx", 1) if (pair[0] + 1) // 2 % 2 == which]


def both_sides(first, second, axis):
    return (
        lax.ppermute(first, axis, pairs_of(axis, 0)),
        lax.ppermute(second, axis, pairs_of(axis, 1)),
    )


def column_ends(odd_x, odd_y, core, chip, head, tail, level_rows):
    lo = jnp.where(odd_x == 1, core, chip)
    hi = jnp.where(odd_x == 1, chip, core)
    left = lax.broadcasted_iota(jnp.int32, (1, 64, 128), 2) < 64
    head = [head[:2], jnp.where(left, lo[0:1], hi[0:1])] + (
        [lo[4:5], head[2:], hi[4:5]] if level_rows else []
    )
    tail = [tail[:2], jnp.where(left, hi[3:4], lo[3:4])] + (
        [lo[7:8], tail[2:], hi[7:8]] if level_rows else []
    )
    head, tail = jnp.concatenate(head), jnp.concatenate(tail)
    return jnp.where(odd_y == 1, head, tail), jnp.where(odd_y == 1, tail, head)


def local(level_input, weight_upper, weight_deep, deep_cotangent):
    tiles = lax.axis_size("gx") * lax.axis_size("gy")
    up_scale = 1.0 / math.sqrt(math.prod(level_input.shape[:3]) * tiles)
    deep_scale = 1.0 / math.sqrt(math.prod(deep_cotangent.shape[:3]) * tiles)
    odd_x = (lax.axis_index("gx") & 1).astype(jnp.int32)
    odd_y = (lax.axis_index("gy") & 1).astype(jnp.int32)
    flag_x, flag_y = odd_x.reshape(1), odd_y.reshape(1)
    part = side_bit(CORE).astype(jnp.int32).reshape(1)

    to_core, to_chip, y_head, y_tail = faces(
        flag_x,
        pltpu.with_memory_space_constraint(level_input, pltpu.HBM),
        pltpu.with_memory_space_constraint(deep_cotangent, pltpu.HBM),
    )
    core, chip = both_sides(to_core, to_chip, "gx")
    to_near, to_far = column_ends(odd_x, odd_y, core, chip, y_head, y_tail, True)
    near, far = both_sides(to_near, to_far, "gy")

    sums, deep, inner = inner_grads(
        flag_x, level_input, deep_cotangent, core, chip, weight_upper, weight_deep
    )
    keep, send, outer, to_core, to_chip, y_head, y_tail = outer_grads(
        flag_x, flag_y, part, level_input, deep_cotangent, core, chip, near, far,
        weight_upper, weight_deep, sums, deep, inner,
    )
    at_x, at_y = lax.axis_index("gx"), lax.axis_index("gy")
    total = tree_sum([keep, swap(send, (CORE,), 1)])
    core = lax.ppermute(to_core, "gx", pairs_of("gx", 0))
    total, core = lax.optimization_barrier((total, core))
    total = scatter_sum(total, (Z_NEAR, X_NEAR))
    total, to_chip = lax.optimization_barrier((total, to_chip))
    first = lax.ppermute(to_chip, "gx", chip_pairs(1))
    total = swap_sum(total, Y_NEAR)
    total, to_chip, first = lax.optimization_barrier((total, to_chip, first))
    second = lax.ppermute(to_chip, "gx", chip_pairs(0))
    total = swap_sum(total, Y_FAR)
    chip = jnp.where((((at_x + 1) >> 1) & 1) == 1, first, second)
    inner_part = inner_input(flag_x, inner, outer, core, chip, weight_upper)
    to_near, to_far = column_ends(odd_x, odd_y, core, chip, y_head, y_tail, False)
    total, direct = swap_sum_with(total, Z_FAR, to_far.reshape(-1, 128))
    total, handed_far = swap_sum_with(total, X_FAR, direct)
    total, inner_part = lax.optimization_barrier((total, inner_part))
    total, (near, handed_near, _) = gather(
        total, (Z_NEAR, X_NEAR), (to_near.reshape(-1, 128), direct, None)
    )
    plane, depth = at_y >> 2, at_y & 3
    none = jnp.zeros_like(direct)
    handed = jnp.where(
        ((depth == 0) & (plane == 2)) | ((depth == 3) & (plane == 1)), handed_far, handed_near
    )
    ends = (at_y == 0) | (at_y == lax.axis_size("gy") - 1)
    far = jnp.where((depth == 1) | (depth == 2), direct, jnp.where(ends, none, handed))
    input_grad = outer_input(
        flag_x, flag_y, inner, outer, core, chip, near.reshape(to_near.shape),
        far.reshape(to_far.shape), weight_upper, inner_part,
    )
    other = swap(total, (CORE,), 1)
    upper, deep = unpack(part, total, other, up_scale, deep_scale)
    return (input_grad, upper, deep)


def solution(mesh):
    placed = (P("gx", "gy", None, None), P(), P(), P("gx", "gy", None, None))
    return jax.shard_map(
        local,
        mesh=mesh,
        in_specs=placed,
        out_specs=(P("gx", "gy", None, None), P(), P()),
        check_vma=False,
    )
```

```python
import functools
import math

import jax
import jax.numpy as jnp
from jax import lax
from jax.experimental import pallas as pl
from jax.experimental.pallas import tpu as pltpu
from jax.sharding import PartitionSpec as P

F32 = jnp.float32
BF16 = jnp.bfloat16
VMEM_BYTES = 28 * 1024 * 1024

PAIR_ROW = 9 * 64
DEEP_ROW = 14 * 64
PAY_ROWS = 41 * 64
HALF_ROWS = PAY_ROWS // 2

CORE = ("gx", 1, (0, 1))
Y_NEAR = ("gx", 3, (1, 2))
Y_FAR = ("gx", 7, (2,))
Z_NEAR = ("gy", 1, (0, 1))
Z_FAR = ("gy", 3, (1,))
X_NEAR = ("gy", 4, (2, 3))
X_FAR = ("gy", 12, (3,))


def depth_taps(row, gap):
    row = row.astype(F32)
    edge = jnp.zeros((1, row.shape[1]), F32)
    below = jnp.concatenate([edge, row[:-1]], axis=0)
    above = jnp.concatenate([row[1:], edge], axis=0)
    pieces = [below, row, above]
    if gap:
        pieces.append(jnp.zeros((row.shape[0], gap), F32))
    return jnp.concatenate(pieces, axis=1).astype(BF16)


INNER = (1, 2)
OUTER = (0, 3)


def window(taps, at_x, at_y, ys):
    return jnp.concatenate(
        [taps[2 * x + at_x, 2 * y + at_y] for x in range(2) for y in ys], axis=0
    )


def deep_window(taps, at_x, at_y, ys):
    return jnp.concatenate([taps[x + at_x, y + at_y] for x in range(2) for y in ys], axis=0)


def faces_kernel(
    odd, own, cot, to_core, to_chip, y_head, y_tail, x_first, x_last, y_first, y_last, deep, sems
):
    copies = [
        pltpu.make_async_copy(source, target, sems.at[k])
        for k, (source, target) in enumerate(
            [
                (own.at[0], x_first),
                (own.at[3], x_last),
                (own.at[:, 0], y_first),
                (own.at[:, 7], y_last),
                (cot, deep),
            ]
        )
    ]
    for copy in copies:
        copy.start()
    for copy in copies:
        copy.wait()
    swapped = odd[0] == 1
    for k in range(4):
        head = jnp.concatenate([x_first[2 * k + 1], x_first[2 * k]], axis=1)
        tail = jnp.concatenate([x_last[2 * k], x_last[2 * k + 1]], axis=1)
        to_core[k] = jnp.where(swapped, head, tail)
        to_chip[k] = jnp.where(swapped, tail, head)
        to_core[4 + k] = jnp.where(swapped, deep[0, k], deep[1, k])
        to_chip[4 + k] = jnp.where(swapped, deep[1, k], deep[0, k])
    for k in range(2):
        y_head[k] = jnp.concatenate([y_first[2 * k], y_first[2 * k + 1]], axis=1)
        y_tail[k] = jnp.concatenate([y_last[2 * k], y_last[2 * k + 1]], axis=1)
        y_head[2 + k] = deep[k, 0]
        y_tail[2 + k] = deep[k, 3]


def faces(odd, own, cot):
    hbm = pl.BlockSpec(memory_space=pltpu.HBM)
    return pl.pallas_call(
        faces_kernel,
        in_specs=[pl.BlockSpec(memory_space=pltpu.SMEM), hbm, hbm],
        out_shape=[pltpu.VMEM((8, 64, 128), BF16)] * 2 + [pltpu.VMEM((4, 64, 128), BF16)] * 2,
        scratch_shapes=[
            pltpu.VMEM((8, 64, 64), BF16),
            pltpu.VMEM((8, 64, 64), BF16),
            pltpu.VMEM((4, 64, 64), BF16),
            pltpu.VMEM((4, 64, 64), BF16),
            pltpu.VMEM((2, 4, 64, 128), BF16),
            pltpu.SemaphoreType.DMA((5,)),
        ],
        name="faces",
    )(odd, own, cot)


def level_column(x, y, own, x_lo, x_hi, y_lo, y_hi):
    if y == 0 or y == 9:
        pairs = y_lo if y == 0 else y_hi
        if 1 <= x <= 4:
            return half(pairs(((x - 1) // 2)), (x - 1) % 2)
        return half(pairs(2), int((x == 5) == (y == 9)))
    if x == 0:
        return half(x_lo((y - 1) // 2), (y - 1) % 2)
    if x == 5:
        return half(x_hi((y - 1) // 2), 1 - (y - 1) % 2)
    return own(x - 1, y - 1)


def half(value, which):
    return value[:, which * 64 : which * 64 + 64]


def build_blocks(w_up, blocks):
    empty = jnp.zeros((192, 64), BF16)
    for x in range(3):
        for y in range(4):
            left = w_up[x, y].reshape(192, 64) if y < 3 else empty
            right = w_up[x, y - 1].reshape(192, 64) if y > 0 else empty
            pair = jnp.concatenate([left, right], axis=1)
            blocks[x, y, 0:192, 0:128] = pair
            blocks[x + 1, y, 0:192, 128:256] = pair
    for y in range(4):
        blocks[3, y, 0:192, 0:128] = jnp.zeros((192, 128), BF16)
        blocks[0, y, 0:192, 128:256] = jnp.zeros((192, 128), BF16)
        for x in range(4):
            blocks[x, y, 192:256, :] = jnp.zeros((64, 256), BF16)


def column_grads(ys, taps, cot_taps, blocks, w_deep, sums, deep):
    rows = 2 * len(ys) * 64
    pre = jnp.zeros((rows, 256), F32)
    for x in range(4):
        for y in range(4):
            pre = pre + jnp.dot(
                window(taps, x, y, ys), blocks[x, y], preferred_element_type=F32
            )
    sig = 1.0 / (1.0 + jnp.exp(-pre))
    act = pre * sig
    summed = act[:, :128] + act[:, 128:]
    pooled = 0.25 * (summed[:, :64] + summed[:, 64:])
    pooled_t = pooled.T.astype(BF16)

    pooled_grad = jnp.zeros((rows, 64), F32)
    for a in range(3):
        for b in range(3):
            weight = jnp.concatenate([w_deep[2 - a, 2 - b, 2 - j] for j in range(3)], axis=1)
            pooled_grad = pooled_grad + lax.dot_general(
                deep_window(cot_taps, a, b, ys), weight, (((1,), (1,)), ((), ())),
                preferred_element_type=F32,
            )
    wide = pooled_grad.astype(BF16).astype(F32)
    wide = jnp.concatenate([wide, wide], axis=1)
    wide = jnp.concatenate([wide, wide], axis=1)
    grad = 0.25 * wide * (sig * (1.0 + pre * (1.0 - sig)))
    grad_t = grad.T.astype(BF16)

    for a in range(3):
        for b in range(3):
            out = jnp.dot(
                pooled_t, deep_window(cot_taps, 2 - a, 2 - b, ys), preferred_element_type=F32
            )
            for j in range(3):
                deep((a * 3 + b) * 3 + 2 - j, out[:, j * 128 : j * 128 + 128])
    for x in range(4):
        for y in range(4):
            part = jnp.dot(grad_t, window(taps, x, y, ys), preferred_element_type=F32)
            for s in range(2):
                for t in range(2):
                    a, b = x - s, y - t
                    if 0 <= a < 3 and 0 <= b < 3:
                        top = (s * 2 + t) * 64
                        sums(a * 3 + b, part[top : top + 64], s == 0 and t == 0)
    return grad.astype(BF16)


def inner_kernel(odd_x, own, cot, core, chip, w_up, w_deep, sums, deep, inner, taps, cot_taps, blocks):
    swap_x = odd_x[0] == 1

    def x_lo(k):
        return jnp.where(swap_x, core[k], chip[k])

    def x_hi(k):
        return jnp.where(swap_x, chip[k], core[k])

    for x in range(6):
        for y in range(2, 8):
            row = level_column(x, y, lambda u, v: own[u, v], x_lo, x_hi, None, None)
            taps[x, y] = depth_taps(row, 64)
    for x in range(4):
        for y in range(1, 5):
            if x == 0:
                row = x_lo(3 + y)
            elif x == 3:
                row = x_hi(3 + y)
            else:
                row = cot[x - 1, y - 1]
            cot_taps[x, y] = depth_taps(row, 0)
    build_blocks(w_up, blocks)

    def add_sum(k, piece, first):
        sums[k] = piece if first else sums[k] + piece

    def add_deep(k, piece):
        deep[k] = piece

    inner[...] = column_grads(INNER, taps, cot_taps, blocks, w_deep, add_sum, add_deep)


def inner_grads(odd_x, own, cot, core, chip, w_up, w_deep):
    smem = pl.BlockSpec(memory_space=pltpu.SMEM)
    vmem = pl.BlockSpec(memory_space=pltpu.VMEM)
    return pl.pallas_call(
        inner_kernel,
        in_specs=[smem] + [vmem] * 6,
        out_shape=[
            jax.ShapeDtypeStruct((9, 64, 256), F32),
            jax.ShapeDtypeStruct((27, 64, 128), F32),
            jax.ShapeDtypeStruct((256, 256), BF16),
        ],
        scratch_shapes=[
            pltpu.VMEM((6, 10, 64, 256), BF16),
            pltpu.VMEM((4, 6, 64, 384), BF16),
            pltpu.VMEM((4, 4, 256, 256), BF16),
        ],
        compiler_params=pltpu.CompilerParams(vmem_limit_bytes=VMEM_BYTES),
        cost_estimate=pl.CostEstimate(
            flops=2_000_000_000, bytes_accessed=4_000_000, transcendentals=65536
        ),
        name="inner_grads",
    )(odd_x, own, cot, core, chip, w_up, w_deep)


def outer_kernel(
    odd_x, odd_y, part, own, cot, core, chip, near, far, w_up, w_deep, sums_in, deep_in, inner,
    keep, send, outer, to_core, to_chip, gy_head, gy_tail,
    taps, cot_taps, blocks, sums, payload,
):
    swap_x = odd_x[0] == 1
    swap_y = odd_y[0] == 1

    def x_lo(k):
        return jnp.where(swap_x, core[k], chip[k])

    def x_hi(k):
        return jnp.where(swap_x, chip[k], core[k])

    def y_lo(k):
        return jnp.where(swap_y, near[k], far[k])

    def y_hi(k):
        return jnp.where(swap_y, far[k], near[k])

    for x in range(6):
        for y in (0, 1, 2, 3, 6, 7, 8, 9):
            row = level_column(x, y, lambda u, v: own[u, v], x_lo, x_hi, y_lo, y_hi)
            taps[x, y] = depth_taps(row, 64)
    for x in range(4):
        for y in range(6):
            if y == 0:
                row = y_lo(3 + x)
            elif y == 5:
                row = y_hi(3 + x)
            elif x == 0:
                row = x_lo(3 + y)
            elif x == 3:
                row = x_hi(3 + y)
            else:
                row = cot[x - 1, y - 1]
            cot_taps[x, y] = depth_taps(row, 0)
    build_blocks(w_up, blocks)

    def add_sum(k, piece, first):
        sums[k] = (sums_in[k] if first else sums[k]) + piece

    def add_deep(k, piece):
        top = DEEP_ROW + k * 64
        payload[top : top + 64, :] = (deep_in[k] + piece).astype(BF16)

    rounded = column_grads(OUTER, taps, cot_taps, blocks, w_deep, add_sum, add_deep)
    outer[...] = rounded

    def block(x, y):
        top = (x * 2 + (y in (2, 3))) * 64
        return (inner if y in INNER else rounded)[top : top + 64]

    for k in range(4):
        head = block(0, k)[:, 0:128]
        head = jnp.concatenate([half(head, 1), half(head, 0)], axis=1)
        tail = block(1, k)[:, 128:256]
        to_core[k] = jnp.where(swap_x, head, tail)
        to_chip[k] = jnp.where(swap_x, tail, head)
    for k in range(2):
        first, last = block(k, 0), block(k, 3)
        gy_head[k] = jnp.concatenate([first[:, 0:64], first[:, 128:192]], axis=1)
        gy_tail[k] = jnp.concatenate([last[:, 64:128], last[:, 192:256]], axis=1)

    for k in range(9):
        payload[k * 64 : k * 64 + 64, :] = sums[k, :, 0:128].astype(BF16)
    for k in range(5):
        left = sums[2 * k, :, 128:192]
        right = sums[2 * k + 1, :, 128:192] if k < 4 else jnp.zeros((64, 64), F32)
        top = PAIR_ROW + k * 64
        payload[top : top + 64, :] = jnp.concatenate([left, right], axis=1).astype(BF16)
    mine = pl.multiple_of(part[0] * HALF_ROWS, HALF_ROWS)
    keep[...] = payload[pl.ds(mine, HALF_ROWS), :]
    send[...] = payload[pl.ds(HALF_ROWS - mine, HALF_ROWS), :]


def outer_grads(odd_x, odd_y, part, own, cot, core, chip, near, far, w_up, w_deep, sums, deep, inner):
    smem = pl.BlockSpec(memory_space=pltpu.SMEM)
    vmem = pl.BlockSpec(memory_space=pltpu.VMEM)
    return pl.pallas_call(
        outer_kernel,
        in_specs=[smem] * 3 + [vmem] * 11,
        out_shape=[
            jax.ShapeDtypeStruct((HALF_ROWS, 128), BF16),
            jax.ShapeDtypeStruct((HALF_ROWS, 128), BF16),
            jax.ShapeDtypeStruct((256, 256), BF16),
            jax.ShapeDtypeStruct((4, 64, 128), BF16),
            jax.ShapeDtypeStruct((4, 64, 128), BF16),
            jax.ShapeDtypeStruct((2, 64, 128), BF16),
            jax.ShapeDtypeStruct((2, 64, 128), BF16),
        ],
        scratch_shapes=[
            pltpu.VMEM((6, 10, 64, 256), BF16),
            pltpu.VMEM((4, 6, 64, 384), BF16),
            pltpu.VMEM((4, 4, 256, 256), BF16),
            pltpu.VMEM((9, 64, 256), F32),
            pltpu.VMEM((PAY_ROWS, 128), BF16),
        ],
        compiler_params=pltpu.CompilerParams(vmem_limit_bytes=VMEM_BYTES),
        cost_estimate=pl.CostEstimate(
            flops=2_000_000_000, bytes_accessed=4_000_000, transcendentals=65536
        ),
        name="outer_grads",
    )(odd_x, odd_y, part, own, cot, core, chip, near, far, w_up, w_deep, sums, deep, inner)


def input_columns(ys, taps, w_up):
    empty = jnp.zeros((64, 256), BF16)
    spare = jnp.zeros((64, 64), BF16)
    weights = {}
    for a in range(3):
        for b in range(3):
            weights[a, b] = jnp.concatenate(
                [w_up[a, b, 2], w_up[a, b, 1], w_up[a, b, 0], spare], axis=1
            )
    total = jnp.zeros((2 * len(ys) * 64, 256), F32)
    for x in range(4):
        for y in range(4):
            block = jnp.concatenate(
                [weights.get((s + 2 - x, t + 2 - y), empty) for s in range(2) for t in range(2)],
                axis=0,
            )
            total = total + lax.dot_general(
                window(taps, x, y, ys), block, (((1,), (1,)), ((), ())),
                preferred_element_type=F32,
            )
    return total.astype(BF16)


def picked(inner, outer, x, y):
    at = (x % 2) * 128 + (y % 2) * 64
    top = ((x // 2) * 2 + (y // 2 in (2, 3))) * 64
    return (inner if y // 2 in INNER else outer)[top : top + 64, at : at + 64]


def inner_input_kernel(odd_x, inner, outer, core, chip, w_up, out, taps):
    swap_x = odd_x[0] == 1

    def x_lo(k):
        return jnp.where(swap_x, core[k], chip[k])

    def x_hi(k):
        return jnp.where(swap_x, chip[k], core[k])

    def own(u, v):
        return picked(inner, outer, u, v)

    for x in range(6):
        for y in range(2, 8):
            taps[x, y] = depth_taps(level_column(x, y, own, x_lo, x_hi, None, None), 64)
    out[...] = input_columns(INNER, taps, w_up)


def inner_input(odd_x, inner, outer, core, chip, w_up):
    smem = pl.BlockSpec(memory_space=pltpu.SMEM)
    vmem = pl.BlockSpec(memory_space=pltpu.VMEM)
    return pl.pallas_call(
        inner_input_kernel,
        in_specs=[smem] + [vmem] * 5,
        out_shape=jax.ShapeDtypeStruct((256, 256), BF16),
        scratch_shapes=[pltpu.VMEM((6, 10, 64, 256), BF16)],
        compiler_params=pltpu.CompilerParams(vmem_limit_bytes=VMEM_BYTES),
        cost_estimate=pl.CostEstimate(
            flops=500_000_000, bytes_accessed=2_000_000, transcendentals=0
        ),
        name="inner_input",
    )(odd_x, inner, outer, core, chip, w_up)


def outer_input_kernel(
    odd_x, odd_y, inner, outer, core, chip, near, far, w_up, inner_part, out, taps
):
    swap_x = odd_x[0] == 1
    swap_y = odd_y[0] == 1

    def x_lo(k):
        return jnp.where(swap_x, core[k], chip[k])

    def x_hi(k):
        return jnp.where(swap_x, chip[k], core[k])

    def y_lo(k):
        return jnp.where(swap_y, near[k], far[k])

    def y_hi(k):
        return jnp.where(swap_y, far[k], near[k])

    def own(u, v):
        return picked(inner, outer, u, v)

    for x in range(6):
        for y in (0, 1, 2, 3, 6, 7, 8, 9):
            taps[x, y] = depth_taps(level_column(x, y, own, x_lo, x_hi, y_lo, y_hi), 64)
    outer_part = input_columns(OUTER, taps, w_up)
    for x in range(4):
        for y in range(8):
            out[x, y] = picked(inner_part, outer_part, x, y)


def outer_input(odd_x, odd_y, inner, outer, core, chip, near, far, w_up, inner_part):
    smem = pl.BlockSpec(memory_space=pltpu.SMEM)
    vmem = pl.BlockSpec(memory_space=pltpu.VMEM)
    return pl.pallas_call(
        outer_input_kernel,
        in_specs=[smem, smem] + [vmem] * 8,
        out_shape=jax.ShapeDtypeStruct((4, 8, 64, 64), BF16),
        scratch_shapes=[pltpu.VMEM((6, 10, 64, 256), BF16)],
        compiler_params=pltpu.CompilerParams(vmem_limit_bytes=VMEM_BYTES),
        cost_estimate=pl.CostEstimate(
            flops=500_000_000, bytes_accessed=4_000_000, transcendentals=0
        ),
        name="outer_input",
    )(odd_x, odd_y, inner, outer, core, chip, near, far, w_up, inner_part)


def unpack_kernel(up_scale, deep_scale, odd, mine, other, up, deep, payload):
    first = pl.multiple_of(odd[0] * HALF_ROWS, HALF_ROWS)
    payload[pl.ds(first, HALF_ROWS), :] = mine[...]
    payload[pl.ds(HALF_ROWS - first, HALF_ROWS), :] = other[...]
    for k in range(9):
        a, b = k // 3, k % 3
        pair = payload[k * 64 : k * 64 + 64, :].astype(F32).T * up_scale
        up[a, b, 0] = pair[:64]
        up[a, b, 1] = pair[64:]
    for k in range(5):
        top = PAIR_ROW + k * 64
        pair = payload[top : top + 64, :].astype(F32).T * up_scale
        up[2 * k // 3, 2 * k % 3, 2] = pair[:64]
        if k < 4:
            up[(2 * k + 1) // 3, (2 * k + 1) % 3, 2] = pair[64:]
    for k in range(27):
        top = DEEP_ROW + k * 64
        deep[k // 9, k // 3 % 3, k % 3] = payload[top : top + 64, :].astype(F32) * deep_scale


def unpack(odd, mine, other, up_scale, deep_scale):
    vmem = pl.BlockSpec(memory_space=pltpu.VMEM)
    return pl.pallas_call(
        functools.partial(unpack_kernel, up_scale, deep_scale),
        in_specs=[pl.BlockSpec(memory_space=pltpu.SMEM), vmem, vmem],
        out_shape=[
            jax.ShapeDtypeStruct((3, 3, 3, 64, 64), F32),
            jax.ShapeDtypeStruct((3, 3, 3, 64, 128), F32),
        ],
        scratch_shapes=[pltpu.VMEM((PAY_ROWS, 128), BF16)],
        compiler_params=pltpu.CompilerParams(vmem_limit_bytes=VMEM_BYTES),
        name="unpack",
    )(odd, mine, other)


def side_bit(step):
    index = lax.axis_index(step[0])
    return sum(index >> bit for bit in step[2]) & 1


def swap(value, steps, which):
    masks = {"gx": 0, "gy": 0}
    for place, (axis, mask, _) in enumerate(steps):
        if (which >> place) & 1:
            masks[axis] ^= mask
    axes = [axis for axis in ("gx", "gy") if masks[axis]]
    if len(axes) == 1:
        axis = axes[0]
        count = lax.axis_size(axis)
        return lax.ppermute(value, axis, [(i, i ^ masks[axis]) for i in range(count)])
    rows, cols = lax.axis_size("gx"), lax.axis_size("gy")
    pairs = [
        (i * cols + j, (i ^ masks["gx"]) * cols + (j ^ masks["gy"]))
        for i in range(rows)
        for j in range(cols)
    ]
    return lax.ppermute(value, ("gx", "gy"), pairs)


def place_of(steps):
    return sum(side_bit(step) << place for place, step in enumerate(steps))


def tree_sum(values):
    values = [value.astype(F32) for value in values]
    while len(values) > 1:
        values = [values[i] + values[i + 1] for i in range(0, len(values), 2)]
    return values[0].astype(BF16)


def scatter_sum(value, steps):
    parts = 1 << len(steps)
    rows = value.shape[0] // parts
    me = place_of(steps)
    found = [lax.dynamic_slice_in_dim(value, me * rows, rows, 0)]
    for k in range(1, parts):
        piece = lax.dynamic_slice_in_dim(value, (me ^ k) * rows, rows, 0)
        found.append(swap(piece, steps, k))
    return tree_sum(found)


def swap_sum(value, step):
    return tree_sum([value, swap(value, (step,), 1)])


def swap_sum_with(value, step, rider):
    rows = value.shape[0]
    got = swap(jnp.concatenate([value, rider]), (step,), 1)
    return tree_sum([value, got[:rows]]), got[rows:]


def gather(value, steps, riders):
    parts = 1 << len(steps)
    rows = value.shape[0]
    me = place_of(steps)
    found, came = [value], []
    for k in range(1, parts):
        rider = riders[k - 1]
        sent = value if rider is None else jnp.concatenate([value, rider])
        got = swap(sent, steps, k)
        found.append(got[:rows])
        came.append(got[rows:])
    for place in range(len(steps)):
        near = ((me >> place) & 1) == 0
        other = 1 << place
        found = [
            jnp.where(near, found[i & ~other], found[i | other])
            if not i & other
            else jnp.where(near, found[i | other], found[i & ~other])
            for i in range(parts)
        ]
    return jnp.concatenate(found), came


def pairs_of(axis, first):
    count = lax.axis_size(axis)
    found = []
    for i in range(first, count, 2):
        found += [(i, (i + 1) % count), ((i + 1) % count, i)]
    return found


def both_sides(first, second, axis):
    even = lax.ppermute(first, axis, pairs_of(axis, 0))
    odd = lax.ppermute(second, axis, pairs_of(axis, 1))
    return even, inside(odd, axis)


def inside(value, axis):
    index = lax.axis_index(axis)
    edge = (index == 0) | (index == lax.axis_size(axis) - 1)
    return jnp.where(edge, jnp.zeros_like(value), value)


def column_ends(odd_x, odd_y, core, chip, head, tail, level_rows):
    lo = jnp.where(odd_x == 1, core, chip)
    hi = jnp.where(odd_x == 1, chip, core)
    left = lax.broadcasted_iota(jnp.int32, (1, 64, 128), 2) < 64
    head = [head[:2], jnp.where(left, lo[0:1], hi[0:1])] + (
        [lo[4:5], head[2:], hi[4:5]] if level_rows else []
    )
    tail = [tail[:2], jnp.where(left, hi[3:4], lo[3:4])] + (
        [lo[7:8], tail[2:], hi[7:8]] if level_rows else []
    )
    head, tail = jnp.concatenate(head), jnp.concatenate(tail)
    return jnp.where(odd_y == 1, head, tail), jnp.where(odd_y == 1, tail, head)


def local(level_input, weight_upper, weight_deep, deep_cotangent):
    tiles = lax.axis_size("gx") * lax.axis_size("gy")
    up_scale = 1.0 / math.sqrt(math.prod(level_input.shape[:3]) * tiles)
    deep_scale = 1.0 / math.sqrt(math.prod(deep_cotangent.shape[:3]) * tiles)
    odd_x = (lax.axis_index("gx") & 1).astype(jnp.int32)
    odd_y = (lax.axis_index("gy") & 1).astype(jnp.int32)
    flag_x, flag_y = odd_x.reshape(1), odd_y.reshape(1)
    part = side_bit(CORE).astype(jnp.int32).reshape(1)

    to_core, to_chip, y_head, y_tail = faces(
        flag_x,
        pltpu.with_memory_space_constraint(level_input, pltpu.HBM),
        pltpu.with_memory_space_constraint(deep_cotangent, pltpu.HBM),
    )
    core, chip = both_sides(to_core, to_chip, "gx")
    to_near, to_far = column_ends(odd_x, odd_y, core, chip, y_head, y_tail, True)
    near, far = both_sides(to_near, to_far, "gy")

    sums, deep, inner = inner_grads(
        flag_x, level_input, deep_cotangent, core, chip, weight_upper, weight_deep
    )
    keep, send, outer, to_core, to_chip, y_head, y_tail = outer_grads(
        flag_x, flag_y, part, level_input, deep_cotangent, core, chip, near, far,
        weight_upper, weight_deep, sums, deep, inner,
    )
    at_x, at_y = lax.axis_index("gx"), lax.axis_index("gy")
    total = tree_sum([keep, swap(send, (CORE,), 1)])
    core = lax.ppermute(to_core, "gx", pairs_of("gx", 0))
    total, core = lax.optimization_barrier((total, core))
    total = scatter_sum(total, (Z_NEAR, X_NEAR))
    total, to_chip = lax.optimization_barrier((total, to_chip))
    first = swap(to_chip, (Y_NEAR,), 1)
    total = swap_sum(total, Y_NEAR)
    total, to_chip = lax.optimization_barrier((total, to_chip))
    second = swap(to_chip, (Y_FAR,), 1)
    total = swap_sum(total, Y_FAR)
    chip = jnp.where((((at_x + 1) >> 1) & 1) == 1, first, second)
    chip = inside(chip, "gx")
    inner_part = inner_input(flag_x, inner, outer, core, chip, weight_upper)
    to_near, to_far = column_ends(odd_x, odd_y, core, chip, y_head, y_tail, False)
    total, direct = swap_sum_with(total, Z_FAR, to_far.reshape(-1, 128))
    near = swap(to_near, (Z_NEAR,), 1)
    total, near = lax.optimization_barrier((total, near))
    total, handed_far = swap_sum_with(total, X_FAR, direct)
    total, inner_part = lax.optimization_barrier((total, inner_part))
    total, (_, handed_near, _) = gather(total, (Z_NEAR, X_NEAR), (None, direct, None))
    plane, depth = at_y >> 2, at_y & 3
    none = jnp.zeros_like(direct)
    handed = jnp.where(
        ((depth == 0) & (plane == 2)) | ((depth == 3) & (plane == 1)), handed_far, handed_near
    )
    ends = (at_y == 0) | (at_y == lax.axis_size("gy") - 1)
    far = jnp.where((depth == 1) | (depth == 2), direct, jnp.where(ends, none, handed))
    input_grad = outer_input(
        flag_x, flag_y, inner, outer, core, chip, near, far.reshape(to_far.shape), weight_upper, inner_part,
    )
    other = swap(total, (CORE,), 1)
    upper, deep = unpack(part, total, other, up_scale, deep_scale)
    return (input_grad, upper, deep)


def solution(mesh):
    placed = (P("gx", "gy", None, None), P(), P(), P("gx", "gy", None, None))
    return jax.shard_map(
        local,
        mesh=mesh,
        in_specs=placed,
        out_specs=(P("gx", "gy", None, None), P(), P()),
        check_vma=False,
    )
```

```python
import functools
import math

import jax
import jax.numpy as jnp
from jax import lax
from jax.experimental import pallas as pl
from jax.experimental.pallas import tpu as pltpu
from jax.sharding import PartitionSpec as P

F32 = jnp.float32
BF16 = jnp.bfloat16
VMEM_BYTES = 28 * 1024 * 1024

PAIR_ROW = 9 * 64
DEEP_ROW = 14 * 64
PAY_ROWS = 41 * 64
HALF_ROWS = PAY_ROWS // 2

CORE = ("gx", 1, (0, 1))
Y_NEAR = ("gx", 3, (1, 2))
Y_FAR = ("gx", 7, (2,))
Z_NEAR = ("gy", 1, (0, 1))
Z_FAR = ("gy", 3, (1,))
X_NEAR = ("gy", 4, (2, 3))
X_FAR = ("gy", 12, (3,))


def depth_taps(row, gap):
    row = row.astype(F32)
    edge = jnp.zeros((1, row.shape[1]), F32)
    below = jnp.concatenate([edge, row[:-1]], axis=0)
    above = jnp.concatenate([row[1:], edge], axis=0)
    pieces = [below, row, above]
    if gap:
        pieces.append(jnp.zeros((row.shape[0], gap), F32))
    return jnp.concatenate(pieces, axis=1).astype(BF16)


INNER = (1, 2)
OUTER = (0, 3)


def window(taps, at_x, at_y, ys):
    return jnp.concatenate(
        [taps[2 * x + at_x, 2 * y + at_y] for x in range(2) for y in ys], axis=0
    )


def deep_window(taps, at_x, at_y, ys):
    return jnp.concatenate([taps[x + at_x, y + at_y] for x in range(2) for y in ys], axis=0)


def faces_kernel(
    odd, own, cot, to_core, to_chip, y_head, y_tail, x_first, x_last, y_first, y_last, deep, sems
):
    copies = [
        pltpu.make_async_copy(source, target, sems.at[k])
        for k, (source, target) in enumerate(
            [
                (own.at[0], x_first),
                (own.at[3], x_last),
                (own.at[:, 0], y_first),
                (own.at[:, 7], y_last),
                (cot, deep),
            ]
        )
    ]
    for copy in copies:
        copy.start()
    for copy in copies:
        copy.wait()
    swapped = odd[0] == 1
    for k in range(4):
        head = jnp.concatenate([x_first[2 * k + 1], x_first[2 * k]], axis=1)
        tail = jnp.concatenate([x_last[2 * k], x_last[2 * k + 1]], axis=1)
        to_core[k] = jnp.where(swapped, head, tail)
        to_chip[k] = jnp.where(swapped, tail, head)
        to_core[4 + k] = jnp.where(swapped, deep[0, k], deep[1, k])
        to_chip[4 + k] = jnp.where(swapped, deep[1, k], deep[0, k])
    for k in range(2):
        y_head[k] = jnp.concatenate([y_first[2 * k], y_first[2 * k + 1]], axis=1)
        y_tail[k] = jnp.concatenate([y_last[2 * k], y_last[2 * k + 1]], axis=1)
        y_head[2 + k] = deep[k, 0]
        y_tail[2 + k] = deep[k, 3]


def faces(odd, own, cot):
    hbm = pl.BlockSpec(memory_space=pltpu.HBM)
    return pl.pallas_call(
        faces_kernel,
        in_specs=[pl.BlockSpec(memory_space=pltpu.SMEM), hbm, hbm],
        out_shape=[pltpu.VMEM((8, 64, 128), BF16)] * 2 + [pltpu.VMEM((4, 64, 128), BF16)] * 2,
        scratch_shapes=[
            pltpu.VMEM((8, 64, 64), BF16),
            pltpu.VMEM((8, 64, 64), BF16),
            pltpu.VMEM((4, 64, 64), BF16),
            pltpu.VMEM((4, 64, 64), BF16),
            pltpu.VMEM((2, 4, 64, 128), BF16),
            pltpu.SemaphoreType.DMA((5,)),
        ],
        name="faces",
    )(odd, own, cot)


def level_column(x, y, own, x_lo, x_hi, y_lo, y_hi):
    if y == 0 or y == 9:
        pairs = y_lo if y == 0 else y_hi
        if 1 <= x <= 4:
            return half(pairs(((x - 1) // 2)), (x - 1) % 2)
        return half(pairs(2), int((x == 5) == (y == 9)))
    if x == 0:
        return half(x_lo((y - 1) // 2), (y - 1) % 2)
    if x == 5:
        return half(x_hi((y - 1) // 2), 1 - (y - 1) % 2)
    return own(x - 1, y - 1)


def half(value, which):
    return value[:, which * 64 : which * 64 + 64]


def build_blocks(w_up, blocks):
    empty = jnp.zeros((192, 64), BF16)
    for x in range(3):
        for y in range(4):
            left = w_up[x, y].reshape(192, 64) if y < 3 else empty
            right = w_up[x, y - 1].reshape(192, 64) if y > 0 else empty
            pair = jnp.concatenate([left, right], axis=1)
            blocks[x, y, 0:192, 0:128] = pair
            blocks[x + 1, y, 0:192, 128:256] = pair
    for y in range(4):
        blocks[3, y, 0:192, 0:128] = jnp.zeros((192, 128), BF16)
        blocks[0, y, 0:192, 128:256] = jnp.zeros((192, 128), BF16)
        for x in range(4):
            blocks[x, y, 192:256, :] = jnp.zeros((64, 256), BF16)


def column_grads(ys, taps, cot_taps, blocks, w_deep, sums, deep):
    rows = 2 * len(ys) * 64
    pre = jnp.zeros((rows, 256), F32)
    for x in range(4):
        for y in range(4):
            pre = pre + jnp.dot(
                window(taps, x, y, ys), blocks[x, y], preferred_element_type=F32
            )
    sig = 1.0 / (1.0 + jnp.exp(-pre))
    act = pre * sig
    summed = act[:, :128] + act[:, 128:]
    pooled = 0.25 * (summed[:, :64] + summed[:, 64:])
    pooled_t = pooled.T.astype(BF16)

    pooled_grad = jnp.zeros((rows, 64), F32)
    for a in range(3):
        for b in range(3):
            weight = jnp.concatenate([w_deep[2 - a, 2 - b, 2 - j] for j in range(3)], axis=1)
            pooled_grad = pooled_grad + lax.dot_general(
                deep_window(cot_taps, a, b, ys), weight, (((1,), (1,)), ((), ())),
                preferred_element_type=F32,
            )
    wide = pooled_grad.astype(BF16).astype(F32)
    wide = jnp.concatenate([wide, wide], axis=1)
    wide = jnp.concatenate([wide, wide], axis=1)
    grad = 0.25 * wide * (sig * (1.0 + pre * (1.0 - sig)))
    grad_t = grad.T.astype(BF16)

    for a in range(3):
        for b in range(3):
            out = jnp.dot(
                pooled_t, deep_window(cot_taps, 2 - a, 2 - b, ys), preferred_element_type=F32
            )
            for j in range(3):
                deep((a * 3 + b) * 3 + 2 - j, out[:, j * 128 : j * 128 + 128])
    for x in range(4):
        for y in range(4):
            kept = [
                (s, t)
                for s in range(2)
                for t in range(2)
                if 0 <= x - s < 3 and 0 <= y - t < 3
            ]
            left = jnp.concatenate(
                [grad_t[(s * 2 + t) * 64 : (s * 2 + t) * 64 + 64] for s, t in kept], axis=0
            )
            part = jnp.dot(left, window(taps, x, y, ys), preferred_element_type=F32)
            for k, (s, t) in enumerate(kept):
                sums((x - s) * 3 + y - t, part[k * 64 : k * 64 + 64], s == 0 and t == 0)
    return grad.astype(BF16)


def inner_kernel(odd_x, own, cot, core, chip, w_up, w_deep, sums, deep, inner, taps, cot_taps, blocks):
    swap_x = odd_x[0] == 1

    def x_lo(k):
        return jnp.where(swap_x, core[k], chip[k])

    def x_hi(k):
        return jnp.where(swap_x, chip[k], core[k])

    for x in range(6):
        for y in range(2, 8):
            row = level_column(x, y, lambda u, v: own[u, v], x_lo, x_hi, None, None)
            taps[x, y] = depth_taps(row, 64)
    for x in range(4):
        for y in range(1, 5):
            if x == 0:
                row = x_lo(3 + y)
            elif x == 3:
                row = x_hi(3 + y)
            else:
                row = cot[x - 1, y - 1]
            cot_taps[x, y] = depth_taps(row, 0)
    build_blocks(w_up, blocks)

    def add_sum(k, piece, first):
        sums[k] = piece if first else sums[k] + piece

    def add_deep(k, piece):
        deep[k] = piece

    inner[...] = column_grads(INNER, taps, cot_taps, blocks, w_deep, add_sum, add_deep)


def inner_grads(odd_x, own, cot, core, chip, w_up, w_deep):
    smem = pl.BlockSpec(memory_space=pltpu.SMEM)
    vmem = pl.BlockSpec(memory_space=pltpu.VMEM)
    return pl.pallas_call(
        inner_kernel,
        in_specs=[smem] + [vmem] * 6,
        out_shape=[
            jax.ShapeDtypeStruct((9, 64, 256), F32),
            jax.ShapeDtypeStruct((27, 64, 128), F32),
            jax.ShapeDtypeStruct((256, 256), BF16),
        ],
        scratch_shapes=[
            pltpu.VMEM((6, 10, 64, 256), BF16),
            pltpu.VMEM((4, 6, 64, 384), BF16),
            pltpu.VMEM((4, 4, 256, 256), BF16),
        ],
        compiler_params=pltpu.CompilerParams(vmem_limit_bytes=VMEM_BYTES),
        cost_estimate=pl.CostEstimate(
            flops=2_000_000_000, bytes_accessed=4_000_000, transcendentals=65536
        ),
        name="inner_grads",
    )(odd_x, own, cot, core, chip, w_up, w_deep)


def outer_kernel(
    odd_x, odd_y, part, own, cot, core, chip, near, far, w_up, w_deep, sums_in, deep_in, inner,
    keep, send, outer, to_core, to_chip, gy_head, gy_tail,
    taps, cot_taps, blocks, sums, payload,
):
    swap_x = odd_x[0] == 1
    swap_y = odd_y[0] == 1

    def x_lo(k):
        return jnp.where(swap_x, core[k], chip[k])

    def x_hi(k):
        return jnp.where(swap_x, chip[k], core[k])

    def y_lo(k):
        return jnp.where(swap_y, near[k], far[k])

    def y_hi(k):
        return jnp.where(swap_y, far[k], near[k])

    for x in range(6):
        for y in (0, 1, 2, 3, 6, 7, 8, 9):
            row = level_column(x, y, lambda u, v: own[u, v], x_lo, x_hi, y_lo, y_hi)
            taps[x, y] = depth_taps(row, 64)
    for x in range(4):
        for y in range(6):
            if y == 0:
                row = y_lo(3 + x)
            elif y == 5:
                row = y_hi(3 + x)
            elif x == 0:
                row = x_lo(3 + y)
            elif x == 3:
                row = x_hi(3 + y)
            else:
                row = cot[x - 1, y - 1]
            cot_taps[x, y] = depth_taps(row, 0)
    build_blocks(w_up, blocks)

    def add_sum(k, piece, first):
        sums[k] = (sums_in[k] if first else sums[k]) + piece

    def add_deep(k, piece):
        top = DEEP_ROW + k * 64
        payload[top : top + 64, :] = (deep_in[k] + piece).astype(BF16)

    rounded = column_grads(OUTER, taps, cot_taps, blocks, w_deep, add_sum, add_deep)
    outer[...] = rounded

    def block(x, y):
        top = (x * 2 + (y in (2, 3))) * 64
        return (inner if y in INNER else rounded)[top : top + 64]

    for k in range(4):
        head = block(0, k)[:, 0:128]
        head = jnp.concatenate([half(head, 1), half(head, 0)], axis=1)
        tail = block(1, k)[:, 128:256]
        to_core[k] = jnp.where(swap_x, head, tail)
        to_chip[k] = jnp.where(swap_x, tail, head)
    for k in range(2):
        first, last = block(k, 0), block(k, 3)
        gy_head[k] = jnp.concatenate([first[:, 0:64], first[:, 128:192]], axis=1)
        gy_tail[k] = jnp.concatenate([last[:, 64:128], last[:, 192:256]], axis=1)

    for k in range(9):
        payload[k * 64 : k * 64 + 64, :] = sums[k, :, 0:128].astype(BF16)
    for k in range(5):
        left = sums[2 * k, :, 128:192]
        right = sums[2 * k + 1, :, 128:192] if k < 4 else jnp.zeros((64, 64), F32)
        top = PAIR_ROW + k * 64
        payload[top : top + 64, :] = jnp.concatenate([left, right], axis=1).astype(BF16)
    mine = pl.multiple_of(part[0] * HALF_ROWS, HALF_ROWS)
    keep[...] = payload[pl.ds(mine, HALF_ROWS), :]
    send[...] = payload[pl.ds(HALF_ROWS - mine, HALF_ROWS), :]


def outer_grads(odd_x, odd_y, part, own, cot, core, chip, near, far, w_up, w_deep, sums, deep, inner):
    smem = pl.BlockSpec(memory_space=pltpu.SMEM)
    vmem = pl.BlockSpec(memory_space=pltpu.VMEM)
    return pl.pallas_call(
        outer_kernel,
        in_specs=[smem] * 3 + [vmem] * 11,
        out_shape=[
            jax.ShapeDtypeStruct((HALF_ROWS, 128), BF16),
            jax.ShapeDtypeStruct((HALF_ROWS, 128), BF16),
            jax.ShapeDtypeStruct((256, 256), BF16),
            jax.ShapeDtypeStruct((4, 64, 128), BF16),
            jax.ShapeDtypeStruct((4, 64, 128), BF16),
            jax.ShapeDtypeStruct((2, 64, 128), BF16),
            jax.ShapeDtypeStruct((2, 64, 128), BF16),
        ],
        scratch_shapes=[
            pltpu.VMEM((6, 10, 64, 256), BF16),
            pltpu.VMEM((4, 6, 64, 384), BF16),
            pltpu.VMEM((4, 4, 256, 256), BF16),
            pltpu.VMEM((9, 64, 256), F32),
            pltpu.VMEM((PAY_ROWS, 128), BF16),
        ],
        compiler_params=pltpu.CompilerParams(vmem_limit_bytes=VMEM_BYTES),
        cost_estimate=pl.CostEstimate(
            flops=2_000_000_000, bytes_accessed=4_000_000, transcendentals=65536
        ),
        name="outer_grads",
    )(odd_x, odd_y, part, own, cot, core, chip, near, far, w_up, w_deep, sums, deep, inner)


def input_columns(ys, at_ys, taps, w_up):
    empty = jnp.zeros((64, 256), BF16)
    spare = jnp.zeros((64, 64), BF16)
    weights = {}
    for a in range(3):
        for b in range(3):
            weights[a, b] = jnp.concatenate(
                [w_up[a, b, 2], w_up[a, b, 1], w_up[a, b, 0], spare], axis=1
            )
    total = jnp.zeros((2 * len(ys) * 64, 256), F32)
    for x in range(4):
        for y in at_ys:
            block = jnp.concatenate(
                [weights.get((s + 2 - x, t + 2 - y), empty) for s in range(2) for t in range(2)],
                axis=0,
            )
            total = total + lax.dot_general(
                window(taps, x, y, ys), block, (((1,), (1,)), ((), ())),
                preferred_element_type=F32,
            )
    return total


def picked(inner, outer, x, y):
    at = (x % 2) * 128 + (y % 2) * 64
    top = ((x // 2) * 2 + (y // 2 in (2, 3))) * 64
    return (inner if y // 2 in INNER else outer)[top : top + 64, at : at + 64]


def inner_input_kernel(odd_x, inner, outer, core, chip, w_up, out, taps):
    swap_x = odd_x[0] == 1

    def x_lo(k):
        return jnp.where(swap_x, core[k], chip[k])

    def x_hi(k):
        return jnp.where(swap_x, chip[k], core[k])

    def own(u, v):
        return picked(inner, outer, u, v)

    for x in range(6):
        taps[x, 0] = jnp.zeros((64, 256), BF16)
        taps[x, 9] = jnp.zeros((64, 256), BF16)
        for y in range(1, 9):
            taps[x, y] = depth_taps(level_column(x, y, own, x_lo, x_hi, None, None), 64)
    out[...] = input_columns(range(4), range(4), taps, w_up)


def inner_input(odd_x, inner, outer, core, chip, w_up):
    smem = pl.BlockSpec(memory_space=pltpu.SMEM)
    vmem = pl.BlockSpec(memory_space=pltpu.VMEM)
    return pl.pallas_call(
        inner_input_kernel,
        in_specs=[smem] + [vmem] * 5,
        out_shape=jax.ShapeDtypeStruct((512, 256), F32),
        scratch_shapes=[pltpu.VMEM((6, 10, 64, 256), BF16)],
        compiler_params=pltpu.CompilerParams(vmem_limit_bytes=VMEM_BYTES),
        cost_estimate=pl.CostEstimate(
            flops=500_000_000, bytes_accessed=2_000_000, transcendentals=0
        ),
        name="inner_input",
    )(odd_x, inner, outer, core, chip, w_up)


def outer_input_kernel(odd_y, near, far, w_up, part, out, taps):
    swap_y = odd_y[0] == 1

    def y_lo(k):
        return jnp.where(swap_y, near[k], far[k])

    def y_hi(k):
        return jnp.where(swap_y, far[k], near[k])

    for x in range(6):
        for y in (0, 9):
            taps[x, y] = depth_taps(level_column(x, y, None, None, None, y_lo, y_hi), 64)
    ends = {
        0: input_columns((0,), (0,), taps, w_up),
        3: input_columns((3,), (3,), taps, w_up),
    }
    for x in range(2):
        for y in range(4):
            top = (x * 4 + y) * 64
            rows = part[top : top + 64]
            if y in OUTER:
                rows = rows + ends[y][x * 64 : x * 64 + 64]
            rows = rows.astype(BF16)
            for s in range(2):
                for t in range(2):
                    at = s * 128 + t * 64
                    out[2 * x + s, 2 * y + t] = rows[:, at : at + 64]


def outer_input(odd_y, near, far, w_up, part):
    vmem = pl.BlockSpec(memory_space=pltpu.VMEM)
    return pl.pallas_call(
        outer_input_kernel,
        in_specs=[pl.BlockSpec(memory_space=pltpu.SMEM)] + [vmem] * 4,
        out_shape=jax.ShapeDtypeStruct((4, 8, 64, 64), BF16),
        scratch_shapes=[pltpu.VMEM((6, 10, 64, 256), BF16)],
        compiler_params=pltpu.CompilerParams(vmem_limit_bytes=VMEM_BYTES),
        cost_estimate=pl.CostEstimate(
            flops=300_000_000, bytes_accessed=4_000_000, transcendentals=0
        ),
        name="outer_input",
    )(odd_y, near, far, w_up, part)


def unpack_kernel(
    up_scale, deep_scale, odd, mine, other, up_out, deep_out, payload, up, deep, sems
):
    first = pl.multiple_of(odd[0] * HALF_ROWS, HALF_ROWS)
    payload[pl.ds(first, HALF_ROWS), :] = mine[...]
    payload[pl.ds(HALF_ROWS - first, HALF_ROWS), :] = other[...]
    copies = []
    pairs = {}
    for a in range(3):
        for k in range(a * 9, a * 9 + 9):
            top = DEEP_ROW + k * 64
            deep[a, k // 3 % 3, k % 3] = payload[top : top + 64, :].astype(F32) * deep_scale
        copies.append(pltpu.make_async_copy(deep.at[a], deep_out.at[a], sems.at[a]))
        copies[-1].start()
    for a in range(3):
        for b in range(3):
            k = a * 3 + b
            pair = payload[k * 64 : k * 64 + 64, :].astype(F32).T * up_scale
            up[a, b, 0] = pair[:64]
            up[a, b, 1] = pair[64:]
            if k % 2 == 0:
                top = PAIR_ROW + k // 2 * 64
                pairs[k // 2] = payload[top : top + 64, :].astype(F32).T * up_scale
            up[a, b, 2] = pairs[k // 2][k % 2 * 64 : k % 2 * 64 + 64]
        copies.append(pltpu.make_async_copy(up.at[a], up_out.at[a], sems.at[3 + a]))
        copies[-1].start()
    for copy in copies:
        copy.wait()


def unpack(odd, mine, other, up_scale, deep_scale):
    vmem = pl.BlockSpec(memory_space=pltpu.VMEM)
    hbm = pl.BlockSpec(memory_space=pltpu.HBM)
    return pl.pallas_call(
        functools.partial(unpack_kernel, up_scale, deep_scale),
        in_specs=[pl.BlockSpec(memory_space=pltpu.SMEM), vmem, vmem],
        out_specs=[hbm, hbm],
        out_shape=[
            jax.ShapeDtypeStruct((3, 3, 3, 64, 64), F32),
            jax.ShapeDtypeStruct((3, 3, 3, 64, 128), F32),
        ],
        scratch_shapes=[
            pltpu.VMEM((PAY_ROWS, 128), BF16),
            pltpu.VMEM((3, 3, 3, 64, 64), F32),
            pltpu.VMEM((3, 3, 3, 64, 128), F32),
            pltpu.SemaphoreType.DMA((6,)),
        ],
        compiler_params=pltpu.CompilerParams(vmem_limit_bytes=VMEM_BYTES),
        name="unpack",
    )(odd, mine, other)


def side_bit(step):
    index = lax.axis_index(step[0])
    return sum(index >> bit for bit in step[2]) & 1


def swap(value, steps, which):
    masks = {"gx": 0, "gy": 0}
    for place, (axis, mask, _) in enumerate(steps):
        if (which >> place) & 1:
            masks[axis] ^= mask
    axes = [axis for axis in ("gx", "gy") if masks[axis]]
    if len(axes) == 1:
        axis = axes[0]
        count = lax.axis_size(axis)
        return lax.ppermute(value, axis, [(i, i ^ masks[axis]) for i in range(count)])
    rows, cols = lax.axis_size("gx"), lax.axis_size("gy")
    pairs = [
        (i * cols + j, (i ^ masks["gx"]) * cols + (j ^ masks["gy"]))
        for i in range(rows)
        for j in range(cols)
    ]
    return lax.ppermute(value, ("gx", "gy"), pairs)


def place_of(steps):
    return sum(side_bit(step) << place for place, step in enumerate(steps))


def tree_sum(values):
    values = [value.astype(F32) for value in values]
    while len(values) > 1:
        values = [values[i] + values[i + 1] for i in range(0, len(values), 2)]
    return values[0].astype(BF16)


def scatter_sum(value, steps):
    parts = 1 << len(steps)
    rows = value.shape[0] // parts
    me = place_of(steps)
    found = [lax.dynamic_slice_in_dim(value, me * rows, rows, 0)]
    for k in range(1, parts):
        piece = lax.dynamic_slice_in_dim(value, (me ^ k) * rows, rows, 0)
        found.append(swap(piece, steps, k))
    return tree_sum(found)


def swap_sum(value, step):
    return tree_sum([value, swap(value, (step,), 1)])


def swap_sum_with(value, step, rider):
    rows = value.shape[0]
    got = swap(jnp.concatenate([value, rider]), (step,), 1)
    return tree_sum([value, got[:rows]]), got[rows:]


def gather(value, steps, riders):
    parts = 1 << len(steps)
    rows = value.shape[0]
    me = place_of(steps)
    found, came = [value], []
    for k in range(1, parts):
        rider = riders[k - 1]
        sent = value if rider is None else jnp.concatenate([value, rider])
        got = swap(sent, steps, k)
        found.append(got[:rows])
        came.append(got[rows:])
    for place in range(len(steps)):
        near = ((me >> place) & 1) == 0
        other = 1 << place
        found = [
            jnp.where(near, found[i & ~other], found[i | other])
            if not i & other
            else jnp.where(near, found[i | other], found[i & ~other])
            for i in range(parts)
        ]
    return jnp.concatenate(found), came


def pairs_of(axis, first):
    count = lax.axis_size(axis)
    found = []
    for i in range(first, count, 2):
        found += [(i, (i + 1) % count), ((i + 1) % count, i)]
    return found


def both_sides(first, second, axis):
    even = lax.ppermute(first, axis, pairs_of(axis, 0))
    odd = lax.ppermute(second, axis, pairs_of(axis, 1))
    return even, inside(odd, axis)


def inside(value, axis):
    index = lax.axis_index(axis)
    edge = (index == 0) | (index == lax.axis_size(axis) - 1)
    return jnp.where(edge, jnp.zeros_like(value), value)


def column_ends(odd_x, odd_y, core, chip, head, tail, level_rows):
    lo = jnp.where(odd_x == 1, core, chip)
    hi = jnp.where(odd_x == 1, chip, core)
    left = lax.broadcasted_iota(jnp.int32, (1, 64, 128), 2) < 64
    head = [head[:2], jnp.where(left, lo[0:1], hi[0:1])] + (
        [lo[4:5], head[2:], hi[4:5]] if level_rows else []
    )
    tail = [tail[:2], jnp.where(left, hi[3:4], lo[3:4])] + (
        [lo[7:8], tail[2:], hi[7:8]] if level_rows else []
    )
    head, tail = jnp.concatenate(head), jnp.concatenate(tail)
    return jnp.where(odd_y == 1, head, tail), jnp.where(odd_y == 1, tail, head)


def local(level_input, weight_upper, weight_deep, deep_cotangent):
    tiles = lax.axis_size("gx") * lax.axis_size("gy")
    up_scale = 1.0 / math.sqrt(math.prod(level_input.shape[:3]) * tiles)
    deep_scale = 1.0 / math.sqrt(math.prod(deep_cotangent.shape[:3]) * tiles)
    odd_x = (lax.axis_index("gx") & 1).astype(jnp.int32)
    odd_y = (lax.axis_index("gy") & 1).astype(jnp.int32)
    flag_x, flag_y = odd_x.reshape(1), odd_y.reshape(1)
    part = side_bit(CORE).astype(jnp.int32).reshape(1)

    to_core, to_chip, y_head, y_tail = faces(
        flag_x,
        pltpu.with_memory_space_constraint(level_input, pltpu.HBM),
        pltpu.with_memory_space_constraint(deep_cotangent, pltpu.HBM),
    )
    core, chip = both_sides(to_core, to_chip, "gx")
    to_near, to_far = column_ends(odd_x, odd_y, core, chip, y_head, y_tail, True)
    near, far = both_sides(to_near, to_far, "gy")

    sums, deep, inner = inner_grads(
        flag_x, level_input, deep_cotangent, core, chip, weight_upper, weight_deep
    )
    keep, send, outer, to_core, to_chip, y_head, y_tail = outer_grads(
        flag_x, flag_y, part, level_input, deep_cotangent, core, chip, near, far,
        weight_upper, weight_deep, sums, deep, inner,
    )
    at_x, at_y = lax.axis_index("gx"), lax.axis_index("gy")
    total = tree_sum([keep, swap(send, (CORE,), 1)])
    core = lax.ppermute(to_core, "gx", pairs_of("gx", 0))
    total, core = lax.optimization_barrier((total, core))
    total = scatter_sum(total, (Z_NEAR, X_NEAR))
    total, to_chip = lax.optimization_barrier((total, to_chip))
    first = swap(to_chip, (Y_NEAR,), 1)
    total = swap_sum(total, Y_NEAR)
    total, to_chip = lax.optimization_barrier((total, to_chip))
    second = swap(to_chip, (Y_FAR,), 1)
    total = swap_sum(total, Y_FAR)
    chip = jnp.where((((at_x + 1) >> 1) & 1) == 1, first, second)
    chip = inside(chip, "gx")
    inner_part = inner_input(flag_x, inner, outer, core, chip, weight_upper)
    to_near, to_far = column_ends(odd_x, odd_y, core, chip, y_head, y_tail, False)
    total, direct = swap_sum_with(total, Z_FAR, to_far.reshape(-1, 128))
    near = swap(to_near, (Z_NEAR,), 1)
    total, near = lax.optimization_barrier((total, near))
    total, handed_far = swap_sum_with(total, X_FAR, direct)
    total, inner_part = lax.optimization_barrier((total, inner_part))
    total, (_, handed_near, _) = gather(total, (Z_NEAR, X_NEAR), (None, direct, None))
    plane, depth = at_y >> 2, at_y & 3
    none = jnp.zeros_like(direct)
    handed = jnp.where(
        ((depth == 0) & (plane == 2)) | ((depth == 3) & (plane == 1)), handed_far, handed_near
    )
    ends = (at_y == 0) | (at_y == lax.axis_size("gy") - 1)
    far = jnp.where((depth == 1) | (depth == 2), direct, jnp.where(ends, none, handed))
    input_grad = outer_input(
        flag_y, near, far.reshape(to_far.shape), weight_upper, inner_part
    )
    other = swap(total, (CORE,), 1)
    upper, deep = unpack(part, total, other, up_scale, deep_scale)
    return (input_grad, upper, deep)


def solution(mesh):
    placed = (P("gx", "gy", None, None), P(), P(), P("gx", "gy", None, None))
    return jax.shard_map(
        local,
        mesh=mesh,
        in_specs=placed,
        out_specs=(P("gx", "gy", None, None), P(), P()),
        check_vma=False,
    )
```

```python
import functools
import math

import jax
import jax.numpy as jnp
from jax import lax
from jax.experimental import pallas as pl
from jax.experimental.pallas import tpu as pltpu
from jax.sharding import PartitionSpec as P

F32 = jnp.float32
BF16 = jnp.bfloat16
VMEM_BYTES = 28 * 1024 * 1024

PAIR_ROW = 9 * 64
DEEP_ROW = 14 * 64
PAY_ROWS = 41 * 64
HALF_ROWS = PAY_ROWS // 2

CORE = ("gx", 1, (0, 1))
Y_NEAR = ("gx", 3, (1, 2))
Y_FAR = ("gx", 7, (2,))
Z_NEAR = ("gy", 1, (0, 1))
Z_FAR = ("gy", 3, (1,))
X_NEAR = ("gy", 4, (2, 3))
X_FAR = ("gy", 12, (3,))


def depth_taps(row, gap):
    row = row.astype(F32)
    edge = jnp.zeros((1, row.shape[1]), F32)
    below = jnp.concatenate([edge, row[:-1]], axis=0)
    above = jnp.concatenate([row[1:], edge], axis=0)
    pieces = [below, row, above]
    if gap:
        pieces.append(jnp.zeros((row.shape[0], gap), F32))
    return jnp.concatenate(pieces, axis=1).astype(BF16)


INNER = (1, 2)
OUTER = (0, 3)


def window(taps, at_x, at_y, ys):
    return jnp.concatenate(
        [taps[2 * x + at_x, 2 * y + at_y] for x in range(2) for y in ys], axis=0
    )


def deep_window(taps, at_x, at_y, ys):
    return jnp.concatenate([taps[x + at_x, y + at_y] for x in range(2) for y in ys], axis=0)


def faces_kernel(
    odd, own, cot, to_core, to_chip, y_head, y_tail, x_first, x_last, y_first, y_last, deep, sems
):
    copies = [
        pltpu.make_async_copy(source, target, sems.at[k])
        for k, (source, target) in enumerate(
            [
                (own.at[0], x_first),
                (own.at[3], x_last),
                (own.at[:, 0], y_first),
                (own.at[:, 7], y_last),
                (cot, deep),
            ]
        )
    ]
    for copy in copies:
        copy.start()
    for copy in copies:
        copy.wait()
    swapped = odd[0] == 1
    for k in range(4):
        head = jnp.concatenate([x_first[2 * k + 1], x_first[2 * k]], axis=1)
        tail = jnp.concatenate([x_last[2 * k], x_last[2 * k + 1]], axis=1)
        to_core[k] = jnp.where(swapped, head, tail)
        to_chip[k] = jnp.where(swapped, tail, head)
        to_core[4 + k] = jnp.where(swapped, deep[0, k], deep[1, k])
        to_chip[4 + k] = jnp.where(swapped, deep[1, k], deep[0, k])
    for k in range(2):
        y_head[k] = jnp.concatenate([y_first[2 * k], y_first[2 * k + 1]], axis=1)
        y_tail[k] = jnp.concatenate([y_last[2 * k], y_last[2 * k + 1]], axis=1)
        y_head[2 + k] = deep[k, 0]
        y_tail[2 + k] = deep[k, 3]


def faces(odd, own, cot):
    hbm = pl.BlockSpec(memory_space=pltpu.HBM)
    return pl.pallas_call(
        faces_kernel,
        in_specs=[pl.BlockSpec(memory_space=pltpu.SMEM), hbm, hbm],
        out_shape=[pltpu.VMEM((8, 64, 128), BF16)] * 2 + [pltpu.VMEM((4, 64, 128), BF16)] * 2,
        scratch_shapes=[
            pltpu.VMEM((8, 64, 64), BF16),
            pltpu.VMEM((8, 64, 64), BF16),
            pltpu.VMEM((4, 64, 64), BF16),
            pltpu.VMEM((4, 64, 64), BF16),
            pltpu.VMEM((2, 4, 64, 128), BF16),
            pltpu.SemaphoreType.DMA((5,)),
        ],
        name="faces",
    )(odd, own, cot)


def level_column(x, y, own, x_lo, x_hi, y_lo, y_hi):
    if y == 0 or y == 9:
        pairs = y_lo if y == 0 else y_hi
        if 1 <= x <= 4:
            return half(pairs(((x - 1) // 2)), (x - 1) % 2)
        return half(pairs(2), int((x == 5) == (y == 9)))
    if x == 0:
        return half(x_lo((y - 1) // 2), (y - 1) % 2)
    if x == 5:
        return half(x_hi((y - 1) // 2), 1 - (y - 1) % 2)
    return own(x - 1, y - 1)


def half(value, which):
    return value[:, which * 64 : which * 64 + 64]


def build_blocks(w_up, blocks):
    empty = jnp.zeros((192, 64), BF16)
    for x in range(3):
        for y in range(4):
            left = w_up[x, y].reshape(192, 64) if y < 3 else empty
            right = w_up[x, y - 1].reshape(192, 64) if y > 0 else empty
            pair = jnp.concatenate([left, right], axis=1)
            blocks[x, y, 0:192, 0:128] = pair
            blocks[x + 1, y, 0:192, 128:256] = pair
    for y in range(4):
        blocks[3, y, 0:192, 0:128] = jnp.zeros((192, 128), BF16)
        blocks[0, y, 0:192, 128:256] = jnp.zeros((192, 128), BF16)
        for x in range(4):
            blocks[x, y, 192:256, :] = jnp.zeros((64, 256), BF16)


def column_grads(ys, taps, cot_taps, blocks, w_deep, sums, deep):
    rows = 2 * len(ys) * 64
    pre = jnp.zeros((rows, 256), F32)
    for x in range(4):
        for y in range(4):
            pre = pre + jnp.dot(
                window(taps, x, y, ys), blocks[x, y], preferred_element_type=F32
            )
    sig = 1.0 / (1.0 + jnp.exp(-pre))
    act = pre * sig
    summed = act[:, :128] + act[:, 128:]
    pooled = 0.25 * (summed[:, :64] + summed[:, 64:])
    pooled_t = pooled.T.astype(BF16)

    pooled_grad = jnp.zeros((rows, 64), F32)
    for a in range(3):
        for b in range(3):
            weight = jnp.concatenate([w_deep[2 - a, 2 - b, 2 - j] for j in range(3)], axis=1)
            pooled_grad = pooled_grad + lax.dot_general(
                deep_window(cot_taps, a, b, ys), weight, (((1,), (1,)), ((), ())),
                preferred_element_type=F32,
            )
    wide = pooled_grad.astype(BF16).astype(F32)
    wide = jnp.concatenate([wide, wide], axis=1)
    wide = jnp.concatenate([wide, wide], axis=1)
    grad = 0.25 * wide * (sig * (1.0 + pre * (1.0 - sig)))
    grad_t = grad.T.astype(BF16)

    for a in range(3):
        for b in range(3):
            out = jnp.dot(
                pooled_t, deep_window(cot_taps, 2 - a, 2 - b, ys), preferred_element_type=F32
            )
            for j in range(3):
                deep((a * 3 + b) * 3 + 2 - j, out[:, j * 128 : j * 128 + 128])
    for x in range(4):
        for y in range(4):
            kept = [
                (s, t)
                for s in range(2)
                for t in range(2)
                if 0 <= x - s < 3 and 0 <= y - t < 3
            ]
            left = jnp.concatenate(
                [grad_t[(s * 2 + t) * 64 : (s * 2 + t) * 64 + 64] for s, t in kept], axis=0
            )
            part = jnp.dot(left, window(taps, x, y, ys), preferred_element_type=F32)
            for k, (s, t) in enumerate(kept):
                sums((x - s) * 3 + y - t, part[k * 64 : k * 64 + 64], s == 0 and t == 0)
    return grad.astype(BF16)


def inner_kernel(odd_x, own, cot, core, chip, w_up, w_deep, sums, deep, inner, taps, cot_taps, blocks):
    swap_x = odd_x[0] == 1

    def x_lo(k):
        return jnp.where(swap_x, core[k], chip[k])

    def x_hi(k):
        return jnp.where(swap_x, chip[k], core[k])

    for x in range(6):
        for y in range(2, 8):
            row = level_column(x, y, lambda u, v: own[u, v], x_lo, x_hi, None, None)
            taps[x, y] = depth_taps(row, 64)
    for x in range(4):
        for y in range(1, 5):
            if x == 0:
                row = x_lo(3 + y)
            elif x == 3:
                row = x_hi(3 + y)
            else:
                row = cot[x - 1, y - 1]
            cot_taps[x, y] = depth_taps(row, 0)
    build_blocks(w_up, blocks)

    def add_sum(k, piece, first):
        sums[k] = piece if first else sums[k] + piece

    def add_deep(k, piece):
        deep[k] = piece

    inner[...] = column_grads(INNER, taps, cot_taps, blocks, w_deep, add_sum, add_deep)


def inner_grads(odd_x, own, cot, core, chip, w_up, w_deep):
    smem = pl.BlockSpec(memory_space=pltpu.SMEM)
    vmem = pl.BlockSpec(memory_space=pltpu.VMEM)
    return pl.pallas_call(
        inner_kernel,
        in_specs=[smem] + [vmem] * 6,
        out_shape=[
            jax.ShapeDtypeStruct((9, 64, 256), F32),
            jax.ShapeDtypeStruct((27, 64, 128), F32),
            jax.ShapeDtypeStruct((256, 256), BF16),
        ],
        scratch_shapes=[
            pltpu.VMEM((6, 10, 64, 256), BF16),
            pltpu.VMEM((4, 6, 64, 384), BF16),
            pltpu.VMEM((4, 4, 256, 256), BF16),
        ],
        compiler_params=pltpu.CompilerParams(vmem_limit_bytes=VMEM_BYTES),
        cost_estimate=pl.CostEstimate(
            flops=2_000_000_000, bytes_accessed=4_000_000, transcendentals=65536
        ),
        name="inner_grads",
    )(odd_x, own, cot, core, chip, w_up, w_deep)


def outer_kernel(
    odd_x, odd_y, part, own, cot, core, chip, near, far, w_up, w_deep, sums_in, deep_in, inner,
    keep, send, outer, to_core, to_chip, gy_head, gy_tail,
    taps, cot_taps, blocks, sums, payload,
):
    swap_x = odd_x[0] == 1
    swap_y = odd_y[0] == 1

    def x_lo(k):
        return jnp.where(swap_x, core[k], chip[k])

    def x_hi(k):
        return jnp.where(swap_x, chip[k], core[k])

    def y_lo(k):
        return jnp.where(swap_y, near[k], far[k])

    def y_hi(k):
        return jnp.where(swap_y, far[k], near[k])

    for x in range(6):
        for y in (0, 1, 2, 3, 6, 7, 8, 9):
            row = level_column(x, y, lambda u, v: own[u, v], x_lo, x_hi, y_lo, y_hi)
            taps[x, y] = depth_taps(row, 64)
    for x in range(4):
        for y in range(6):
            if y == 0:
                row = y_lo(3 + x)
            elif y == 5:
                row = y_hi(3 + x)
            elif x == 0:
                row = x_lo(3 + y)
            elif x == 3:
                row = x_hi(3 + y)
            else:
                row = cot[x - 1, y - 1]
            cot_taps[x, y] = depth_taps(row, 0)
    build_blocks(w_up, blocks)

    def add_sum(k, piece, first):
        sums[k] = (sums_in[k] if first else sums[k]) + piece

    def add_deep(k, piece):
        top = DEEP_ROW + k * 64
        payload[top : top + 64, :] = (deep_in[k] + piece).astype(BF16)

    rounded = column_grads(OUTER, taps, cot_taps, blocks, w_deep, add_sum, add_deep)
    outer[...] = rounded

    def block(x, y):
        top = (x * 2 + (y in (2, 3))) * 64
        return (inner if y in INNER else rounded)[top : top + 64]

    for k in range(4):
        head = block(0, k)[:, 0:128]
        head = jnp.concatenate([half(head, 1), half(head, 0)], axis=1)
        tail = block(1, k)[:, 128:256]
        to_core[k] = jnp.where(swap_x, head, tail)
        to_chip[k] = jnp.where(swap_x, tail, head)
    for k in range(2):
        first, last = block(k, 0), block(k, 3)
        gy_head[k] = jnp.concatenate([first[:, 0:64], first[:, 128:192]], axis=1)
        gy_tail[k] = jnp.concatenate([last[:, 64:128], last[:, 192:256]], axis=1)

    for k in range(9):
        payload[k * 64 : k * 64 + 64, :] = sums[k, :, 0:128].astype(BF16)
    for k in range(5):
        left = sums[2 * k, :, 128:192]
        right = sums[2 * k + 1, :, 128:192] if k < 4 else jnp.zeros((64, 64), F32)
        top = PAIR_ROW + k * 64
        payload[top : top + 64, :] = jnp.concatenate([left, right], axis=1).astype(BF16)
    mine = pl.multiple_of(part[0] * HALF_ROWS, HALF_ROWS)
    keep[...] = payload[pl.ds(mine, HALF_ROWS), :]
    send[...] = payload[pl.ds(HALF_ROWS - mine, HALF_ROWS), :]


def outer_grads(odd_x, odd_y, part, own, cot, core, chip, near, far, w_up, w_deep, sums, deep, inner):
    smem = pl.BlockSpec(memory_space=pltpu.SMEM)
    vmem = pl.BlockSpec(memory_space=pltpu.VMEM)
    return pl.pallas_call(
        outer_kernel,
        in_specs=[smem] * 3 + [vmem] * 11,
        out_shape=[
            jax.ShapeDtypeStruct((HALF_ROWS, 128), BF16),
            jax.ShapeDtypeStruct((HALF_ROWS, 128), BF16),
            jax.ShapeDtypeStruct((256, 256), BF16),
            jax.ShapeDtypeStruct((4, 64, 128), BF16),
            jax.ShapeDtypeStruct((4, 64, 128), BF16),
            jax.ShapeDtypeStruct((2, 64, 128), BF16),
            jax.ShapeDtypeStruct((2, 64, 128), BF16),
        ],
        scratch_shapes=[
            pltpu.VMEM((6, 10, 64, 256), BF16),
            pltpu.VMEM((4, 6, 64, 384), BF16),
            pltpu.VMEM((4, 4, 256, 256), BF16),
            pltpu.VMEM((9, 64, 256), F32),
            pltpu.VMEM((PAY_ROWS, 128), BF16),
        ],
        compiler_params=pltpu.CompilerParams(vmem_limit_bytes=VMEM_BYTES),
        cost_estimate=pl.CostEstimate(
            flops=2_000_000_000, bytes_accessed=4_000_000, transcendentals=65536
        ),
        name="outer_grads",
    )(odd_x, odd_y, part, own, cot, core, chip, near, far, w_up, w_deep, sums, deep, inner)


def input_columns(ys, at_ys, taps, w_up):
    empty = jnp.zeros((64, 256), BF16)
    spare = jnp.zeros((64, 64), BF16)
    weights = {}
    for a in range(3):
        for b in range(3):
            weights[a, b] = jnp.concatenate(
                [w_up[a, b, 2], w_up[a, b, 1], w_up[a, b, 0], spare], axis=1
            )
    total = jnp.zeros((2 * len(ys) * 64, 256), F32)
    for x in range(4):
        for y in at_ys:
            block = jnp.concatenate(
                [weights.get((s + 2 - x, t + 2 - y), empty) for s in range(2) for t in range(2)],
                axis=0,
            )
            total = total + lax.dot_general(
                window(taps, x, y, ys), block, (((1,), (1,)), ((), ())),
                preferred_element_type=F32,
            )
    return total


def picked(inner, outer, x, y):
    at = (x % 2) * 128 + (y % 2) * 64
    top = ((x // 2) * 2 + (y // 2 in (2, 3))) * 64
    return (inner if y // 2 in INNER else outer)[top : top + 64, at : at + 64]


def inner_input_kernel(odd_x, inner, outer, core, chip, w_up, out, taps):
    swap_x = odd_x[0] == 1

    def x_lo(k):
        return jnp.where(swap_x, core[k], chip[k])

    def x_hi(k):
        return jnp.where(swap_x, chip[k], core[k])

    def own(u, v):
        return picked(inner, outer, u, v)

    for x in range(6):
        taps[x, 0] = jnp.zeros((64, 256), BF16)
        taps[x, 9] = jnp.zeros((64, 256), BF16)
        for y in range(1, 9):
            taps[x, y] = depth_taps(level_column(x, y, own, x_lo, x_hi, None, None), 64)
    out[...] = input_columns(range(4), range(4), taps, w_up)


def inner_input(odd_x, inner, outer, core, chip, w_up):
    smem = pl.BlockSpec(memory_space=pltpu.SMEM)
    vmem = pl.BlockSpec(memory_space=pltpu.VMEM)
    return pl.pallas_call(
        inner_input_kernel,
        in_specs=[smem] + [vmem] * 5,
        out_shape=jax.ShapeDtypeStruct((512, 256), F32),
        scratch_shapes=[pltpu.VMEM((6, 10, 64, 256), BF16)],
        compiler_params=pltpu.CompilerParams(vmem_limit_bytes=VMEM_BYTES),
        cost_estimate=pl.CostEstimate(
            flops=500_000_000, bytes_accessed=2_000_000, transcendentals=0
        ),
        name="inner_input",
    )(odd_x, inner, outer, core, chip, w_up)


def outer_input_kernel(odd_y, near, far, w_up, part, out, taps):
    swap_y = odd_y[0] == 1

    def y_lo(k):
        return jnp.where(swap_y, near[k], far[k])

    def y_hi(k):
        return jnp.where(swap_y, far[k], near[k])

    for x in range(6):
        for y in (0, 9):
            taps[x, y] = depth_taps(level_column(x, y, None, None, None, y_lo, y_hi), 64)
    ends = {
        0: input_columns((0,), (0,), taps, w_up),
        3: input_columns((3,), (3,), taps, w_up),
    }
    for x in range(2):
        for y in range(4):
            top = (x * 4 + y) * 64
            rows = part[top : top + 64]
            if y in OUTER:
                rows = rows + ends[y][x * 64 : x * 64 + 64]
            rows = rows.astype(BF16)
            for s in range(2):
                for t in range(2):
                    at = s * 128 + t * 64
                    out[2 * x + s, 2 * y + t] = rows[:, at : at + 64]


def outer_input(odd_y, near, far, w_up, part):
    vmem = pl.BlockSpec(memory_space=pltpu.VMEM)
    return pl.pallas_call(
        outer_input_kernel,
        in_specs=[pl.BlockSpec(memory_space=pltpu.SMEM)] + [vmem] * 4,
        out_shape=jax.ShapeDtypeStruct((4, 8, 64, 64), BF16),
        scratch_shapes=[pltpu.VMEM((6, 10, 64, 256), BF16)],
        compiler_params=pltpu.CompilerParams(vmem_limit_bytes=VMEM_BYTES),
        cost_estimate=pl.CostEstimate(
            flops=300_000_000, bytes_accessed=4_000_000, transcendentals=0
        ),
        name="outer_input",
    )(odd_y, near, far, w_up, part)


def unpack_kernel(
    up_scale, deep_scale, odd, mine, other, up_out, deep_out, payload, up, deep, sems
):
    first = pl.multiple_of(odd[0] * HALF_ROWS, HALF_ROWS)
    payload[pl.ds(first, HALF_ROWS), :] = mine[...]
    payload[pl.ds(HALF_ROWS - first, HALF_ROWS), :] = other[...]
    copies = []
    pairs = {}
    for a in range(3):
        for k in range(a * 9, a * 9 + 9):
            top = DEEP_ROW + k * 64
            deep[a, k // 3 % 3, k % 3] = payload[top : top + 64, :].astype(F32) * deep_scale
        copies.append(pltpu.make_async_copy(deep.at[a], deep_out.at[a], sems.at[a]))
        copies[-1].start()
    for a in range(3):
        for b in range(3):
            k = a * 3 + b
            pair = payload[k * 64 : k * 64 + 64, :].astype(F32).T * up_scale
            up[a, b, 0] = pair[:64]
            up[a, b, 1] = pair[64:]
            if k % 2 == 0:
                top = PAIR_ROW + k // 2 * 64
                pairs[k // 2] = payload[top : top + 64, :].astype(F32).T * up_scale
            up[a, b, 2] = pairs[k // 2][k % 2 * 64 : k % 2 * 64 + 64]
        copies.append(pltpu.make_async_copy(up.at[a], up_out.at[a], sems.at[3 + a]))
        copies[-1].start()
    for copy in copies:
        copy.wait()


def unpack(odd, mine, other, up_scale, deep_scale):
    vmem = pl.BlockSpec(memory_space=pltpu.VMEM)
    hbm = pl.BlockSpec(memory_space=pltpu.HBM)
    return pl.pallas_call(
        functools.partial(unpack_kernel, up_scale, deep_scale),
        in_specs=[pl.BlockSpec(memory_space=pltpu.SMEM), vmem, vmem],
        out_specs=[hbm, hbm],
        out_shape=[
            jax.ShapeDtypeStruct((3, 3, 3, 64, 64), F32),
            jax.ShapeDtypeStruct((3, 3, 3, 64, 128), F32),
        ],
        scratch_shapes=[
            pltpu.VMEM((PAY_ROWS, 128), BF16),
            pltpu.VMEM((3, 3, 3, 64, 64), F32),
            pltpu.VMEM((3, 3, 3, 64, 128), F32),
            pltpu.SemaphoreType.DMA((6,)),
        ],
        compiler_params=pltpu.CompilerParams(vmem_limit_bytes=VMEM_BYTES),
        name="unpack",
    )(odd, mine, other)


def side_bit(step):
    index = lax.axis_index(step[0])
    return sum(index >> bit for bit in step[2]) & 1


def swap(value, steps, which):
    masks = {"gx": 0, "gy": 0}
    for place, (axis, mask, _) in enumerate(steps):
        if (which >> place) & 1:
            masks[axis] ^= mask
    axes = [axis for axis in ("gx", "gy") if masks[axis]]
    if len(axes) == 1:
        axis = axes[0]
        count = lax.axis_size(axis)
        return lax.ppermute(value, axis, [(i, i ^ masks[axis]) for i in range(count)])
    rows, cols = lax.axis_size("gx"), lax.axis_size("gy")
    pairs = [
        (i * cols + j, (i ^ masks["gx"]) * cols + (j ^ masks["gy"]))
        for i in range(rows)
        for j in range(cols)
    ]
    return lax.ppermute(value, ("gx", "gy"), pairs)


def place_of(steps):
    return sum(side_bit(step) << place for place, step in enumerate(steps))


def tree_sum(values):
    values = [value.astype(F32) for value in values]
    while len(values) > 1:
        values = [values[i] + values[i + 1] for i in range(0, len(values), 2)]
    return values[0].astype(BF16)


def scatter_sum(value, steps):
    parts = 1 << len(steps)
    rows = value.shape[0] // parts
    me = place_of(steps)
    found = [lax.dynamic_slice_in_dim(value, me * rows, rows, 0)]
    for k in range(1, parts):
        piece = lax.dynamic_slice_in_dim(value, (me ^ k) * rows, rows, 0)
        found.append(swap(piece, steps, k))
    return tree_sum(found)


def swap_sum(value, step):
    return tree_sum([value, swap(value, (step,), 1)])


def swap_sum_with(value, step, rider):
    rows = value.shape[0]
    got = swap(jnp.concatenate([value, rider]), (step,), 1)
    return tree_sum([value, got[:rows]]), got[rows:]


def gather(value, steps, riders):
    parts = 1 << len(steps)
    rows = value.shape[0]
    me = place_of(steps)
    found, came = [value], []
    for k in range(1, parts):
        rider = riders[k - 1]
        sent = value if rider is None else jnp.concatenate([value, rider])
        got = swap(sent, steps, k)
        found.append(got[:rows])
        came.append(got[rows:])
    for place in range(len(steps)):
        near = ((me >> place) & 1) == 0
        other = 1 << place
        found = [
            jnp.where(near, found[i & ~other], found[i | other])
            if not i & other
            else jnp.where(near, found[i | other], found[i & ~other])
            for i in range(parts)
        ]
    return jnp.concatenate(found), came


def pairs_of(axis, first):
    count = lax.axis_size(axis)
    found = []
    for i in range(first, count, 2):
        found += [(i, (i + 1) % count), ((i + 1) % count, i)]
    return found


def both_sides(first, second, axis):
    even = lax.ppermute(first, axis, pairs_of(axis, 0))
    odd = lax.ppermute(second, axis, pairs_of(axis, 1))
    return even, inside(odd, axis)


def inside(value, axis):
    index = lax.axis_index(axis)
    edge = (index == 0) | (index == lax.axis_size(axis) - 1)
    return jnp.where(edge, jnp.zeros_like(value), value)


def column_ends(odd_x, odd_y, core, chip, head, tail, level_rows):
    lo = jnp.where(odd_x == 1, core, chip)
    hi = jnp.where(odd_x == 1, chip, core)
    left = lax.broadcasted_iota(jnp.int32, (1, 64, 128), 2) < 64
    head = [head[:2], jnp.where(left, lo[0:1], hi[0:1])] + (
        [lo[4:5], head[2:], hi[4:5]] if level_rows else []
    )
    tail = [tail[:2], jnp.where(left, hi[3:4], lo[3:4])] + (
        [lo[7:8], tail[2:], hi[7:8]] if level_rows else []
    )
    head, tail = jnp.concatenate(head), jnp.concatenate(tail)
    return jnp.where(odd_y == 1, head, tail), jnp.where(odd_y == 1, tail, head)


def local(level_input, weight_upper, weight_deep, deep_cotangent):
    tiles = lax.axis_size("gx") * lax.axis_size("gy")
    up_scale = 1.0 / math.sqrt(math.prod(level_input.shape[:3]) * tiles)
    deep_scale = 1.0 / math.sqrt(math.prod(deep_cotangent.shape[:3]) * tiles)
    odd_x = (lax.axis_index("gx") & 1).astype(jnp.int32)
    odd_y = (lax.axis_index("gy") & 1).astype(jnp.int32)
    flag_x, flag_y = odd_x.reshape(1), odd_y.reshape(1)
    part = side_bit(CORE).astype(jnp.int32).reshape(1)

    to_core, to_chip, y_head, y_tail = faces(
        flag_x,
        pltpu.with_memory_space_constraint(level_input, pltpu.HBM),
        pltpu.with_memory_space_constraint(deep_cotangent, pltpu.HBM),
    )
    core, chip = both_sides(to_core, to_chip, "gx")
    to_near, to_far = column_ends(odd_x, odd_y, core, chip, y_head, y_tail, True)
    near, far = both_sides(to_near, to_far, "gy")

    sums, deep, inner = inner_grads(
        flag_x, level_input, deep_cotangent, core, chip, weight_upper, weight_deep
    )
    keep, send, outer, to_core, to_chip, y_head, y_tail = outer_grads(
        flag_x, flag_y, part, level_input, deep_cotangent, core, chip, near, far,
        weight_upper, weight_deep, sums, deep, inner,
    )
    at_x, at_y = lax.axis_index("gx"), lax.axis_index("gy")
    total = tree_sum([keep, swap(send, (CORE,), 1)])
    core = lax.ppermute(to_core, "gx", pairs_of("gx", 0))
    total, core = lax.optimization_barrier((total, core))
    total = scatter_sum(total, (Z_NEAR, X_NEAR))
    total, to_chip = lax.optimization_barrier((total, to_chip))
    second = swap(to_chip, (Y_FAR,), 1)
    total = swap_sum(total, Y_FAR)
    total, to_chip = lax.optimization_barrier((total, to_chip))
    first = swap(to_chip, (Y_NEAR,), 1)
    total = swap_sum(total, Y_NEAR)
    chip = jnp.where((((at_x + 1) >> 1) & 1) == 1, first, second)
    chip = inside(chip, "gx")
    inner_part = inner_input(flag_x, inner, outer, core, chip, weight_upper)
    to_near, to_far = column_ends(odd_x, odd_y, core, chip, y_head, y_tail, False)
    total, direct = swap_sum_with(total, Z_FAR, to_far.reshape(-1, 128))
    near = swap(to_near, (Z_NEAR,), 1)
    total, near = lax.optimization_barrier((total, near))
    total, handed_far = swap_sum_with(total, X_FAR, direct)
    total, inner_part = lax.optimization_barrier((total, inner_part))
    total, (_, handed_near, _) = gather(total, (Z_NEAR, X_NEAR), (None, direct, None))
    plane, depth = at_y >> 2, at_y & 3
    none = jnp.zeros_like(direct)
    handed = jnp.where(
        ((depth == 0) & (plane == 2)) | ((depth == 3) & (plane == 1)), handed_far, handed_near
    )
    ends = (at_y == 0) | (at_y == lax.axis_size("gy") - 1)
    far = jnp.where((depth == 1) | (depth == 2), direct, jnp.where(ends, none, handed))
    input_grad = outer_input(
        flag_y, near, far.reshape(to_far.shape), weight_upper, inner_part
    )
    other = swap(total, (CORE,), 1)
    upper, deep = unpack(part, total, other, up_scale, deep_scale)
    return (input_grad, upper, deep)


def solution(mesh):
    placed = (P("gx", "gy", None, None), P(), P(), P("gx", "gy", None, None))
    return jax.shard_map(
        local,
        mesh=mesh,
        in_specs=placed,
        out_specs=(P("gx", "gy", None, None), P(), P()),
        check_vma=False,
    )
```

```python
import functools
import math

import jax
import jax.numpy as jnp
from jax import lax
from jax.experimental import pallas as pl
from jax.experimental.pallas import tpu as pltpu
from jax.sharding import PartitionSpec as P

F32 = jnp.float32
BF16 = jnp.bfloat16
VMEM_BYTES = 28 * 1024 * 1024

PAIR_ROW = 9 * 64
DEEP_ROW = 14 * 64
PAY_ROWS = 41 * 64
HALF_ROWS = PAY_ROWS // 2

CORE = ("gx", 1, (0, 1))
Y_NEAR = ("gx", 3, (1, 2))
Y_FAR = ("gx", 7, (2,))
Z_NEAR = ("gy", 1, (0, 1))
Z_FAR = ("gy", 3, (1,))
X_NEAR = ("gy", 4, (2, 3))
X_FAR = ("gy", 12, (3,))


def depth_taps(row, gap):
    row = row.astype(F32)
    edge = jnp.zeros((1, row.shape[1]), F32)
    below = jnp.concatenate([edge, row[:-1]], axis=0)
    above = jnp.concatenate([row[1:], edge], axis=0)
    pieces = [below, row, above]
    if gap:
        pieces.append(jnp.zeros((row.shape[0], gap), F32))
    return jnp.concatenate(pieces, axis=1).astype(BF16)


INNER = (1, 2)
OUTER = (0, 3)


def shifted(row):
    row = row.astype(F32)
    edge = jnp.zeros((1, row.shape[1]), F32)
    return (
        jnp.concatenate([edge, row[:-1]], axis=0),
        row,
        jnp.concatenate([row[1:], edge], axis=0),
    )


def build_taps(taps, ys, column):
    for y in ys:
        parts = [shifted(column(x, y)) for x in range(6)]
        for block in range(2):
            for x in range(3):
                pieces = parts[2 * block + x] + (parts[2 * block + 3][x],)
                taps[block, x, y] = jnp.concatenate(pieces, axis=1).astype(BF16)


def level_window(taps, at_x, at_y, ys):
    return jnp.concatenate([taps[x, at_x, 2 * y + at_y] for x in range(2) for y in ys], axis=0)


def window(taps, at_x, at_y, ys):
    return jnp.concatenate(
        [taps[2 * x + at_x, 2 * y + at_y] for x in range(2) for y in ys], axis=0
    )


def deep_window(taps, at_x, at_y, ys):
    return jnp.concatenate([taps[x + at_x, y + at_y] for x in range(2) for y in ys], axis=0)


def faces_kernel(
    odd, own, cot, to_core, to_chip, y_head, y_tail, x_first, x_last, y_first, y_last, deep, sems
):
    copies = [
        pltpu.make_async_copy(source, target, sems.at[k])
        for k, (source, target) in enumerate(
            [
                (own.at[0], x_first),
                (own.at[3], x_last),
                (own.at[:, 0], y_first),
                (own.at[:, 7], y_last),
                (cot, deep),
            ]
        )
    ]
    for copy in copies:
        copy.start()
    for copy in copies:
        copy.wait()
    swapped = odd[0] == 1
    for k in range(4):
        head = jnp.concatenate([x_first[2 * k + 1], x_first[2 * k]], axis=1)
        tail = jnp.concatenate([x_last[2 * k], x_last[2 * k + 1]], axis=1)
        to_core[k] = jnp.where(swapped, head, tail)
        to_chip[k] = jnp.where(swapped, tail, head)
        to_core[4 + k] = jnp.where(swapped, deep[0, k], deep[1, k])
        to_chip[4 + k] = jnp.where(swapped, deep[1, k], deep[0, k])
    for k in range(2):
        y_head[k] = jnp.concatenate([y_first[2 * k], y_first[2 * k + 1]], axis=1)
        y_tail[k] = jnp.concatenate([y_last[2 * k], y_last[2 * k + 1]], axis=1)
        y_head[2 + k] = deep[k, 0]
        y_tail[2 + k] = deep[k, 3]


def faces(odd, own, cot):
    hbm = pl.BlockSpec(memory_space=pltpu.HBM)
    return pl.pallas_call(
        faces_kernel,
        in_specs=[pl.BlockSpec(memory_space=pltpu.SMEM), hbm, hbm],
        out_shape=[pltpu.VMEM((8, 64, 128), BF16)] * 2 + [pltpu.VMEM((4, 64, 128), BF16)] * 2,
        scratch_shapes=[
            pltpu.VMEM((8, 64, 64), BF16),
            pltpu.VMEM((8, 64, 64), BF16),
            pltpu.VMEM((4, 64, 64), BF16),
            pltpu.VMEM((4, 64, 64), BF16),
            pltpu.VMEM((2, 4, 64, 128), BF16),
            pltpu.SemaphoreType.DMA((5,)),
        ],
        name="faces",
    )(odd, own, cot)


def level_column(x, y, own, x_lo, x_hi, y_lo, y_hi):
    if y == 0 or y == 9:
        pairs = y_lo if y == 0 else y_hi
        if 1 <= x <= 4:
            return half(pairs(((x - 1) // 2)), (x - 1) % 2)
        return half(pairs(2), int((x == 5) == (y == 9)))
    if x == 0:
        return half(x_lo((y - 1) // 2), (y - 1) % 2)
    if x == 5:
        return half(x_hi((y - 1) // 2), 1 - (y - 1) % 2)
    return own(x - 1, y - 1)


def half(value, which):
    return value[:, which * 64 : which * 64 + 64]


def build_blocks(w_up, blocks):
    empty = jnp.zeros((192, 64), BF16)
    for y in range(4):
        for x in range(3):
            left = w_up[x, y].reshape(192, 64) if y < 3 else empty
            right = w_up[x, y - 1].reshape(192, 64) if y > 0 else empty
            pair = jnp.concatenate([left, right], axis=1)
            blocks[x, y, 0:192, 0:128] = pair
            if x < 2:
                blocks[x + 1, y, 0:192, 128:256] = pair
            else:
                for c in range(3):
                    blocks[c, y, 192:256, 128:256] = pair[c * 64 : c * 64 + 64]
            blocks[x, y, 192:256, 0:128] = jnp.zeros((64, 128), BF16)
        blocks[0, y, 0:192, 128:256] = jnp.zeros((192, 128), BF16)


def column_grads(ys, taps, cot_taps, blocks, w_deep, sums, deep, last):
    rows = 2 * len(ys) * 64
    pre = jnp.zeros((rows, 256), F32)
    for x in range(3):
        for y in range(4):
            pre = pre + jnp.dot(
                level_window(taps, x, y, ys), blocks[x, y], preferred_element_type=F32
            )
    sig = 1.0 / (1.0 + jnp.exp(-pre))
    act = pre * sig
    summed = act[:, :128] + act[:, 128:]
    pooled = 0.25 * (summed[:, :64] + summed[:, 64:])
    pooled_t = pooled.T.astype(BF16)

    pooled_grad = jnp.zeros((rows, 64), F32)
    for a in range(3):
        for b in range(3):
            weight = jnp.concatenate([w_deep[2 - a, 2 - b, 2 - j] for j in range(3)], axis=1)
            pooled_grad = pooled_grad + lax.dot_general(
                deep_window(cot_taps, a, b, ys), weight, (((1,), (1,)), ((), ())),
                preferred_element_type=F32,
            )
    wide = pooled_grad.astype(BF16).astype(F32)
    wide = jnp.concatenate([wide, wide], axis=1)
    wide = jnp.concatenate([wide, wide], axis=1)
    grad = 0.25 * wide * (sig * (1.0 + pre * (1.0 - sig)))
    grad_t = grad.T.astype(BF16)

    for a in range(3):
        for b in range(3):
            out = jnp.dot(
                pooled_t, deep_window(cot_taps, 2 - a, 2 - b, ys), preferred_element_type=F32
            )
            for j in range(3):
                deep((a * 3 + b) * 3 + 2 - j, out[:, j * 128 : j * 128 + 128])
    for x in range(3):
        for y in range(4):
            kept = [(s, t) for s in range(2) for t in range(2) if 0 <= y - t < 3]
            left = jnp.concatenate(
                [grad_t[(s * 2 + t) * 64 : (s * 2 + t) * 64 + 64] for s, t in kept], axis=0
            )
            part = jnp.dot(left, level_window(taps, x, y, ys), preferred_element_type=F32)
            for k, (s, t) in enumerate(kept):
                piece = part[k * 64 : k * 64 + 64]
                if x >= s:
                    sums((x - s) * 3 + y - t, piece, s == 0 and t == 0)
                if s == 1:
                    place = (y - t) * 3 + x
                    tail = piece[:, 192:256]
                    last[place] = tail if t == 0 else last[place] + tail
    return grad.astype(BF16)


def add_last(sums, last):
    for b in range(3):
        for c in range(3):
            at = c * 64
            sums[6 + b, :, at : at + 64] = sums[6 + b, :, at : at + 64] + last[b * 3 + c]


def inner_kernel(odd_x, own, cot, core, chip, w_up, w_deep, sums, deep, inner, taps, cot_taps, blocks, last):
    swap_x = odd_x[0] == 1

    def x_lo(k):
        return jnp.where(swap_x, core[k], chip[k])

    def x_hi(k):
        return jnp.where(swap_x, chip[k], core[k])

    def column(x, y):
        return level_column(x, y, lambda u, v: own[u, v], x_lo, x_hi, None, None)

    build_taps(taps, range(2, 8), column)
    for x in range(4):
        for y in range(1, 5):
            if x == 0:
                row = x_lo(3 + y)
            elif x == 3:
                row = x_hi(3 + y)
            else:
                row = cot[x - 1, y - 1]
            cot_taps[x, y] = depth_taps(row, 0)
    build_blocks(w_up, blocks)

    def add_sum(k, piece, first):
        sums[k] = piece if first else sums[k] + piece

    def add_deep(k, piece):
        deep[k] = piece

    inner[...] = column_grads(INNER, taps, cot_taps, blocks, w_deep, add_sum, add_deep, last)
    add_last(sums, last)


def inner_grads(odd_x, own, cot, core, chip, w_up, w_deep):
    smem = pl.BlockSpec(memory_space=pltpu.SMEM)
    vmem = pl.BlockSpec(memory_space=pltpu.VMEM)
    return pl.pallas_call(
        inner_kernel,
        in_specs=[smem] + [vmem] * 6,
        out_shape=[
            jax.ShapeDtypeStruct((9, 64, 256), F32),
            jax.ShapeDtypeStruct((27, 64, 128), F32),
            jax.ShapeDtypeStruct((256, 256), BF16),
        ],
        scratch_shapes=[
            pltpu.VMEM((2, 3, 10, 64, 256), BF16),
            pltpu.VMEM((4, 6, 64, 384), BF16),
            pltpu.VMEM((3, 4, 256, 256), BF16),
            pltpu.VMEM((9, 64, 64), F32),
        ],
        compiler_params=pltpu.CompilerParams(vmem_limit_bytes=VMEM_BYTES),
        cost_estimate=pl.CostEstimate(
            flops=2_000_000_000, bytes_accessed=4_000_000, transcendentals=65536
        ),
        name="inner_grads",
    )(odd_x, own, cot, core, chip, w_up, w_deep)


def outer_kernel(
    odd_x, odd_y, part, own, cot, core, chip, near, far, w_up, w_deep, sums_in, deep_in, inner,
    keep, send, outer, to_core, to_chip, gy_head, gy_tail,
    taps, cot_taps, blocks, last, sums, payload,
):
    swap_x = odd_x[0] == 1
    swap_y = odd_y[0] == 1

    def x_lo(k):
        return jnp.where(swap_x, core[k], chip[k])

    def x_hi(k):
        return jnp.where(swap_x, chip[k], core[k])

    def y_lo(k):
        return jnp.where(swap_y, near[k], far[k])

    def y_hi(k):
        return jnp.where(swap_y, far[k], near[k])

    def column(x, y):
        return level_column(x, y, lambda u, v: own[u, v], x_lo, x_hi, y_lo, y_hi)

    build_taps(taps, (0, 1, 2, 3, 6, 7, 8, 9), column)
    for x in range(4):
        for y in range(6):
            if y == 0:
                row = y_lo(3 + x)
            elif y == 5:
                row = y_hi(3 + x)
            elif x == 0:
                row = x_lo(3 + y)
            elif x == 3:
                row = x_hi(3 + y)
            else:
                row = cot[x - 1, y - 1]
            cot_taps[x, y] = depth_taps(row, 0)
    build_blocks(w_up, blocks)

    def add_sum(k, piece, first):
        sums[k] = (sums_in[k] if first else sums[k]) + piece

    def add_deep(k, piece):
        top = DEEP_ROW + k * 64
        payload[top : top + 64, :] = (deep_in[k] + piece).astype(BF16)

    rounded = column_grads(OUTER, taps, cot_taps, blocks, w_deep, add_sum, add_deep, last)
    add_last(sums, last)
    outer[...] = rounded

    def block(x, y):
        top = (x * 2 + (y in (2, 3))) * 64
        return (inner if y in INNER else rounded)[top : top + 64]

    for k in range(4):
        head = block(0, k)[:, 0:128]
        head = jnp.concatenate([half(head, 1), half(head, 0)], axis=1)
        tail = block(1, k)[:, 128:256]
        to_core[k] = jnp.where(swap_x, head, tail)
        to_chip[k] = jnp.where(swap_x, tail, head)
    for k in range(2):
        first, last = block(k, 0), block(k, 3)
        gy_head[k] = jnp.concatenate([first[:, 0:64], first[:, 128:192]], axis=1)
        gy_tail[k] = jnp.concatenate([last[:, 64:128], last[:, 192:256]], axis=1)

    for k in range(9):
        payload[k * 64 : k * 64 + 64, :] = sums[k, :, 0:128].astype(BF16)
    for k in range(5):
        left = sums[2 * k, :, 128:192]
        right = sums[2 * k + 1, :, 128:192] if k < 4 else jnp.zeros((64, 64), F32)
        top = PAIR_ROW + k * 64
        payload[top : top + 64, :] = jnp.concatenate([left, right], axis=1).astype(BF16)
    mine = pl.multiple_of(part[0] * HALF_ROWS, HALF_ROWS)
    keep[...] = payload[pl.ds(mine, HALF_ROWS), :]
    send[...] = payload[pl.ds(HALF_ROWS - mine, HALF_ROWS), :]


def outer_grads(odd_x, odd_y, part, own, cot, core, chip, near, far, w_up, w_deep, sums, deep, inner):
    smem = pl.BlockSpec(memory_space=pltpu.SMEM)
    vmem = pl.BlockSpec(memory_space=pltpu.VMEM)
    return pl.pallas_call(
        outer_kernel,
        in_specs=[smem] * 3 + [vmem] * 11,
        out_shape=[
            jax.ShapeDtypeStruct((HALF_ROWS, 128), BF16),
            jax.ShapeDtypeStruct((HALF_ROWS, 128), BF16),
            jax.ShapeDtypeStruct((256, 256), BF16),
            jax.ShapeDtypeStruct((4, 64, 128), BF16),
            jax.ShapeDtypeStruct((4, 64, 128), BF16),
            jax.ShapeDtypeStruct((2, 64, 128), BF16),
            jax.ShapeDtypeStruct((2, 64, 128), BF16),
        ],
        scratch_shapes=[
            pltpu.VMEM((2, 3, 10, 64, 256), BF16),
            pltpu.VMEM((4, 6, 64, 384), BF16),
            pltpu.VMEM((3, 4, 256, 256), BF16),
            pltpu.VMEM((9, 64, 64), F32),
            pltpu.VMEM((9, 64, 256), F32),
            pltpu.VMEM((PAY_ROWS, 128), BF16),
        ],
        compiler_params=pltpu.CompilerParams(vmem_limit_bytes=VMEM_BYTES),
        cost_estimate=pl.CostEstimate(
            flops=2_000_000_000, bytes_accessed=4_000_000, transcendentals=65536
        ),
        name="outer_grads",
    )(odd_x, odd_y, part, own, cot, core, chip, near, far, w_up, w_deep, sums, deep, inner)


def input_columns(ys, at_ys, taps, w_up):
    empty = jnp.zeros((64, 256), BF16)
    spare = jnp.zeros((64, 64), BF16)
    weights = {}
    for a in range(3):
        for b in range(3):
            weights[a, b] = jnp.concatenate(
                [w_up[a, b, 2], w_up[a, b, 1], w_up[a, b, 0], spare], axis=1
            )
    total = jnp.zeros((2 * len(ys) * 64, 256), F32)
    for x in range(4):
        for y in at_ys:
            block = jnp.concatenate(
                [weights.get((s + 2 - x, t + 2 - y), empty) for s in range(2) for t in range(2)],
                axis=0,
            )
            total = total + lax.dot_general(
                window(taps, x, y, ys), block, (((1,), (1,)), ((), ())),
                preferred_element_type=F32,
            )
    return total


def picked(inner, outer, x, y):
    at = (x % 2) * 128 + (y % 2) * 64
    top = ((x // 2) * 2 + (y // 2 in (2, 3))) * 64
    return (inner if y // 2 in INNER else outer)[top : top + 64, at : at + 64]


def inner_input_kernel(odd_x, inner, outer, core, chip, w_up, out, taps):
    swap_x = odd_x[0] == 1

    def x_lo(k):
        return jnp.where(swap_x, core[k], chip[k])

    def x_hi(k):
        return jnp.where(swap_x, chip[k], core[k])

    def own(u, v):
        return picked(inner, outer, u, v)

    for x in range(6):
        taps[x, 0] = jnp.zeros((64, 256), BF16)
        taps[x, 9] = jnp.zeros((64, 256), BF16)
        for y in range(1, 9):
            taps[x, y] = depth_taps(level_column(x, y, own, x_lo, x_hi, None, None), 64)
    out[...] = input_columns(range(4), range(4), taps, w_up)


def inner_input(odd_x, inner, outer, core, chip, w_up):
    smem = pl.BlockSpec(memory_space=pltpu.SMEM)
    vmem = pl.BlockSpec(memory_space=pltpu.VMEM)
    return pl.pallas_call(
        inner_input_kernel,
        in_specs=[smem] + [vmem] * 5,
        out_shape=jax.ShapeDtypeStruct((512, 256), F32),
        scratch_shapes=[pltpu.VMEM((6, 10, 64, 256), BF16)],
        compiler_params=pltpu.CompilerParams(vmem_limit_bytes=VMEM_BYTES),
        cost_estimate=pl.CostEstimate(
            flops=500_000_000, bytes_accessed=2_000_000, transcendentals=0
        ),
        name="inner_input",
    )(odd_x, inner, outer, core, chip, w_up)


def outer_input_kernel(odd_y, near, far, w_up, part, out, taps):
    swap_y = odd_y[0] == 1

    def y_lo(k):
        return jnp.where(swap_y, near[k], far[k])

    def y_hi(k):
        return jnp.where(swap_y, far[k], near[k])

    for x in range(6):
        for y in (0, 9):
            taps[x, y] = depth_taps(level_column(x, y, None, None, None, y_lo, y_hi), 64)
    ends = {
        0: input_columns((0,), (0,), taps, w_up),
        3: input_columns((3,), (3,), taps, w_up),
    }
    for x in range(2):
        for y in range(4):
            top = (x * 4 + y) * 64
            rows = part[top : top + 64]
            if y in OUTER:
                rows = rows + ends[y][x * 64 : x * 64 + 64]
            rows = rows.astype(BF16)
            for s in range(2):
                for t in range(2):
                    at = s * 128 + t * 64
                    out[2 * x + s, 2 * y + t] = rows[:, at : at + 64]


def outer_input(odd_y, near, far, w_up, part):
    vmem = pl.BlockSpec(memory_space=pltpu.VMEM)
    return pl.pallas_call(
        outer_input_kernel,
        in_specs=[pl.BlockSpec(memory_space=pltpu.SMEM)] + [vmem] * 4,
        out_shape=jax.ShapeDtypeStruct((4, 8, 64, 64), BF16),
        scratch_shapes=[pltpu.VMEM((6, 10, 64, 256), BF16)],
        compiler_params=pltpu.CompilerParams(vmem_limit_bytes=VMEM_BYTES),
        cost_estimate=pl.CostEstimate(
            flops=300_000_000, bytes_accessed=4_000_000, transcendentals=0
        ),
        name="outer_input",
    )(odd_y, near, far, w_up, part)


def unpack_kernel(
    up_scale, deep_scale, odd, mine, other, up_out, deep_out, payload, up, deep, sems
):
    first = pl.multiple_of(odd[0] * HALF_ROWS, HALF_ROWS)
    payload[pl.ds(first, HALF_ROWS), :] = mine[...]
    payload[pl.ds(HALF_ROWS - first, HALF_ROWS), :] = other[...]
    copies = []
    pairs = {}
    for a in range(3):
        for k in range(a * 9, a * 9 + 9):
            top = DEEP_ROW + k * 64
            deep[a, k // 3 % 3, k % 3] = payload[top : top + 64, :].astype(F32) * deep_scale
        copies.append(pltpu.make_async_copy(deep.at[a], deep_out.at[a], sems.at[a]))
        copies[-1].start()
    for a in range(3):
        for b in range(3):
            k = a * 3 + b
            pair = payload[k * 64 : k * 64 + 64, :].astype(F32).T * up_scale
            up[a, b, 0] = pair[:64]
            up[a, b, 1] = pair[64:]
            if k % 2 == 0:
                top = PAIR_ROW + k // 2 * 64
                pairs[k // 2] = payload[top : top + 64, :].astype(F32).T * up_scale
            up[a, b, 2] = pairs[k // 2][k % 2 * 64 : k % 2 * 64 + 64]
        copies.append(pltpu.make_async_copy(up.at[a], up_out.at[a], sems.at[3 + a]))
        copies[-1].start()
    for copy in copies:
        copy.wait()


def unpack(odd, mine, other, up_scale, deep_scale):
    vmem = pl.BlockSpec(memory_space=pltpu.VMEM)
    hbm = pl.BlockSpec(memory_space=pltpu.HBM)
    return pl.pallas_call(
        functools.partial(unpack_kernel, up_scale, deep_scale),
        in_specs=[pl.BlockSpec(memory_space=pltpu.SMEM), vmem, vmem],
        out_specs=[hbm, hbm],
        out_shape=[
            jax.ShapeDtypeStruct((3, 3, 3, 64, 64), F32),
            jax.ShapeDtypeStruct((3, 3, 3, 64, 128), F32),
        ],
        scratch_shapes=[
            pltpu.VMEM((PAY_ROWS, 128), BF16),
            pltpu.VMEM((3, 3, 3, 64, 64), F32),
            pltpu.VMEM((3, 3, 3, 64, 128), F32),
            pltpu.SemaphoreType.DMA((6,)),
        ],
        compiler_params=pltpu.CompilerParams(vmem_limit_bytes=VMEM_BYTES),
        name="unpack",
    )(odd, mine, other)


def side_bit(step):
    index = lax.axis_index(step[0])
    return sum(index >> bit for bit in step[2]) & 1


def swap(value, steps, which):
    masks = {"gx": 0, "gy": 0}
    for place, (axis, mask, _) in enumerate(steps):
        if (which >> place) & 1:
            masks[axis] ^= mask
    axes = [axis for axis in ("gx", "gy") if masks[axis]]
    if len(axes) == 1:
        axis = axes[0]
        count = lax.axis_size(axis)
        return lax.ppermute(value, axis, [(i, i ^ masks[axis]) for i in range(count)])
    rows, cols = lax.axis_size("gx"), lax.axis_size("gy")
    pairs = [
        (i * cols + j, (i ^ masks["gx"]) * cols + (j ^ masks["gy"]))
        for i in range(rows)
        for j in range(cols)
    ]
    return lax.ppermute(value, ("gx", "gy"), pairs)


def place_of(steps):
    return sum(side_bit(step) << place for place, step in enumerate(steps))


def tree_sum(values):
    values = [value.astype(F32) for value in values]
    while len(values) > 1:
        values = [values[i] + values[i + 1] for i in range(0, len(values), 2)]
    return values[0].astype(BF16)


def scatter_sum(value, steps):
    parts = 1 << len(steps)
    rows = value.shape[0] // parts
    me = place_of(steps)
    found = [lax.dynamic_slice_in_dim(value, me * rows, rows, 0)]
    for k in range(1, parts):
        piece = lax.dynamic_slice_in_dim(value, (me ^ k) * rows, rows, 0)
        found.append(swap(piece, steps, k))
    return tree_sum(found)


def swap_sum(value, step):
    return tree_sum([value, swap(value, (step,), 1)])


def swap_sum_with(value, step, rider):
    rows = value.shape[0]
    got = swap(jnp.concatenate([value, rider]), (step,), 1)
    return tree_sum([value, got[:rows]]), got[rows:]


def gather(value, steps, riders):
    parts = 1 << len(steps)
    rows = value.shape[0]
    me = place_of(steps)
    found, came = [value], []
    for k in range(1, parts):
        rider = riders[k - 1]
        sent = value if rider is None else jnp.concatenate([value, rider])
        got = swap(sent, steps, k)
        found.append(got[:rows])
        came.append(got[rows:])
    for place in range(len(steps)):
        near = ((me >> place) & 1) == 0
        other = 1 << place
        found = [
            jnp.where(near, found[i & ~other], found[i | other])
            if not i & other
            else jnp.where(near, found[i | other], found[i & ~other])
            for i in range(parts)
        ]
    return jnp.concatenate(found), came


def pairs_of(axis, first):
    count = lax.axis_size(axis)
    found = []
    for i in range(first, count, 2):
        found += [(i, (i + 1) % count), ((i + 1) % count, i)]
    return found


def both_sides(first, second, axis):
    even = lax.ppermute(first, axis, pairs_of(axis, 0))
    odd = lax.ppermute(second, axis, pairs_of(axis, 1))
    return even, inside(odd, axis)


def inside(value, axis):
    index = lax.axis_index(axis)
    edge = (index == 0) | (index == lax.axis_size(axis) - 1)
    return jnp.where(edge, jnp.zeros_like(value), value)


def column_ends(odd_x, odd_y, core, chip, head, tail, level_rows):
    lo = jnp.where(odd_x == 1, core, chip)
    hi = jnp.where(odd_x == 1, chip, core)
    left = lax.broadcasted_iota(jnp.int32, (1, 64, 128), 2) < 64
    head = [head[:2], jnp.where(left, lo[0:1], hi[0:1])] + (
        [lo[4:5], head[2:], hi[4:5]] if level_rows else []
    )
    tail = [tail[:2], jnp.where(left, hi[3:4], lo[3:4])] + (
        [lo[7:8], tail[2:], hi[7:8]] if level_rows else []
    )
    head, tail = jnp.concatenate(head), jnp.concatenate(tail)
    return jnp.where(odd_y == 1, head, tail), jnp.where(odd_y == 1, tail, head)


def local(level_input, weight_upper, weight_deep, deep_cotangent):
    tiles = lax.axis_size("gx") * lax.axis_size("gy")
    up_scale = 1.0 / math.sqrt(math.prod(level_input.shape[:3]) * tiles)
    deep_scale = 1.0 / math.sqrt(math.prod(deep_cotangent.shape[:3]) * tiles)
    odd_x = (lax.axis_index("gx") & 1).astype(jnp.int32)
    odd_y = (lax.axis_index("gy") & 1).astype(jnp.int32)
    flag_x, flag_y = odd_x.reshape(1), odd_y.reshape(1)
    part = side_bit(CORE).astype(jnp.int32).reshape(1)

    to_core, to_chip, y_head, y_tail = faces(
        flag_x,
        pltpu.with_memory_space_constraint(level_input, pltpu.HBM),
        pltpu.with_memory_space_constraint(deep_cotangent, pltpu.HBM),
    )
    core, chip = both_sides(to_core, to_chip, "gx")
    to_near, to_far = column_ends(odd_x, odd_y, core, chip, y_head, y_tail, True)
    near, far = both_sides(to_near, to_far, "gy")

    sums, deep, inner = inner_grads(
        flag_x, level_input, deep_cotangent, core, chip, weight_upper, weight_deep
    )
    keep, send, outer, to_core, to_chip, y_head, y_tail = outer_grads(
        flag_x, flag_y, part, level_input, deep_cotangent, core, chip, near, far,
        weight_upper, weight_deep, sums, deep, inner,
    )
    at_x, at_y = lax.axis_index("gx"), lax.axis_index("gy")
    total = tree_sum([keep, swap(send, (CORE,), 1)])
    core = lax.ppermute(to_core, "gx", pairs_of("gx", 0))
    total, core = lax.optimization_barrier((total, core))
    total = scatter_sum(total, (Z_NEAR, X_NEAR))
    total, to_chip = lax.optimization_barrier((total, to_chip))
    second = swap(to_chip, (Y_FAR,), 1)
    total = swap_sum(total, Y_FAR)
    total, to_chip = lax.optimization_barrier((total, to_chip))
    first = swap(to_chip, (Y_NEAR,), 1)
    total = swap_sum(total, Y_NEAR)
    chip = jnp.where((((at_x + 1) >> 1) & 1) == 1, first, second)
    chip = inside(chip, "gx")
    inner_part = inner_input(flag_x, inner, outer, core, chip, weight_upper)
    to_near, to_far = column_ends(odd_x, odd_y, core, chip, y_head, y_tail, False)
    total, direct = swap_sum_with(total, Z_FAR, to_far.reshape(-1, 128))
    near = swap(to_near, (Z_NEAR,), 1)
    total, near = lax.optimization_barrier((total, near))
    total, handed_far = swap_sum_with(total, X_FAR, direct)
    total, inner_part = lax.optimization_barrier((total, inner_part))
    total, (_, handed_near, _) = gather(total, (Z_NEAR, X_NEAR), (None, direct, None))
    plane, depth = at_y >> 2, at_y & 3
    none = jnp.zeros_like(direct)
    handed = jnp.where(
        ((depth == 0) & (plane == 2)) | ((depth == 3) & (plane == 1)), handed_far, handed_near
    )
    ends = (at_y == 0) | (at_y == lax.axis_size("gy") - 1)
    far = jnp.where((depth == 1) | (depth == 2), direct, jnp.where(ends, none, handed))
    input_grad = outer_input(
        flag_y, near, far.reshape(to_far.shape), weight_upper, inner_part
    )
    other = swap(total, (CORE,), 1)
    upper, deep = unpack(part, total, other, up_scale, deep_scale)
    return (input_grad, upper, deep)


def solution(mesh):
    placed = (P("gx", "gy", None, None), P(), P(), P("gx", "gy", None, None))
    return jax.shard_map(
        local,
        mesh=mesh,
        in_specs=placed,
        out_specs=(P("gx", "gy", None, None), P(), P()),
        check_vma=False,
    )
```

```python
import functools
import math

import jax
import jax.numpy as jnp
from jax import lax
from jax.experimental import pallas as pl
from jax.experimental.pallas import tpu as pltpu
from jax.sharding import PartitionSpec as P

F32 = jnp.float32
BF16 = jnp.bfloat16
VMEM_BYTES = 28 * 1024 * 1024

PAIR_ROW = 9 * 64
DEEP_ROW = 14 * 64
PAY_ROWS = 41 * 64
HALF_ROWS = PAY_ROWS // 2

CORE = ("gx", 1, (0, 1))
Y_NEAR = ("gx", 3, (1, 2))
Y_FAR = ("gx", 7, (2,))
Z_NEAR = ("gy", 1, (0, 1))
Z_FAR = ("gy", 3, (1,))
X_NEAR = ("gy", 4, (2, 3))
X_FAR = ("gy", 12, (3,))


def depth_taps(row, gap):
    row = row.astype(F32)
    edge = jnp.zeros((1, row.shape[1]), F32)
    below = jnp.concatenate([edge, row[:-1]], axis=0)
    above = jnp.concatenate([row[1:], edge], axis=0)
    pieces = [below, row, above]
    if gap:
        pieces.append(jnp.zeros((row.shape[0], gap), F32))
    return jnp.concatenate(pieces, axis=1).astype(BF16)


INNER = (1, 2)
OUTER = (0, 3)


def shifted(row):
    row = row.astype(F32)
    edge = jnp.zeros((1, row.shape[1]), F32)
    return (
        jnp.concatenate([edge, row[:-1]], axis=0),
        row,
        jnp.concatenate([row[1:], edge], axis=0),
    )


def build_taps(taps, ys, column):
    for y in ys:
        parts = [shifted(column(x, y)) for x in range(6)]
        for block in range(2):
            for x in range(3):
                pieces = parts[2 * block + x] + (parts[2 * block + 3][x],)
                taps[block, x, y] = jnp.concatenate(pieces, axis=1).astype(BF16)


def level_window(taps, at_x, at_y, ys):
    return jnp.concatenate([taps[x, at_x, 2 * y + at_y] for x in range(2) for y in ys], axis=0)


def window(taps, at_x, at_y, ys):
    return jnp.concatenate(
        [taps[2 * x + at_x, 2 * y + at_y] for x in range(2) for y in ys], axis=0
    )


def deep_window(taps, at_x, at_y, ys):
    return jnp.concatenate([taps[x + at_x, y + at_y] for x in range(2) for y in ys], axis=0)


def faces_kernel(
    odd, own, cot, to_core, to_chip, y_head, y_tail, x_first, x_last, y_first, y_last, deep, sems
):
    copies = [
        pltpu.make_async_copy(source, target, sems.at[k])
        for k, (source, target) in enumerate(
            [
                (own.at[0], x_first),
                (own.at[3], x_last),
                (own.at[:, 0], y_first),
                (own.at[:, 7], y_last),
                (cot, deep),
            ]
        )
    ]
    for copy in copies:
        copy.start()
    for copy in copies:
        copy.wait()
    swapped = odd[0] == 1
    for k in range(4):
        head = jnp.concatenate([x_first[2 * k + 1], x_first[2 * k]], axis=1)
        tail = jnp.concatenate([x_last[2 * k], x_last[2 * k + 1]], axis=1)
        to_core[k] = jnp.where(swapped, head, tail)
        to_chip[k] = jnp.where(swapped, tail, head)
        to_core[4 + k] = jnp.where(swapped, deep[0, k], deep[1, k])
        to_chip[4 + k] = jnp.where(swapped, deep[1, k], deep[0, k])
    for k in range(2):
        y_head[k] = jnp.concatenate([y_first[2 * k], y_first[2 * k + 1]], axis=1)
        y_tail[k] = jnp.concatenate([y_last[2 * k], y_last[2 * k + 1]], axis=1)
        y_head[2 + k] = deep[k, 0]
        y_tail[2 + k] = deep[k, 3]


def faces(odd, own, cot):
    hbm = pl.BlockSpec(memory_space=pltpu.HBM)
    return pl.pallas_call(
        faces_kernel,
        in_specs=[pl.BlockSpec(memory_space=pltpu.SMEM), hbm, hbm],
        out_shape=[pltpu.VMEM((8, 64, 128), BF16)] * 2 + [pltpu.VMEM((4, 64, 128), BF16)] * 2,
        scratch_shapes=[
            pltpu.VMEM((8, 64, 64), BF16),
            pltpu.VMEM((8, 64, 64), BF16),
            pltpu.VMEM((4, 64, 64), BF16),
            pltpu.VMEM((4, 64, 64), BF16),
            pltpu.VMEM((2, 4, 64, 128), BF16),
            pltpu.SemaphoreType.DMA((5,)),
        ],
        name="faces",
    )(odd, own, cot)


def level_column(x, y, own, x_lo, x_hi, y_lo, y_hi):
    if y == 0 or y == 9:
        pairs = y_lo if y == 0 else y_hi
        if 1 <= x <= 4:
            return half(pairs(((x - 1) // 2)), (x - 1) % 2)
        return half(pairs(2), int((x == 5) == (y == 9)))
    if x == 0:
        return half(x_lo((y - 1) // 2), (y - 1) % 2)
    if x == 5:
        return half(x_hi((y - 1) // 2), 1 - (y - 1) % 2)
    return own(x - 1, y - 1)


def half(value, which):
    return value[:, which * 64 : which * 64 + 64]


def build_blocks(w_up, blocks):
    empty = jnp.zeros((192, 64), BF16)
    for y in range(4):
        for x in range(3):
            left = w_up[x, y].reshape(192, 64) if y < 3 else empty
            right = w_up[x, y - 1].reshape(192, 64) if y > 0 else empty
            pair = jnp.concatenate([left, right], axis=1)
            blocks[x, y, 0:192, 0:128] = pair
            if x < 2:
                blocks[x + 1, y, 0:192, 128:256] = pair
            else:
                for c in range(3):
                    blocks[c, y, 192:256, 128:256] = pair[c * 64 : c * 64 + 64]
            blocks[x, y, 192:256, 0:128] = jnp.zeros((64, 128), BF16)
        blocks[0, y, 0:192, 128:256] = jnp.zeros((192, 128), BF16)


def column_grads(ys, taps, cot_taps, blocks, w_deep, sums, deep, last):
    rows = 2 * len(ys) * 64
    pre = jnp.zeros((rows, 256), F32)
    for x in range(3):
        for y in range(4):
            pre = pre + jnp.dot(
                level_window(taps, x, y, ys), blocks[x, y], preferred_element_type=F32
            )
    sig = 1.0 / (1.0 + jnp.exp(-pre))
    act = pre * sig
    summed = act[:, :128] + act[:, 128:]
    pooled = 0.25 * (summed[:, :64] + summed[:, 64:])
    pooled_t = pooled.T.astype(BF16)

    pooled_grad = jnp.zeros((rows, 64), F32)
    for a in range(3):
        for b in range(3):
            weight = jnp.concatenate([w_deep[2 - a, 2 - b, 2 - j] for j in range(3)], axis=1)
            pooled_grad = pooled_grad + lax.dot_general(
                deep_window(cot_taps, a, b, ys), weight, (((1,), (1,)), ((), ())),
                preferred_element_type=F32,
            )
    wide = pooled_grad.astype(BF16).astype(F32)
    wide = jnp.concatenate([wide, wide], axis=1)
    wide = jnp.concatenate([wide, wide], axis=1)
    grad = 0.25 * wide * (sig * (1.0 + pre * (1.0 - sig)))
    grad_t = grad.T.astype(BF16)

    for a in range(3):
        for b in range(3):
            out = jnp.dot(
                pooled_t, deep_window(cot_taps, 2 - a, 2 - b, ys), preferred_element_type=F32
            )
            for j in range(3):
                deep((a * 3 + b) * 3 + 2 - j, out[:, j * 128 : j * 128 + 128])
    for x in range(3):
        for y in range(4):
            kept = [(s, t) for s in range(2) for t in range(2) if 0 <= y - t < 3]
            left = jnp.concatenate(
                [grad_t[(s * 2 + t) * 64 : (s * 2 + t) * 64 + 64] for s, t in kept], axis=0
            )
            part = jnp.dot(left, level_window(taps, x, y, ys), preferred_element_type=F32)
            for k, (s, t) in enumerate(kept):
                piece = part[k * 64 : k * 64 + 64]
                if x >= s:
                    sums((x - s) * 3 + y - t, piece, s == 0 and t == 0)
                if s == 1:
                    place = (y - t) * 3 + x
                    tail = piece[:, 192:256]
                    last[place] = tail if t == 0 else last[place] + tail
    return grad.astype(BF16)


def add_last(sums, last):
    for b in range(3):
        for c in range(3):
            at = c * 64
            sums[6 + b, :, at : at + 64] = sums[6 + b, :, at : at + 64] + last[b * 3 + c]


def inner_kernel(odd_x, own, cot, core, chip, w_up, w_deep, sums, deep, inner, taps, cot_taps, blocks, last):
    swap_x = odd_x[0] == 1

    def x_lo(k):
        return jnp.where(swap_x, core[k], chip[k])

    def x_hi(k):
        return jnp.where(swap_x, chip[k], core[k])

    def column(x, y):
        return level_column(x, y, lambda u, v: own[u, v], x_lo, x_hi, None, None)

    build_taps(taps, range(2, 8), column)
    for x in range(4):
        for y in range(1, 5):
            if x == 0:
                row = x_lo(3 + y)
            elif x == 3:
                row = x_hi(3 + y)
            else:
                row = cot[x - 1, y - 1]
            cot_taps[x, y] = depth_taps(row, 0)
    build_blocks(w_up, blocks)

    def add_sum(k, piece, first):
        sums[k] = piece if first else sums[k] + piece

    def add_deep(k, piece):
        deep[k] = piece

    inner[...] = column_grads(INNER, taps, cot_taps, blocks, w_deep, add_sum, add_deep, last)
    add_last(sums, last)


def inner_grads(odd_x, own, cot, core, chip, w_up, w_deep):
    smem = pl.BlockSpec(memory_space=pltpu.SMEM)
    vmem = pl.BlockSpec(memory_space=pltpu.VMEM)
    return pl.pallas_call(
        inner_kernel,
        in_specs=[smem] + [vmem] * 6,
        out_shape=[
            jax.ShapeDtypeStruct((9, 64, 256), F32),
            jax.ShapeDtypeStruct((27, 64, 128), F32),
            jax.ShapeDtypeStruct((256, 256), BF16),
        ],
        scratch_shapes=[
            pltpu.VMEM((2, 3, 10, 64, 256), BF16),
            pltpu.VMEM((4, 6, 64, 384), BF16),
            pltpu.VMEM((3, 4, 256, 256), BF16),
            pltpu.VMEM((9, 64, 64), F32),
        ],
        compiler_params=pltpu.CompilerParams(vmem_limit_bytes=VMEM_BYTES),
        cost_estimate=pl.CostEstimate(
            flops=2_000_000_000, bytes_accessed=4_000_000, transcendentals=65536
        ),
        name="inner_grads",
    )(odd_x, own, cot, core, chip, w_up, w_deep)


def outer_kernel(
    odd_x, odd_y, part, own, cot, core, chip, near, far, w_up, w_deep, sums_in, deep_in, inner,
    keep, send, outer, to_core, to_chip, gy_head, gy_tail,
    taps, cot_taps, blocks, last, sums, payload,
):
    swap_x = odd_x[0] == 1
    swap_y = odd_y[0] == 1

    def x_lo(k):
        return jnp.where(swap_x, core[k], chip[k])

    def x_hi(k):
        return jnp.where(swap_x, chip[k], core[k])

    def y_lo(k):
        return jnp.where(swap_y, near[k], far[k])

    def y_hi(k):
        return jnp.where(swap_y, far[k], near[k])

    def column(x, y):
        return level_column(x, y, lambda u, v: own[u, v], x_lo, x_hi, y_lo, y_hi)

    build_taps(taps, (0, 1, 2, 3, 6, 7, 8, 9), column)
    for x in range(4):
        for y in range(6):
            if y == 0:
                row = y_lo(3 + x)
            elif y == 5:
                row = y_hi(3 + x)
            elif x == 0:
                row = x_lo(3 + y)
            elif x == 3:
                row = x_hi(3 + y)
            else:
                row = cot[x - 1, y - 1]
            cot_taps[x, y] = depth_taps(row, 0)
    build_blocks(w_up, blocks)

    def add_sum(k, piece, first):
        sums[k] = (sums_in[k] if first else sums[k]) + piece

    def add_deep(k, piece):
        top = DEEP_ROW + k * 64
        payload[top : top + 64, :] = (deep_in[k] + piece).astype(BF16)

    rounded = column_grads(OUTER, taps, cot_taps, blocks, w_deep, add_sum, add_deep, last)
    add_last(sums, last)
    outer[...] = rounded

    def block(x, y):
        top = (x * 2 + (y in (2, 3))) * 64
        return (inner if y in INNER else rounded)[top : top + 64]

    for k in range(4):
        head = block(0, k)[:, 0:128]
        head = jnp.concatenate([half(head, 1), half(head, 0)], axis=1)
        tail = block(1, k)[:, 128:256]
        to_core[k] = jnp.where(swap_x, head, tail)
        to_chip[k] = jnp.where(swap_x, tail, head)
    for k in range(2):
        first, last = block(k, 0), block(k, 3)
        gy_head[k] = jnp.concatenate([first[:, 0:64], first[:, 128:192]], axis=1)
        gy_tail[k] = jnp.concatenate([last[:, 64:128], last[:, 192:256]], axis=1)

    for k in range(9):
        payload[k * 64 : k * 64 + 64, :] = sums[k, :, 0:128].astype(BF16)
    for k in range(5):
        left = sums[2 * k, :, 128:192]
        right = sums[2 * k + 1, :, 128:192] if k < 4 else jnp.zeros((64, 64), F32)
        top = PAIR_ROW + k * 64
        payload[top : top + 64, :] = jnp.concatenate([left, right], axis=1).astype(BF16)
    mine = pl.multiple_of(part[0] * HALF_ROWS, HALF_ROWS)
    keep[...] = payload[pl.ds(mine, HALF_ROWS), :]
    send[...] = payload[pl.ds(HALF_ROWS - mine, HALF_ROWS), :]


def outer_grads(odd_x, odd_y, part, own, cot, core, chip, near, far, w_up, w_deep, sums, deep, inner):
    smem = pl.BlockSpec(memory_space=pltpu.SMEM)
    vmem = pl.BlockSpec(memory_space=pltpu.VMEM)
    return pl.pallas_call(
        outer_kernel,
        in_specs=[smem] * 3 + [vmem] * 11,
        out_shape=[
            jax.ShapeDtypeStruct((HALF_ROWS, 128), BF16),
            jax.ShapeDtypeStruct((HALF_ROWS, 128), BF16),
            jax.ShapeDtypeStruct((256, 256), BF16),
            jax.ShapeDtypeStruct((4, 64, 128), BF16),
            jax.ShapeDtypeStruct((4, 64, 128), BF16),
            jax.ShapeDtypeStruct((2, 64, 128), BF16),
            jax.ShapeDtypeStruct((2, 64, 128), BF16),
        ],
        scratch_shapes=[
            pltpu.VMEM((2, 3, 10, 64, 256), BF16),
            pltpu.VMEM((4, 6, 64, 384), BF16),
            pltpu.VMEM((3, 4, 256, 256), BF16),
            pltpu.VMEM((9, 64, 64), F32),
            pltpu.VMEM((9, 64, 256), F32),
            pltpu.VMEM((PAY_ROWS, 128), BF16),
        ],
        compiler_params=pltpu.CompilerParams(vmem_limit_bytes=VMEM_BYTES),
        cost_estimate=pl.CostEstimate(
            flops=2_000_000_000, bytes_accessed=4_000_000, transcendentals=65536
        ),
        name="outer_grads",
    )(odd_x, odd_y, part, own, cot, core, chip, near, far, w_up, w_deep, sums, deep, inner)


def input_columns(ys, at_ys, taps, w_up):
    empty = jnp.zeros((64, 256), BF16)
    spare = jnp.zeros((64, 64), BF16)
    weights = {}
    for a in range(3):
        for b in range(3):
            weights[a, b] = jnp.concatenate(
                [w_up[a, b, 2], w_up[a, b, 1], w_up[a, b, 0], spare], axis=1
            )
    total = jnp.zeros((2 * len(ys) * 64, 256), F32)
    for x in range(4):
        for y in at_ys:
            block = jnp.concatenate(
                [weights.get((s + 2 - x, t + 2 - y), empty) for s in range(2) for t in range(2)],
                axis=0,
            )
            total = total + lax.dot_general(
                window(taps, x, y, ys), block, (((1,), (1,)), ((), ())),
                preferred_element_type=F32,
            )
    return total


def picked(inner, outer, x, y):
    at = (x % 2) * 128 + (y % 2) * 64
    top = ((x // 2) * 2 + (y // 2 in (2, 3))) * 64
    return (inner if y // 2 in INNER else outer)[top : top + 64, at : at + 64]


def inner_input_kernel(odd_x, inner, outer, core, chip, w_up, out, taps):
    swap_x = odd_x[0] == 1

    def x_lo(k):
        return jnp.where(swap_x, core[k], chip[k])

    def x_hi(k):
        return jnp.where(swap_x, chip[k], core[k])

    def own(u, v):
        return picked(inner, outer, u, v)

    for x in range(6):
        taps[x, 0] = jnp.zeros((64, 256), BF16)
        taps[x, 9] = jnp.zeros((64, 256), BF16)
        for y in range(1, 9):
            taps[x, y] = depth_taps(level_column(x, y, own, x_lo, x_hi, None, None), 64)
    out[...] = input_columns(range(4), range(4), taps, w_up)


def inner_input(odd_x, inner, outer, core, chip, w_up):
    smem = pl.BlockSpec(memory_space=pltpu.SMEM)
    vmem = pl.BlockSpec(memory_space=pltpu.VMEM)
    return pl.pallas_call(
        inner_input_kernel,
        in_specs=[smem] + [vmem] * 5,
        out_shape=jax.ShapeDtypeStruct((512, 256), F32),
        scratch_shapes=[pltpu.VMEM((6, 10, 64, 256), BF16)],
        compiler_params=pltpu.CompilerParams(vmem_limit_bytes=VMEM_BYTES),
        cost_estimate=pl.CostEstimate(
            flops=500_000_000, bytes_accessed=2_000_000, transcendentals=0
        ),
        name="inner_input",
    )(odd_x, inner, outer, core, chip, w_up)


def outer_input_kernel(odd_y, near, far, w_up, part, out, taps):
    swap_y = odd_y[0] == 1

    def y_lo(k):
        return jnp.where(swap_y, near[k], far[k])

    def y_hi(k):
        return jnp.where(swap_y, far[k], near[k])

    for x in range(6):
        for y in (0, 9):
            taps[x, y] = depth_taps(level_column(x, y, None, None, None, y_lo, y_hi), 64)
    ends = {
        0: input_columns((0,), (0,), taps, w_up),
        3: input_columns((3,), (3,), taps, w_up),
    }
    for x in range(2):
        for y in range(4):
            top = (x * 4 + y) * 64
            rows = part[top : top + 64]
            if y in OUTER:
                rows = rows + ends[y][x * 64 : x * 64 + 64]
            rows = rows.astype(BF16)
            for s in range(2):
                for t in range(2):
                    at = s * 128 + t * 64
                    out[2 * x + s, 2 * y + t] = rows[:, at : at + 64]


def outer_input(odd_y, near, far, w_up, part):
    vmem = pl.BlockSpec(memory_space=pltpu.VMEM)
    return pl.pallas_call(
        outer_input_kernel,
        in_specs=[pl.BlockSpec(memory_space=pltpu.SMEM)] + [vmem] * 4,
        out_shape=jax.ShapeDtypeStruct((4, 8, 64, 64), BF16),
        scratch_shapes=[pltpu.VMEM((6, 10, 64, 256), BF16)],
        compiler_params=pltpu.CompilerParams(vmem_limit_bytes=VMEM_BYTES),
        cost_estimate=pl.CostEstimate(
            flops=300_000_000, bytes_accessed=4_000_000, transcendentals=0
        ),
        name="outer_input",
    )(odd_y, near, far, w_up, part)


def unpack_kernel(
    up_scale, deep_scale, odd, mine, other, up_out, deep_out, up, deep, sems
):
    def rows(top):
        found = []
        for part in range(2):
            start = max(top - part * HALF_ROWS, 0)
            stop = min(top + 64 - part * HALF_ROWS, HALF_ROWS)
            if start < stop:
                found.append(jnp.where(odd[0] == part, mine[start:stop], other[start:stop]))
        return jnp.concatenate(found, axis=0).astype(F32)

    copies = []
    pairs = {}
    for a in range(3):
        for k in range(a * 9, a * 9 + 9):
            top = DEEP_ROW + k * 64
            deep[a, k // 3 % 3, k % 3] = rows(top) * deep_scale
        copies.append(pltpu.make_async_copy(deep.at[a], deep_out.at[a], sems.at[a]))
        copies[-1].start()
    for a in range(3):
        for b in range(3):
            k = a * 3 + b
            pair = rows(k * 64).T * up_scale
            up[a, b, 0] = pair[:64]
            up[a, b, 1] = pair[64:]
            if k % 2 == 0:
                top = PAIR_ROW + k // 2 * 64
                pairs[k // 2] = rows(top).T * up_scale
            up[a, b, 2] = pairs[k // 2][k % 2 * 64 : k % 2 * 64 + 64]
        copies.append(pltpu.make_async_copy(up.at[a], up_out.at[a], sems.at[3 + a]))
        copies[-1].start()
    for copy in copies:
        copy.wait()


def unpack(odd, mine, other, up_scale, deep_scale):
    vmem = pl.BlockSpec(memory_space=pltpu.VMEM)
    hbm = pl.BlockSpec(memory_space=pltpu.HBM)
    return pl.pallas_call(
        functools.partial(unpack_kernel, up_scale, deep_scale),
        in_specs=[pl.BlockSpec(memory_space=pltpu.SMEM), vmem, vmem],
        out_specs=[hbm, hbm],
        out_shape=[
            jax.ShapeDtypeStruct((3, 3, 3, 64, 64), F32),
            jax.ShapeDtypeStruct((3, 3, 3, 64, 128), F32),
        ],
        scratch_shapes=[
            pltpu.VMEM((3, 3, 3, 64, 64), F32),
            pltpu.VMEM((3, 3, 3, 64, 128), F32),
            pltpu.SemaphoreType.DMA((6,)),
        ],
        compiler_params=pltpu.CompilerParams(vmem_limit_bytes=VMEM_BYTES),
        name="unpack",
    )(odd, mine, other)


def side_bit(step):
    index = lax.axis_index(step[0])
    return sum(index >> bit for bit in step[2]) & 1


def swap(value, steps, which):
    masks = {"gx": 0, "gy": 0}
    for place, (axis, mask, _) in enumerate(steps):
        if (which >> place) & 1:
            masks[axis] ^= mask
    axes = [axis for axis in ("gx", "gy") if masks[axis]]
    if len(axes) == 1:
        axis = axes[0]
        count = lax.axis_size(axis)
        return lax.ppermute(value, axis, [(i, i ^ masks[axis]) for i in range(count)])
    rows, cols = lax.axis_size("gx"), lax.axis_size("gy")
    pairs = [
        (i * cols + j, (i ^ masks["gx"]) * cols + (j ^ masks["gy"]))
        for i in range(rows)
        for j in range(cols)
    ]
    return lax.ppermute(value, ("gx", "gy"), pairs)


def place_of(steps):
    return sum(side_bit(step) << place for place, step in enumerate(steps))


def tree_sum(values):
    values = [value.astype(F32) for value in values]
    while len(values) > 1:
        values = [values[i] + values[i + 1] for i in range(0, len(values), 2)]
    return values[0].astype(BF16)


def scatter_sum(value, steps):
    parts = 1 << len(steps)
    rows = value.shape[0] // parts
    me = place_of(steps)
    found = [lax.dynamic_slice_in_dim(value, me * rows, rows, 0)]
    for k in range(1, parts):
        piece = lax.dynamic_slice_in_dim(value, (me ^ k) * rows, rows, 0)
        found.append(swap(piece, steps, k))
    return tree_sum(found)


def swap_sum(value, step):
    return tree_sum([value, swap(value, (step,), 1)])


def swap_sum_with(value, step, rider):
    rows = value.shape[0]
    got = swap(jnp.concatenate([value, rider]), (step,), 1)
    return tree_sum([value, got[:rows]]), got[rows:]


def gather(value, steps, riders):
    parts = 1 << len(steps)
    rows = value.shape[0]
    me = place_of(steps)
    found, came = [value], []
    for k in range(1, parts):
        rider = riders[k - 1]
        sent = value if rider is None else jnp.concatenate([value, rider])
        got = swap(sent, steps, k)
        found.append(got[:rows])
        came.append(got[rows:])
    for place in range(len(steps)):
        near = ((me >> place) & 1) == 0
        other = 1 << place
        found = [
            jnp.where(near, found[i & ~other], found[i | other])
            if not i & other
            else jnp.where(near, found[i | other], found[i & ~other])
            for i in range(parts)
        ]
    return jnp.concatenate(found), came


def pairs_of(axis, first):
    count = lax.axis_size(axis)
    found = []
    for i in range(first, count, 2):
        found += [(i, (i + 1) % count), ((i + 1) % count, i)]
    return found


def both_sides(first, second, axis):
    even = lax.ppermute(first, axis, pairs_of(axis, 0))
    odd = lax.ppermute(second, axis, pairs_of(axis, 1))
    return even, inside(odd, axis)


def inside(value, axis):
    index = lax.axis_index(axis)
    edge = (index == 0) | (index == lax.axis_size(axis) - 1)
    return jnp.where(edge, jnp.zeros_like(value), value)


def column_ends(odd_x, odd_y, core, chip, head, tail, level_rows):
    lo = jnp.where(odd_x == 1, core, chip)
    hi = jnp.where(odd_x == 1, chip, core)
    left = lax.broadcasted_iota(jnp.int32, (1, 64, 128), 2) < 64
    head = [head[:2], jnp.where(left, lo[0:1], hi[0:1])] + (
        [lo[4:5], head[2:], hi[4:5]] if level_rows else []
    )
    tail = [tail[:2], jnp.where(left, hi[3:4], lo[3:4])] + (
        [lo[7:8], tail[2:], hi[7:8]] if level_rows else []
    )
    head, tail = jnp.concatenate(head), jnp.concatenate(tail)
    return jnp.where(odd_y == 1, head, tail), jnp.where(odd_y == 1, tail, head)


def local(level_input, weight_upper, weight_deep, deep_cotangent):
    tiles = lax.axis_size("gx") * lax.axis_size("gy")
    up_scale = 1.0 / math.sqrt(math.prod(level_input.shape[:3]) * tiles)
    deep_scale = 1.0 / math.sqrt(math.prod(deep_cotangent.shape[:3]) * tiles)
    odd_x = (lax.axis_index("gx") & 1).astype(jnp.int32)
    odd_y = (lax.axis_index("gy") & 1).astype(jnp.int32)
    flag_x, flag_y = odd_x.reshape(1), odd_y.reshape(1)
    part = side_bit(CORE).astype(jnp.int32).reshape(1)

    to_core, to_chip, y_head, y_tail = faces(
        flag_x,
        pltpu.with_memory_space_constraint(level_input, pltpu.HBM),
        pltpu.with_memory_space_constraint(deep_cotangent, pltpu.HBM),
    )
    core, chip = both_sides(to_core, to_chip, "gx")
    to_near, to_far = column_ends(odd_x, odd_y, core, chip, y_head, y_tail, True)
    near, far = both_sides(to_near, to_far, "gy")

    sums, deep, inner = inner_grads(
        flag_x, level_input, deep_cotangent, core, chip, weight_upper, weight_deep
    )
    keep, send, outer, to_core, to_chip, y_head, y_tail = outer_grads(
        flag_x, flag_y, part, level_input, deep_cotangent, core, chip, near, far,
        weight_upper, weight_deep, sums, deep, inner,
    )
    at_x, at_y = lax.axis_index("gx"), lax.axis_index("gy")
    total = tree_sum([keep, swap(send, (CORE,), 1)])
    core = lax.ppermute(to_core, "gx", pairs_of("gx", 0))
    total, core = lax.optimization_barrier((total, core))
    total = scatter_sum(total, (Z_NEAR, X_NEAR))
    total, to_chip = lax.optimization_barrier((total, to_chip))
    second = swap(to_chip, (Y_FAR,), 1)
    total = swap_sum(total, Y_FAR)
    total, to_chip = lax.optimization_barrier((total, to_chip))
    first = swap(to_chip, (Y_NEAR,), 1)
    total = swap_sum(total, Y_NEAR)
    chip = jnp.where((((at_x + 1) >> 1) & 1) == 1, first, second)
    chip = inside(chip, "gx")
    inner_part = inner_input(flag_x, inner, outer, core, chip, weight_upper)
    to_near, to_far = column_ends(odd_x, odd_y, core, chip, y_head, y_tail, False)
    total, direct = swap_sum_with(total, Z_FAR, to_far.reshape(-1, 128))
    near = swap(to_near, (Z_NEAR,), 1)
    total, near = lax.optimization_barrier((total, near))
    total, handed_far = swap_sum_with(total, X_FAR, direct)
    total, inner_part = lax.optimization_barrier((total, inner_part))
    total, (_, handed_near, _) = gather(total, (Z_NEAR, X_NEAR), (None, direct, None))
    plane, depth = at_y >> 2, at_y & 3
    none = jnp.zeros_like(direct)
    handed = jnp.where(
        ((depth == 0) & (plane == 2)) | ((depth == 3) & (plane == 1)), handed_far, handed_near
    )
    ends = (at_y == 0) | (at_y == lax.axis_size("gy") - 1)
    far = jnp.where((depth == 1) | (depth == 2), direct, jnp.where(ends, none, handed))
    input_grad = outer_input(
        flag_y, near, far.reshape(to_far.shape), weight_upper, inner_part
    )
    other = swap(total, (CORE,), 1)
    upper, deep = unpack(part, total, other, up_scale, deep_scale)
    return (input_grad, upper, deep)


def solution(mesh):
    placed = (P("gx", "gy", None, None), P(), P(), P("gx", "gy", None, None))
    return jax.shard_map(
        local,
        mesh=mesh,
        in_specs=placed,
        out_specs=(P("gx", "gy", None, None), P(), P()),
        check_vma=False,
    )
```
